32 devices in a mesh: dp: 4 (over x, core), seq: 4 (over z), heads: 2 (over y).
Axes of the slice: x: 2, y: 2, z: 4, core: 2. Of those that a mesh axis runs over, the one named last changes fastest.
Arguments:
- block_input: bfloat16 [2, 4, 1024, 1536], P(None, 'dp', 'seq'), may hold values from -6 to 6
- output_grad: bfloat16 [2, 4, 1024, 1536], P(None, 'dp', 'seq'), may hold values from -6 to 6
- input_gain: bfloat16 [1536], P(('dp', 'seq')), may hold values from 0.099609375 to 1.8984375
- gate_weight: bfloat16 [1536, 3072], P(('dp', 'seq'), 'heads'), may hold values from -0.15625 to 0.15625
- value_weight: bfloat16 [1536, 3072], P(('dp', 'seq'), 'heads'), may hold values from -0.15625 to 0.15625
- state_weight: bfloat16 [1536, 256], P(('dp', 'seq')), may hold values from -0.15625 to 0.15625
- step_weight: bfloat16 [1536, 48], P(('dp', 'seq'), 'heads'), may hold values from -0.15625 to 0.15625
- out_weight: bfloat16 [3072, 1536], P('heads', ('dp', 'seq')), may hold values from -0.109375 to 0.109375
- value_taps: float32 [5, 3072], P(None, 'heads'), may hold values from -0.6 to 0.6
- state_taps: float32 [5, 256], replicated, may hold values from -0.6 to 0.6
- step_bias: float32 [48], P('heads'), may hold values from -1 to 1
- log_decay: float32 [48], P('heads'), may hold values from -10 to -3, as said below
- skip_gain: float32 [48], P('heads'), may hold values from 0.5 to 1.5
- mixer_gain: float32 [3072], P('heads'), may hold values from 0.1 to 1.9
Outputs:
- block_output: bfloat16 [2, 4, 1024, 1536], P(None, 'dp', 'seq')
- grad_input: bfloat16 [2, 4, 1024, 1536], P(None, 'dp', 'seq')
- grad_input_gain: float32 [1536], P(('dp', 'seq'))
- grad_gate_weight: float32 [1536, 3072], P(('dp', 'seq'), 'heads')
- grad_value_weight: float32 [1536, 3072], P(('dp', 'seq'), 'heads')
- grad_state_weight: float32 [1536, 256], P(('dp', 'seq'))
- grad_step_weight: float32 [1536, 48], P(('dp', 'seq'), 'heads')
- grad_out_weight: float32 [3072, 1536], P('heads', ('dp', 'seq'))
- grad_value_taps: float32 [5, 3072], P(None, 'heads')
- grad_state_taps: float32 [5, 256], replicated
- grad_step_bias: float32 [48], P('heads')
- grad_log_decay: float32 [48], P('heads')
- grad_skip_gain: float32 [48], P('heads')
- grad_mixer_gain: float32 [3072], P('heads')
The draws below stay inside these ranges and needn't reach their ends.
Inputs may be any that keep to these rules, and one draw needn't show every extreme that they name: `log_decay`: the log of each head's decay rate.
All inputs are finite; a program needn't handle non-finite values.
Results may differ from the reference program's by a relative error of at most 0.0028.
The reference program's roundings to bfloat16 on the way count: a program that leaves them out, or rounds other values in their place, can miss the bound.
Values may be sent and summed in bfloat16 or wider, within the bound.
No kernel may reach another device: no remote copies, remote signals or barrier semaphores. Data moves between devices by JAX's collectives and lax.ppermute only.
A program may use at most 192 MiB of HBM per device.

```python
import math
import jax
import jax.numpy as jnp
from jax import lax

D = 1536
HEADS = 48
HEAD_DIM = 64
STATE = 128
CONV = 4
GROUP = 256
MB = 2
INNER = 3072
SEQ_LEN = 1024
SEQS = 4


def draw_log_decay(key, part):
    key = jax.random.fold_in(key, 7)
    lower_end = math.log(1.0 / (4.0 * SEQ_LEN))
    upper_end = math.log(1.0 / 30.0)
    return jax.random.uniform(key, (HEADS,), jnp.float32, lower_end, upper_end)


def block_scale(rng, extent, cuts, low, largest):
    loudness, own = 1.0, jax.random.fold_in(rng, 6)
    for position, parts in cuts:
        draws = jnp.exp(jax.random.uniform(jax.random.fold_in(own, position), (parts,), jnp.float32, low / len(cuts), largest / len(cuts)))
        loudness = loudness * jnp.repeat(draws, extent[position] // parts).reshape([-1 if axis == position else 1 for axis in range(len(extent))])
    return loudness


def scatter_about(key, dims, deviation, bound, cuts=(), held_as=jnp.bfloat16):
    loudness = block_scale(key, dims, cuts, -0.22, 0.18) if cuts else 1.0
    values = jax.random.normal(key, dims, jnp.float32) * deviation * loudness
    return jnp.minimum(jnp.maximum(values, -bound), bound).astype(held_as)


def setup_inputs(seed: int = 0) -> dict:
    seeds = jax.random.split(jax.random.key(seed), 15)
    return {
        "block_input": scatter_about(seeds[0], (MB, SEQS, SEQ_LEN, D), 1.0, 6.0, ((1, 4), (2, 4))),
        "output_grad": scatter_about(seeds[1], (MB, SEQS, SEQ_LEN, D), 1.0, 6.0, ((1, 4), (2, 4))),
        "input_gain": jnp.clip(1.0 + 0.18 * jax.random.normal(seeds[2], (D,), jnp.float32), 0.099609375, 1.8984375).astype(jnp.bfloat16),
        "gate_weight": scatter_about(seeds[3], (D, INNER), D ** -0.5, 0.15625, ((0, 16), (1, 2))),
        "value_weight": scatter_about(seeds[4], (D, INNER), D ** -0.5, 0.15625, ((0, 16), (1, 2))),
        "state_weight": scatter_about(seeds[5], (D, 2 * STATE), D ** -0.5, 0.15625, ((0, 16),)),
        "step_weight": scatter_about(seeds[6], (D, HEADS), D ** -0.5, 0.15625, ((0, 16), (1, 2))),
        "out_weight": scatter_about(seeds[7], (INNER, D), INNER ** -0.5, 0.109375, ((0, 2), (1, 16))),
        "value_taps": jnp.clip(jax.random.uniform(seeds[8], (CONV + 1, INNER), jnp.float32, -0.6, 0.6) * block_scale(seeds[8], (CONV + 1, INNER), ((1, 2),), -0.4, 0.0), -0.6, 0.6),
        "state_taps": jnp.clip(jax.random.uniform(seeds[9], (CONV + 1, 2 * STATE), jnp.float32, -0.6, 0.6), -0.6, 0.6),
        "step_bias": jnp.clip(jax.random.uniform(seeds[10], (HEADS,), jnp.float32, -1.0, 1.0) * block_scale(seeds[10], (HEADS,), ((0, 2),), -0.4, 0.0), -1.0, 1.0),
        "log_decay": draw_log_decay(jax.random.fold_in(seeds[14], 71), 0),
        "skip_gain": jnp.clip(0.5 + 1.0 * jax.random.uniform(seeds[12], (HEADS,), jnp.float32) ** block_scale(seeds[12], (HEADS,), ((0, 2),), -0.2, 0.2), 0.5, 1.5),
        "mixer_gain": jnp.clip(1.0 + 0.18 * jax.random.normal(seeds[13], (INNER,), jnp.float32), 0.1, 1.9),
    }


@jax.custom_vjp
def low(v):
    return lax.optimization_barrier(v.astype(jnp.bfloat16)).astype(jnp.float32)

@jax.custom_vjp
def low_back(v):
    return v

def low_keep(v):
    return (low(v), None)

def low_pass(kept, grad):
    return (grad,)

def back_keep(v):
    return (v, None)

def back_low(kept, grad):
    return (low(grad),)
low.defvjp(low_keep, low_pass)
low_back.defvjp(back_keep, back_low)
EPS = 1e-05
HIGH = lax.Precision.HIGHEST

def norm_rows(values, gain):
    return values * lax.rsqrt(lax.optimization_barrier(jnp.mean(values * values, axis=-1, keepdims=True)) + EPS) * gain

def conv_silu(values, taps):
    length = values.shape[0]
    padded = jnp.concatenate([jnp.zeros((CONV - 1, values.shape[1]), jnp.float32), values], axis=0)
    total = jnp.zeros_like(values) + taps[CONV]
    for offset in range(CONV):
        total = total + padded[offset:offset + length] * taps[offset]
    return jax.nn.silu(total)

def scan_block(carried, pieces, rates, skip_gain):
    block_values, block_b, block_c, block_step = pieces
    cumulative = jnp.cumsum(-block_step * rates, axis=0)
    gaps = cumulative[:, None, :] - cumulative[None, :, :]
    causal = (jnp.arange(GROUP)[:, None] >= jnp.arange(GROUP)[None, :])[:, :, None]
    decays = jnp.where(causal, jnp.exp(jnp.where(causal, gaps, 0.0)), 0.0)
    scores = jnp.dot(block_c, block_b.T, precision=HIGH)
    weights = decays * scores[:, :, None] * block_step[None, :, :]
    within = jnp.einsum('tsh,shp->thp', weights, block_values, precision=HIGH)
    incoming = jnp.exp(cumulative)[:, :, None] * jnp.einsum('tn,hnp->thp', block_c, carried, precision=HIGH)
    result = within + incoming + skip_gain[None, :, None] * block_values
    final = cumulative[-1]
    ending = jnp.exp(final[None, :] - cumulative) * block_step
    new_state = jnp.exp(final)[:, None, None] * carried + jnp.einsum('th,tn,thp->hnp', ending, block_b, block_values, precision=HIGH)
    return (new_state, result)

def sequence_forward(sequence, parameters):
    input_gain, gate_weight, value_weight, state_weight, step_weight, out_weight, value_taps, state_taps, step_bias, log_decay, skip_gain, mixer_gain = parameters
    normed = low(norm_rows(sequence, input_gain))
    gate_lin = low_back(jnp.dot(normed, gate_weight, precision=HIGH))
    values_pre = low_back(jnp.dot(normed, value_weight, precision=HIGH))
    states_pre = low_back(jnp.dot(normed, state_weight, precision=HIGH))
    step_pre = low_back(jnp.dot(normed, step_weight, precision=HIGH))
    values = conv_silu(values_pre, value_taps)
    states = conv_silu(states_pre, state_taps)
    stepsize = jax.nn.softplus(step_pre + step_bias)
    rates = jnp.exp(log_decay)
    blocks = SEQ_LEN // GROUP
    pieces = (values.reshape(blocks, GROUP, HEADS, HEAD_DIM), states[:, :STATE].reshape(blocks, GROUP, STATE), states[:, STATE:].reshape(blocks, GROUP, STATE), stepsize.reshape(blocks, GROUP, HEADS))

    def one_block(carried, block_pieces):
        return scan_block(carried, block_pieces, rates, skip_gain)
    start_state = jnp.zeros((HEADS, STATE, HEAD_DIM), jnp.float32)
    ignored, mixed_blocks = lax.scan(jax.checkpoint(one_block), start_state, pieces)
    mixer = mixed_blocks.reshape(SEQ_LEN, INNER)
    gated = mixer * jax.nn.silu(gate_lin)
    out_normed = low(norm_rows(gated, mixer_gain))
    return sequence + jnp.dot(out_normed, out_weight, precision=HIGH)

def reference(block_input, output_grad, input_gain, gate_weight, value_weight, state_weight, step_weight, out_weight, value_taps, state_taps, step_bias, log_decay, skip_gain, mixer_gain):
    parameters = tuple((item.astype(jnp.float32) for item in (input_gain, gate_weight, value_weight, state_weight, step_weight, out_weight, value_taps, state_taps, step_bias, log_decay, skip_gain, mixer_gain)))
    sequences = block_input.reshape(MB * SEQS, SEQ_LEN, D).astype(jnp.float32)
    cotangents = output_grad.reshape(MB * SEQS, SEQ_LEN, D).astype(jnp.float32)

    def forward(inputs, weights):

        def one_sequence(carry, sequence):
            return (carry, jax.checkpoint(sequence_forward)(sequence, weights))
        ignored, results = lax.scan(one_sequence, jnp.zeros((), jnp.float32), inputs)
        return results
    results, pullback = jax.vjp(forward, sequences, parameters)
    grad_rows, grads = pullback(cotangents)
    block_output = results.reshape(block_input.shape).astype(jnp.bfloat16)
    grad_input = grad_rows.reshape(block_input.shape).astype(jnp.bfloat16)
    return (block_output, grad_input, grads[0], grads[1], grads[2], grads[3], grads[4], grads[5], grads[6], grads[7], grads[8], grads[9], grads[10], grads[11])
```

```python
import jax
import jax.numpy as jnp
from jax import lax
from jax.experimental import pallas as pl
from jax.experimental.pallas import tpu as pltpu
from jax.sharding import PartitionSpec as P

STATE = 128
CONV = 4
MB = 2
INNER = 3072


EPS = 1e-05
HIGH = lax.Precision.HIGHEST


def shifted(block, axis, distance):
    devices = range(lax.axis_size(axis))
    route = [(i - distance, i) for i in devices if i - distance in devices]
    return lax.ppermute(block, axis, route)


def entering(x, axis, combine, identity, reverse):
    peers, index = (lax.axis_size(axis), lax.axis_index(axis))
    everything = jax.tree.map(lambda part: lax.all_gather(part, axis), x)
    start = jax.tree.map(
        lambda part, zero: jnp.broadcast_to(jnp.asarray(zero, part.dtype), part.shape), x, identity
    )

    def step(k, before):
        at = peers - 1 - k if reverse else k
        reached = at > index if reverse else at < index
        new = combine(before, jax.tree.map(lambda part: part[at], everything))
        return jax.tree.map(lambda a, b: jnp.where(reached, a, b), new, before)

    return lax.fori_loop(0, peers, step, start)


def norm_rows(values, gain):
    return values * lax.rsqrt(jnp.mean(values * values, axis=-1, keepdims=True) + EPS) * gain


def conv_silu(extended, taps):
    length = extended.shape[1] - (CONV - 1)
    total = jnp.zeros((extended.shape[0], length, extended.shape[2]), jnp.float32) + taps[CONV]
    for offset in range(CONV):
        total = total + extended[:, offset : offset + length] * taps[offset]
    return jax.nn.silu(total)


def local_parts(
    values_ext, states_ext, step_pre, value_taps, state_taps, step_bias, log_decay, skip_gain
):
    values_conv = conv_silu(values_ext, value_taps)
    states_conv = conv_silu(states_ext, state_taps)
    batch, length, channels = values_conv.shape
    heads_here = step_pre.shape[-1]
    values = values_conv.reshape(batch, length, heads_here, channels // heads_here)
    input_mat = states_conv[..., :STATE]
    output_mat = states_conv[..., STATE:]
    stepsize = jax.nn.softplus(step_pre + step_bias)
    cumulative = jnp.cumsum(-stepsize * jnp.exp(log_decay), axis=1)
    gaps = cumulative[:, :, None, :] - cumulative[:, None, :, :]
    causal = (jnp.arange(length)[:, None] >= jnp.arange(length)[None, :])[None, :, :, None]
    decays = jnp.where(causal, jnp.exp(jnp.where(causal, gaps, 0.0)), 0.0)
    scores = jnp.einsum("btn,bsn->bts", output_mat, input_mat, precision=HIGH)
    weights = decays * scores[..., None] * stepsize[:, None, :, :]
    within = (
        jnp.einsum("btsh,bshp->bthp", weights, values, precision=HIGH) + skip_gain[:, None] * values
    )
    final = cumulative[:, -1]
    ending = jnp.exp(final[:, None, :] - cumulative) * stepsize
    local_state = jnp.einsum("bth,btn,bthp->bhnp", ending, input_mat, values, precision=HIGH)
    return (within, local_state, jnp.exp(final), cumulative, output_mat)


def carried_part(cumulative, output_mat, state_in):
    return jnp.exp(cumulative)[..., None] * jnp.einsum(
        "btn,bhnp->bthp", output_mat, state_in, precision=HIGH
    )


def whole_block(
    values_ext,
    states_ext,
    step_pre,
    value_taps,
    state_taps,
    step_bias,
    log_decay,
    skip_gain,
    state_in,
):
    within, local_state, span_decay, cumulative, output_mat = local_parts(
        values_ext, states_ext, step_pre, value_taps, state_taps, step_bias, log_decay, skip_gain
    )
    result = within + carried_part(cumulative, output_mat, state_in)
    return (result.reshape(result.shape[0], result.shape[1], -1), local_state, span_decay)


def compose(earlier, later):
    return (earlier[0] * later[0], later[0][..., None, None] * earlier[1] + later[1])


def shards(
    block_input,
    output_grad,
    input_gain,
    gate_weight,
    value_weight,
    state_weight,
    step_weight,
    out_weight,
    value_taps,
    state_taps,
    step_bias,
    log_decay,
    skip_gain,
    mixer_gain,
):
    margin = CONV - 1
    width = block_input.shape[-1]
    inner_here = gate_weight.shape[1]
    state_cols = state_weight.shape[1]
    heads_here = step_weight.shape[1]
    acc_gain = jnp.zeros((width,), jnp.float32)
    acc_gate = jnp.zeros((width, inner_here), jnp.float32)
    acc_value = jnp.zeros((width, inner_here), jnp.float32)
    acc_state = jnp.zeros((width, state_cols), jnp.float32)
    acc_step = jnp.zeros((width, heads_here), jnp.float32)
    acc_out = jnp.zeros((inner_here, width), jnp.float32)
    acc_value_taps = jnp.zeros_like(value_taps)
    acc_state_taps = jnp.zeros_like(state_taps)
    acc_step_bias = jnp.zeros_like(step_bias)
    acc_log_decay = jnp.zeros_like(log_decay)
    acc_skip = jnp.zeros_like(skip_gain)
    acc_mixer_gain = jnp.zeros_like(mixer_gain)
    outputs = []
    input_grads = []
    for micro_batch in range(MB):
        weights_now = (
            lax.all_gather(input_gain, ("dp", "seq"), axis=0, tiled=True),
            lax.all_gather(gate_weight, ("dp", "seq"), axis=0, tiled=True),
            lax.all_gather(value_weight, ("dp", "seq"), axis=0, tiled=True),
            lax.all_gather(state_weight, ("dp", "seq"), axis=0, tiled=True),
            lax.all_gather(step_weight, ("dp", "seq"), axis=0, tiled=True),
            lax.all_gather(out_weight, ("dp", "seq"), axis=1, tiled=True),
        )
        gain_full, gate_full, value_full, state_full, step_full, out_full = weights_now
        tokens = block_input[micro_batch].astype(jnp.float32)
        normed = norm_rows(tokens, gain_full.astype(jnp.float32)).astype(jnp.bfloat16)
        gate_lin = jnp.einsum("btd,di->bti", normed, gate_full, preferred_element_type=jnp.float32)
        values_pre = jnp.einsum(
            "btd,di->bti", normed, value_full, preferred_element_type=jnp.float32
        )
        states_pre = jnp.einsum(
            "btd,di->bti", normed, state_full, preferred_element_type=jnp.float32
        )
        step_pre = jnp.einsum("btd,di->bti", normed, step_full, preferred_element_type=jnp.float32)
        outgoing = jnp.concatenate([values_pre[:, -margin:], states_pre[:, -margin:]], axis=2)
        incoming = shifted(outgoing, "seq", 1)
        values_ext = jnp.concatenate([incoming[..., :inner_here], values_pre], axis=1)
        states_ext = jnp.concatenate([incoming[..., inner_here:], states_pre], axis=1)
        within, local_state, span_decay, cumulative, output_mat = local_parts(
            values_ext,
            states_ext,
            step_pre,
            value_taps,
            state_taps,
            step_bias,
            log_decay,
            skip_gain,
        )
        prefix = entering(
            (span_decay, local_state),
            "seq",
            compose,
            (jnp.ones_like(span_decay), jnp.zeros_like(local_state)),
            False,
        )
        state_in = prefix[1]
        mixer = (within + carried_part(cumulative, output_mat, state_in)).reshape(gate_lin.shape)
        silu_gate = jax.nn.silu(gate_lin)
        gated = mixer * silu_gate
        total_sq = lax.psum(jnp.sum(gated * gated, axis=-1), "heads")
        inverse = lax.rsqrt(total_sq / INNER + EPS)[..., None]
        out_normed = (gated * inverse * mixer_gain).astype(jnp.bfloat16)
        partial_out = jnp.einsum(
            "bti,id->btd", out_normed, out_full, preferred_element_type=jnp.float32
        )
        branch = lax.psum(partial_out, "heads")
        outputs.append((tokens + branch).astype(jnp.bfloat16))
        weights_back = (
            lax.all_gather(input_gain, ("dp", "seq"), axis=0, tiled=True),
            lax.all_gather(gate_weight, ("dp", "seq"), axis=0, tiled=True),
            lax.all_gather(value_weight, ("dp", "seq"), axis=0, tiled=True),
            lax.all_gather(state_weight, ("dp", "seq"), axis=0, tiled=True),
            lax.all_gather(step_weight, ("dp", "seq"), axis=0, tiled=True),
            lax.all_gather(out_weight, ("dp", "seq"), axis=1, tiled=True),
        )
        gain_full, gate_full, value_full, state_full, step_full, out_full = weights_back
        grad_out = output_grad[micro_batch]
        d_out_normed = jnp.einsum(
            "btd,id->bti", grad_out, out_full, preferred_element_type=jnp.float32
        )
        acc_out = acc_out + jnp.einsum(
            "bti,btd->id", out_normed, grad_out, preferred_element_type=jnp.float32
        )
        acc_mixer_gain = acc_mixer_gain + jnp.sum(d_out_normed * gated * inverse, axis=(0, 1))
        weighted = d_out_normed * mixer_gain
        dot_total = lax.psum(jnp.sum(weighted * gated, axis=-1), "heads")
        d_gated = inverse * weighted - gated * (inverse * inverse * inverse) * (
            dot_total[..., None] / INNER
        )
        d_mixer = d_gated * silu_gate
        sigmoid_gate = jax.nn.sigmoid(gate_lin)
        d_gate_lin = d_gated * mixer * sigmoid_gate * (1.0 + gate_lin * (1.0 - sigmoid_gate))
        carry_grad = jnp.einsum(
            "bth,btn,bthp->bhnp",
            jnp.exp(cumulative),
            output_mat,
            d_mixer.reshape(within.shape),
            precision=HIGH,
        )
        suffix = entering(
            (span_decay, carry_grad),
            "seq",
            compose,
            (jnp.ones_like(span_decay), jnp.zeros_like(carry_grad)),
            True,
        )
        later_grad = suffix[1]
        d_decay = jnp.sum(later_grad * state_in, axis=(2, 3))
        ignored, pullback = jax.vjp(
            whole_block,
            values_ext,
            states_ext,
            step_pre,
            value_taps,
            state_taps,
            step_bias,
            log_decay,
            skip_gain,
            state_in,
        )
        (
            d_values_ext,
            d_states_ext,
            d_step_pre,
            g_value_taps,
            g_state_taps,
            g_step_bias,
            g_log_decay,
            g_skip,
            unused_state,
        ) = pullback((d_mixer, later_grad, d_decay))
        rim_grads = jnp.concatenate([d_values_ext[:, :margin], d_states_ext[:, :margin]], axis=2)
        returned = shifted(rim_grads, "seq", -1)
        d_values_pre = d_values_ext[:, margin:].at[:, -margin:].add(returned[..., :inner_here])
        d_states_pre = d_states_ext[:, margin:].at[:, -margin:].add(returned[..., inner_here:])
        gate_low = d_gate_lin.astype(jnp.bfloat16)
        values_low = d_values_pre.astype(jnp.bfloat16)
        step_low = d_step_pre.astype(jnp.bfloat16)
        d_normed_part = (
            jnp.einsum("bti,di->btd", gate_low, gate_full, preferred_element_type=jnp.float32)
            + jnp.einsum("bti,di->btd", values_low, value_full, preferred_element_type=jnp.float32)
            + jnp.einsum("bti,di->btd", step_low, step_full, preferred_element_type=jnp.float32)
        )
        d_normed_sum, d_states_total, state_taps_total = lax.psum(
            (d_normed_part, d_states_pre, g_state_taps), "heads"
        )
        states_low = d_states_total.astype(jnp.bfloat16)
        d_normed = d_normed_sum + jnp.einsum(
            "bti,di->btd", states_low, state_full, preferred_element_type=jnp.float32
        )
        acc_gate = acc_gate + jnp.einsum(
            "btd,bti->di", normed, gate_low, preferred_element_type=jnp.float32
        )
        acc_value = acc_value + jnp.einsum(
            "btd,bti->di", normed, values_low, preferred_element_type=jnp.float32
        )
        acc_state = acc_state + jnp.einsum(
            "btd,bti->di", normed, states_low, preferred_element_type=jnp.float32
        )
        acc_step = acc_step + jnp.einsum(
            "btd,bti->di", normed, step_low, preferred_element_type=jnp.float32
        )
        scaling = lax.rsqrt(jnp.mean(tokens * tokens, axis=-1, keepdims=True) + EPS)
        acc_gain = acc_gain + jnp.sum(d_normed * tokens * scaling, axis=(0, 1))
        pushed = d_normed * gain_full.astype(jnp.float32)
        d_tokens = scaling * pushed - tokens * (scaling * scaling * scaling) * jnp.mean(
            pushed * tokens, axis=-1, keepdims=True
        )
        input_grads.append((grad_out.astype(jnp.float32) + d_tokens).astype(jnp.bfloat16))
        acc_value_taps = acc_value_taps + g_value_taps
        acc_state_taps = acc_state_taps + state_taps_total
        acc_step_bias = acc_step_bias + g_step_bias
        acc_log_decay = acc_log_decay + g_log_decay
        acc_skip = acc_skip + g_skip
    summed = (
        lax.psum_scatter(acc_gain, ("dp", "seq"), scatter_dimension=0, tiled=True),
        lax.psum_scatter(acc_gate, ("dp", "seq"), scatter_dimension=0, tiled=True),
        lax.psum_scatter(acc_value, ("dp", "seq"), scatter_dimension=0, tiled=True),
        lax.psum_scatter(acc_state, ("dp", "seq"), scatter_dimension=0, tiled=True),
        lax.psum_scatter(acc_step, ("dp", "seq"), scatter_dimension=0, tiled=True),
        lax.psum_scatter(acc_out, ("dp", "seq"), scatter_dimension=1, tiled=True),
    )
    smalls = lax.psum(
        (acc_value_taps, acc_state_taps, acc_step_bias, acc_log_decay, acc_skip, acc_mixer_gain),
        ("dp", "seq"),
    )
    return (
        jnp.stack(outputs),
        jnp.stack(input_grads),
        summed[0],
        summed[1],
        summed[2],
        summed[3],
        summed[4],
        summed[5],
        smalls[0],
        smalls[1],
        smalls[2],
        smalls[3],
        smalls[4],
        smalls[5],
    )


BF = jnp.bfloat16
F32 = jnp.float32
CHUNK = 256
VMEM = 40 * 1024 * 1024


def halves(x):
    top = x.astype(BF)
    return top, (x - top.astype(F32)).astype(BF)


def mm(a, b):
    return lax.dot_general(a, b, (((1,), (0,)), ((), ())), preferred_element_type=F32)


def mm_nt(a, b):
    return lax.dot_general(a, b, (((1,), (1,)), ((), ())), preferred_element_type=F32)


def mm3(a, b):
    wide = mm(a[0], jnp.concatenate([b[0], b[1]], axis=1))
    n = b[0].shape[1]
    return wide[:, :n] + wide[:, n:] + mm(a[1], b[0])


def mm3_nt(a, b):
    return mm_nt(a[0], b[0]) + mm_nt(a[0], b[1]) + mm_nt(a[1], b[0])


def softplus(x):
    return jnp.maximum(x, 0.0) + jnp.log1p(jnp.exp(-jnp.abs(x)))


def taps_applied(extended, taps):
    total = taps[CONV : CONV + 1, :]
    for k in range(CONV):
        total = total + extended[5 + k : 5 + k + CHUNK] * taps[k : k + 1, :]
    return total


def step_terms(step_ref, bias_ref, log_decay_ref):
    shifted_pre = step_ref[...] + bias_ref[...]
    step = softplus(shifted_pre)
    rates = jnp.exp(log_decay_ref[...])
    rows = lax.broadcasted_iota(jnp.int32, (CHUNK, CHUNK), 0)
    cols = lax.broadcasted_iota(jnp.int32, (CHUNK, CHUNK), 1)
    lower = jnp.where(rows >= cols, 1.0, 0.0).astype(F32)
    cum = jnp.dot(lower, -step * rates, precision=HIGH, preferred_element_type=F32)
    return shifted_pre, step, rates, cum


def by_pair(q, p):
    left = lax.broadcasted_iota(jnp.int32, (1, 128), 1) < 64
    return jnp.where(left, q[:, 2 * p : 2 * p + 1], q[:, 2 * p + 1 : 2 * p + 2])


def forward_kernel(
    vpre, spre, spre_step, vtaps, staps, bias, log_decay, skip, mixer, starts, state, vtail, stail
):
    @pl.when(pl.program_id(0) == 0)
    def _():
        state[...] = jnp.zeros_like(state)
        vtail[...] = jnp.zeros_like(vtail)
        stail[...] = jnp.zeros_like(stail)

    vx, sx = vpre[...], spre[...]
    values = jax.nn.silu(taps_applied(jnp.concatenate([vtail[...], vx], axis=0), vtaps[...]))
    states = jax.nn.silu(taps_applied(jnp.concatenate([stail[...], sx], axis=0), staps[...]))
    vtail[...] = vx[CHUNK - 8 :]
    stail[...] = sx[CHUNK - 8 :]
    b, c = states[:, :STATE], states[:, STATE:]
    shifted_pre, step, rates, cum = step_terms(spre_step, bias, log_decay)
    cum_t = cum.T
    final = cum[CHUNK - 1 :, :]
    grown, ending, whole = jnp.exp(cum), jnp.exp(final - cum), jnp.exp(final)
    b2, c2, bt2 = halves(b), halves(c), halves(b.T)
    scores = mm3_nt(c2, b2)
    rows = lax.broadcasted_iota(jnp.int32, (CHUNK, CHUNK), 0)
    cols = lax.broadcasted_iota(jnp.int32, (CHUNK, CHUNK), 1)
    barred = jnp.where(rows >= cols, 0.0, -1e30).astype(F32)
    left = lax.broadcasted_iota(jnp.int32, (1, 128), 1) < 64
    starts[0] = state[...]
    for p in range(vx.shape[1] // 128):
        lanes = slice(128 * p, 128 * p + 128)
        v = values[:, lanes]
        weighted = v * by_pair(step, p)
        w2 = halves(weighted)
        both = jnp.concatenate([w2[0], w2[1]], axis=1)
        parts = []
        for h in (2 * p, 2 * p + 1):
            mix = halves(jnp.exp(cum[:, h : h + 1] - cum_t[h : h + 1, :] + barred) * scores)
            wide = mm(mix[0], both)
            parts.append(wide[:, :128] + wide[:, 128:] + mm(mix[1], w2[0]))
        held = state[:, lanes]
        carried = by_pair(grown, p) * mm3(c2, halves(held))
        mixer[:, lanes] = jnp.where(left, parts[0], parts[1]) + carried + skip[:, lanes] * v
        state[:, lanes] = held * by_pair(whole, p) + mm3(bt2, halves(weighted * by_pair(ending, p)))


def forward_scan(vpre, spre, step_pre, vtaps, staps, bias, log_decay, skip):
    tokens, width = vpre.shape
    chunks = tokens // CHUNK
    row = lambda n: pl.BlockSpec((CHUNK, n), lambda i: (i, 0))
    fixed = lambda x: pl.BlockSpec(x.shape, lambda i: (0, 0))
    return pl.pallas_call(
        forward_kernel,
        grid=(chunks,),
        in_specs=[row(width), row(2 * STATE), row(128)]
        + [fixed(x) for x in (vtaps, staps, bias, log_decay, skip)],
        out_specs=[row(width), pl.BlockSpec((1, STATE, width), lambda i: (i, 0, 0))],
        out_shape=[
            jax.ShapeDtypeStruct((tokens, width), F32),
            jax.ShapeDtypeStruct((chunks, STATE, width), F32),
        ],
        scratch_shapes=[
            pltpu.VMEM((STATE, width), F32),
            pltpu.VMEM((8, width), F32),
            pltpu.VMEM((8, 2 * STATE), F32),
        ],
        compiler_params=pltpu.CompilerParams(vmem_limit_bytes=VMEM),
        cost_estimate=pl.CostEstimate(
            flops=chunks * 12 * 4 * CHUNK * CHUNK * 256,
            bytes_accessed=tokens * width * 8,
            transcendentals=chunks * 12 * CHUNK * CHUNK,
        ),
        name="scan_forward",
    )(vpre, spre, step_pre, vtaps, staps, bias, log_decay, skip)


def silu_slope(total):
    s = jax.nn.sigmoid(total)
    return s * (1.0 + total * (1.0 - s))


def taps_back(d_total, later, taps):
    extended = jnp.concatenate([d_total, later], axis=0)
    result = 0.0
    for k in range(CONV):
        result = result + extended[3 - k : 3 - k + CHUNK] * taps[k : k + 1, :]
    return result


def taps_grads(d_total, extended):
    rows = [
        jnp.sum(d_total * extended[5 + k : 5 + k + CHUNK], axis=0, keepdims=True)
        for k in range(CONV)
    ]
    return rows + [jnp.sum(d_total, axis=0, keepdims=True)]


def backward_kernel(
    vpre, vbefore, spre, sbefore, spre_step, vtaps, staps, bias, log_decay, skip, chooser,
    mixer, d_mixer, starts,
    values_low, d_spre, step_low, value_sums, state_sums, step_sums,
    later_grad, later_state, vhead, shead, products, d_values,
):
    place = pl.program_id(0)

    @pl.when(place == 0)
    def _():
        for ref in (later_grad, later_state, vhead, shead, value_sums, state_sums, step_sums):
            ref[...] = jnp.zeros_like(ref)

    first = place == pl.num_programs(0) - 1
    vx, sx = vpre[...], spre[...]
    vext = jnp.concatenate([jnp.where(first, 0.0, vbefore[...]), vx], axis=0)
    sext = jnp.concatenate([jnp.where(first, 0.0, sbefore[...]), sx], axis=0)
    vtotal, stotal = taps_applied(vext, vtaps[...]), taps_applied(sext, staps[...])
    values, states = jax.nn.silu(vtotal), jax.nn.silu(stotal)
    b, c = states[:, :STATE], states[:, STATE:]
    shifted_pre, step, rates, cum = step_terms(spre_step, bias, log_decay)
    cum_t = cum.T
    final = cum[CHUNK - 1 :, :]
    grown, ending, whole = jnp.exp(cum), jnp.exp(final - cum), jnp.exp(final)
    b2, c2, ct2 = halves(b), halves(c), halves(c.T)
    scores_t = mm3_nt(b2, c2)
    rows = lax.broadcasted_iota(jnp.int32, (CHUNK, CHUNK), 0)
    cols = lax.broadcasted_iota(jnp.int32, (CHUNK, CHUNK), 1)
    barred = jnp.where(cols >= rows, 0.0, -1e30).astype(F32)
    left = lax.broadcasted_iota(jnp.int32, (1, 128), 1) < 64
    zero = jnp.zeros((CHUNK, 128), BF)
    d_scores_t = jnp.zeros((CHUNK, CHUNK), F32)
    d_b = jnp.zeros((CHUNK, STATE), F32)
    d_c = jnp.zeros((CHUNK, STATE), F32)
    skip_rows = []
    final_rows = []
    pairs = vx.shape[1] // 128
    for p in range(pairs):
        lanes = slice(128 * p, 128 * p + 128)
        v, dy = values[:, lanes], d_mixer[:, lanes]
        weighted = v * by_pair(step, p)
        w2, d2 = halves(weighted), halves(dy)
        both = jnp.concatenate([d2[0], d2[1]], axis=1)
        w_rest = pltpu.roll(weighted - w2[0].astype(F32), 64, 1).astype(BF)
        d_top = pltpu.roll(d2[0].astype(F32), 64, 1).astype(BF)
        parts = []
        for h, mine in ((2 * p, left), (2 * p + 1, ~left)):
            decay = jnp.exp(cum_t[h : h + 1, :] - cum[:, h : h + 1] + barred)
            mix = halves(decay * scores_t)
            wide = mm(mix[0], both)
            parts.append(wide[:, :128] + wide[:, 128:] + mm(mix[1], d2[0]))
            one = jnp.concatenate(
                [jnp.where(mine, w2[0], w_rest), jnp.where(mine, w2[0], zero)], axis=1
            )
            other = jnp.concatenate(
                [jnp.where(mine, d2[0], d_top), jnp.where(mine, d2[1], zero)], axis=1
            )
            d_scores_t = d_scores_t + mm_nt(one, other) * decay
        held, after = starts[0, :, lanes], later_grad[:, lanes]
        after2 = halves(after)
        ends = by_pair(ending, p)
        d_weighted = jnp.where(left, parts[0], parts[1]) + ends * mm3(b2, after2)
        gain = skip[:, lanes]
        products[:, lanes] = dy * (mixer[:, lanes] - gain * v)
        products[:, 128 * (pairs + p) : 128 * (pairs + p) + 128] = v * d_weighted
        d_values[:, lanes] = by_pair(step, p) * d_weighted + gain * dy
        skip_rows.append(jnp.sum(v * dy, axis=0, keepdims=True))
        final_rows.append(jnp.sum(after * later_state[:, lanes], axis=0, keepdims=True))
        faded = halves(by_pair(grown, p) * dy)
        d_c = d_c + mm3_nt(faded, halves(held))
        d_b = d_b + mm3_nt(halves(weighted * ends), after2)
        later_grad[:, lanes] = after * by_pair(whole, p) + mm3(ct2, faded)
    later_state[...] = starts[0]
    d2 = halves(d_scores_t)
    dt2 = halves(d_scores_t.T)
    d_b = d_b + mm3(d2, c2)
    d_c = d_c + mm3(dt2, b2)
    width = 128 * pairs
    pick = chooser[...]

    def by_head(x):
        top, rest = halves(x)
        return mm(top, pick) + mm(rest, pick)

    reached = by_head(products[:, :width])
    pulled = by_head(products[:, width:])
    at_end = by_head(jnp.broadcast_to(jnp.concatenate(final_rows, axis=1), (8, width)))[:1]
    rows128 = lax.broadcasted_iota(jnp.int32, (CHUNK, 128), 0)
    d_cum = reached - step * pulled + jnp.where(rows128 == CHUNK - 1, at_end, 0.0)
    upper = jnp.where(cols >= rows, 1.0, 0.0).astype(F32)
    d_rate = jnp.dot(upper, d_cum, precision=HIGH, preferred_element_type=F32)
    d_step = pulled - rates * d_rate
    d_shifted = d_step * jax.nn.sigmoid(shifted_pre)
    step_low[...] = d_shifted.astype(BF)
    step_sums[0:1, :] += jnp.sum(d_shifted, axis=0, keepdims=True)
    step_sums[1:2, :] -= jnp.sum(d_rate * step, axis=0, keepdims=True) * rates
    d_vtotal = d_values[...] * silu_slope(vtotal)
    values_low[...] = taps_back(d_vtotal, vhead[...], vtaps[...]).astype(BF)
    value_sums[...] += jnp.concatenate(
        taps_grads(d_vtotal, vext)
        + [jnp.concatenate(skip_rows, axis=1), jnp.zeros((2, width), F32)],
        axis=0,
    )
    vhead[...] = d_vtotal[:8]
    d_stotal = jnp.concatenate([d_b, d_c], axis=1) * silu_slope(stotal)
    d_spre[...] = taps_back(d_stotal, shead[...], staps[...])
    state_sums[...] += jnp.concatenate(
        taps_grads(d_stotal, sext) + [jnp.zeros((3, 2 * STATE), F32)], axis=0
    )
    shead[...] = d_stotal[:8]


def backward_scan(
    vpre, spre, step_pre, vtaps, staps, bias, log_decay, skip, mixer, d_mixer, starts
):
    tokens, width = vpre.shape
    chunks = tokens // CHUNK
    heads = jnp.arange(width)[:, None] // 64
    chooser = (heads == jnp.arange(128)[None, :]).astype(BF)
    row = lambda n: pl.BlockSpec((CHUNK, n), lambda i: (chunks - 1 - i, 0))
    before = lambda n: pl.BlockSpec(
        (8, n), lambda i: (jnp.maximum((chunks - 1 - i) * (CHUNK // 8) - 1, 0), 0)
    )
    fixed = lambda x: pl.BlockSpec(x.shape, lambda i: (0, 0))
    summed = lambda n: pl.BlockSpec((8, n), lambda i: (0, 0))
    return pl.pallas_call(
        backward_kernel,
        grid=(chunks,),
        in_specs=[row(width), before(width), row(2 * STATE), before(2 * STATE), row(128)]
        + [fixed(x) for x in (vtaps, staps, bias, log_decay, skip, chooser)]
        + [row(width), row(width), pl.BlockSpec((1, STATE, width), lambda i: (chunks - 1 - i, 0, 0))],
        out_specs=[
            row(width), row(2 * STATE), row(128), summed(width), summed(2 * STATE), summed(128),
        ],
        out_shape=[
            jax.ShapeDtypeStruct((tokens, width), BF),
            jax.ShapeDtypeStruct((tokens, 2 * STATE), F32),
            jax.ShapeDtypeStruct((tokens, 128), BF),
            jax.ShapeDtypeStruct((8, width), F32),
            jax.ShapeDtypeStruct((8, 2 * STATE), F32),
            jax.ShapeDtypeStruct((8, 128), F32),
        ],
        scratch_shapes=[
            pltpu.VMEM((STATE, width), F32),
            pltpu.VMEM((STATE, width), F32),
            pltpu.VMEM((8, width), F32),
            pltpu.VMEM((8, 2 * STATE), F32),
            pltpu.VMEM((CHUNK, 2 * width), F32),
            pltpu.VMEM((CHUNK, width), F32),
        ],
        compiler_params=pltpu.CompilerParams(vmem_limit_bytes=VMEM),
        cost_estimate=pl.CostEstimate(
            flops=chunks * 12 * 8 * CHUNK * CHUNK * 256,
            bytes_accessed=tokens * width * 16,
            transcendentals=chunks * 12 * CHUNK * CHUNK,
        ),
        name="scan_backward",
    )(vpre, vpre, spre, spre, step_pre, vtaps, staps, bias, log_decay, skip, chooser, mixer, d_mixer, starts)


def place(arrays, piece, targets, rows):
    count = sum(x.shape[0] // piece for x in arrays)
    assert count == len(targets)
    width, dtype = arrays[0].shape[1], arrays[0].dtype

    def kernel(at, *refs):
        sources, out, done = refs[: len(arrays)], refs[len(arrays)], refs[len(arrays) + 1]
        copies = []
        for source in sources:
            for j in range(source.shape[0] // piece):
                k = len(copies)
                start = pl.multiple_of(at[k], piece)
                copies.append(
                    pltpu.make_async_copy(
                        source.at[pl.ds(j * piece, piece)], out.at[pl.ds(start, piece)], done.at[k]
                    )
                )
        for copy in copies:
            copy.start()
        for copy in copies:
            copy.wait()

    return pl.pallas_call(
        kernel,
        grid_spec=pltpu.PrefetchScalarGridSpec(
            num_scalar_prefetch=1,
            grid=(1,),
            in_specs=[pl.BlockSpec(memory_space=pl.ANY)] * len(arrays),
            out_specs=pl.BlockSpec(memory_space=pltpu.VMEM),
            scratch_shapes=[pltpu.SemaphoreType.DMA((count,))],
        ),
        out_shape=jax.ShapeDtypeStruct((rows, width), dtype),
        compiler_params=pltpu.CompilerParams(vmem_limit_bytes=16 * 1024 * 1024),
        cost_estimate=pl.CostEstimate(
            flops=0, bytes_accessed=2 * rows * width * dtype.itemsize, transcendentals=0
        ),
        name="place",
    )(jnp.stack([jnp.asarray(t, jnp.int32) for t in targets]), *arrays)


def swap(x, axis, bit=1):
    return lax.ppermute(x, axis, [(i, i ^ bit) for i in range(lax.axis_size(axis))])


def turned(x, axis, distance):
    n = lax.axis_size(axis)
    return lax.ppermute(x, axis, [(i, (i + distance) % n) for i in range(n)])


def at(x, index, axis):
    return lax.dynamic_index_in_dim(x, index, axis, keepdims=False)


def part(x, index, size, axis):
    return lax.dynamic_slice_in_dim(x, index * size, size, axis)


def ordered(flag, mine, other, axis):
    first = jnp.where(flag == 0, mine, other)
    second = jnp.where(flag == 0, other, mine)
    return jnp.concatenate([first, second], axis=axis)


def whole_sequences(
    block_input, output_grad, input_gain, gate_weight, value_weight, state_weight, step_weight,
    out_weight, value_taps, state_taps, step_bias, log_decay, skip_gain, mixer_gain,
):
    xi, ci, zi, yi = (lax.axis_index(n) for n in ("x", "core", "seq", "heads"))
    nz = lax.axis_size("seq")
    nx = lax.axis_size("x")
    d_model = block_input.shape[-1]
    group = block_input.shape[2]
    sub = group // 4
    tokens = group * nz
    own = sub * nz
    rows = gate_weight.shape[0]
    cols = gate_weight.shape[1] // 2
    heads = step_weight.shape[1] // 2
    slot = 2 * (zi // 2) + ci

    def tokens_in(x):
        rounds = []
        for r in range(nz):
            j = zi ^ r
            start = yi * (2 * sub) + (j % 2) * sub
            piece = lax.dynamic_slice(x, (j // 2, 0, start, 0), (1, 1, sub, d_model))
            route = [
                (c * nz + z, ((z ^ r) % 2) * nz + 2 * ((z ^ r) // 2) + c)
                for c in range(2)
                for z in range(nz)
            ]
            rounds.append(lax.ppermute(piece.reshape(sub, d_model), ("core", "seq"), route))
        return place(rounds, sub, [(slot ^ r) * sub for r in range(nz)], own)

    def tokens_back(x):
        mine, other = [], []
        for r in range(nz):
            piece = part(x, slot ^ r, sub, 0)
            route = [
                (((z ^ r) % 2) * nz + 2 * ((z ^ r) // 2) + c, c * nz + z)
                for c in range(2)
                for z in range(nz)
            ]
            mine.append(lax.ppermute(piece, ("core", "seq"), route))
            other.append(swap(mine[-1], "heads"))
        targets = [
            (((zi ^ r) // 2) * 4 + 2 * y + (zi ^ r) % 2) * sub
            for y in (yi, 1 - yi)
            for r in range(nz)
        ]
        return place(mine + other, sub, targets, 2 * group).reshape(block_input.shape)

    def spread(x):
        by_y = swap(x, "heads")
        by_core = swap(x, "core")
        by_both = swap(by_y, "core")
        targets = [
            (4 * k + 2 * y + c) * sub
            for y, c in ((yi, ci), (1 - yi, ci), (yi, 1 - ci), (1 - yi, 1 - ci))
            for k in range(nz)
        ]
        return place([x, by_y, by_core, by_both], sub, targets, tokens), by_core

    def reduced(x, link=BF):
        split = x.reshape(nz, 2, 2, sub, x.shape[-1])
        summed = at(split, ci, 2) + swap(at(split, 1 - ci, 2), "core")
        sent = swap(at(summed, 1 - yi, 1).astype(link), "heads").astype(F32)
        return (at(summed, yi, 1) + sent).reshape(own, x.shape[-1])

    def gathered(weight):
        width = weight.shape[1] // 2
        received = swap(part(weight, 1 - ci, width, 1), "core")
        block = ordered(ci, part(weight, ci, width, 1), received, 0)
        right = turned(block, "seq", 1)
        left = turned(block, "seq", -1)
        across = swap(block, "x")
        far = turned(right, "seq", 1)
        blocks = [block, right, left, far, across]
        blocks += [swap(right, "x"), swap(left, "x"), swap(far, "x")]
        targets = [
            ((x * 2 + c) * nz + z % nz) * rows
            for x in (xi, 1 - xi)
            for z in (zi, zi + nz - 1, zi + 1, zi + 2)
            for c in range(2)
        ]
        return place(blocks, rows, targets, d_model)

    def scattered(grad):
        half = d_model // 2
        summed = part(grad, xi, half, 0) + swap(
            part(grad, 1 - xi, half, 0).astype(BF), "x"
        ).astype(F32)
        summed = summed.reshape(2, nz, rows, grad.shape[1])
        total = at(summed, zi, 1)
        for d in range(1, nz):
            sent = at(summed, (zi + d) % nz, 1).astype(BF)
            total = total + turned(sent, "seq", d).astype(F32)
        return total

    def to_core(total):
        received = swap(at(total, 1 - ci, 0), "core")
        return at(total, ci, 0), received

    gain = ordered(ci, input_gain[None], swap(input_gain[None], "core"), 0)
    near = [gain] + [turned(gain, "seq", d) for d in range(1, nz)]
    by_z = jnp.stack(near)[(zi - jnp.arange(nz)) % nz]
    gain = ordered(xi, by_z[None], swap(by_z[None], "x"), 0)
    gain = jnp.transpose(gain, (0, 2, 1, 3)).reshape(1, d_model).astype(F32)

    kept = tokens_in(block_input)
    x_own = kept.astype(F32)
    scaling = lax.rsqrt(jnp.mean(x_own * x_own, axis=-1, keepdims=True) + EPS)
    normed_own = (x_own * scaling * gain).astype(BF)
    normed, normed_core = spread(normed_own)

    pad = 128 - heads
    first = jnp.concatenate(
        [
            jnp.concatenate(
                [
                    value_weight[:, cols * k : cols * k + cols],
                    state_weight[:, STATE * k : STATE * k + STATE],
                    step_weight[:, heads * k : heads * k + heads],
                    jnp.zeros((rows, pad), BF),
                ],
                axis=1,
            )
            for k in range(2)
        ],
        axis=1,
    )
    first_full = gathered(first)
    gate_full = gathered(gate_weight)
    og_own = tokens_in(output_grad)
    og, og_core = spread(og_own)
    out_full = gathered(out_weight.T)

    project = lambda a, b: jnp.dot(a, b, preferred_element_type=F32)
    weights_in = (first_full[:, :cols], first_full[:, cols : cols + STATE], first_full[:, cols + STATE :])
    values_pre = project(normed, weights_in[0])
    states_half = project(normed, weights_in[1])
    step_pre = project(normed, weights_in[2])
    states_pre = ordered(ci, states_half, swap(states_half, "core"), 1)

    vtaps = part(value_taps, ci, cols, 1)
    lanes = lambda v: jnp.pad(part(v, ci, heads, 0), (0, pad))[None]
    bias, decays = lanes(step_bias), lanes(log_decay)
    skip = jnp.repeat(part(skip_gain, ci, heads, 0), cols // heads)[None]
    gain_mixer = part(mixer_gain, ci, cols, 0)[None]
    mixer, starts = forward_scan(
        values_pre, states_pre, step_pre, vtaps, state_taps, bias, decays, skip
    )
    gate_lin = project(normed, gate_full)
    d_out = project(og, out_full)
    sigmoid_gate = jax.nn.sigmoid(gate_lin)
    silu_gate = gate_lin * sigmoid_gate
    gated = mixer * silu_gate
    weighted = d_out * gain_mixer
    sums = jnp.stack([jnp.sum(gated * gated, axis=1), jnp.sum(weighted * gated, axis=1)])
    sums = sums + swap(sums, "core")
    sums = sums + swap(sums, "heads")
    inverse = lax.rsqrt(sums[0] / INNER + EPS)[:, None]
    out_normed = (gated * inverse * gain_mixer).astype(BF)
    d_gated = inverse * weighted - gated * (inverse * inverse * inverse) * (sums[1][:, None] / INNER)
    d_mixer = d_gated * silu_gate
    gate_low = (d_gated * mixer * sigmoid_gate * (1.0 + gate_lin * (1.0 - sigmoid_gate))).astype(BF)
    g_mixer_gain = jnp.sum(d_out * gated * inverse, axis=0)

    transposed = lambda a, b: lax.dot_general(
        a, b, (((0,), (0,)), ((), ())), preferred_element_type=F32
    )
    back = lambda a, b: lax.dot_general(a, b, (((1,), (1,)), ((), ())), preferred_element_type=F32)
    g_out = scattered(transposed(og, out_normed))
    g_gate = scattered(transposed(normed, gate_low))
    branch = reduced(back(out_normed, out_full))
    block_output = tokens_back((x_own + branch).astype(BF))

    values_low, d_states, step_low, value_sums, state_sums, step_sums = backward_scan(
        values_pre, states_pre, step_pre, vtaps, state_taps, bias, decays, skip, mixer, d_mixer, starts
    )
    states_own = reduced(d_states, F32).astype(BF)
    g_value = scattered(transposed(normed, values_low))
    d_normed = reduced(
        back(gate_low, gate_full) + back(values_low, weights_in[0]) + back(step_low, weights_in[2])
    )
    states_weights = ordered(ci, weights_in[1], swap(weights_in[1], "core"), 1)
    d_normed = d_normed + back(states_own, states_weights)
    states_both = jnp.concatenate([states_own, swap(states_own, "core")], axis=0)
    normed_both = jnp.concatenate([normed_own, normed_core], axis=0)
    g_small = scattered(
        jnp.concatenate(
            [
                transposed(normed_both, part(states_both, ci, STATE, 1)),
                transposed(normed, step_low),
            ],
            axis=1,
        )
    )

    pushed = d_normed * gain
    d_tokens = scaling * pushed - x_own * (scaling * scaling * scaling) * jnp.mean(
        pushed * x_own, axis=-1, keepdims=True
    )
    grad_input = tokens_back((og_own.astype(F32) + d_tokens).astype(BF))
    g_input_gain = jnp.sum(d_normed * x_own * scaling, axis=0)

    per_core = jnp.concatenate(
        [value_sums[:6], g_mixer_gain[None], jnp.pad(step_sums[:2].reshape(1, -1), ((0, 0), (0, cols - 256)))],
        axis=0,
    ).reshape(-1, 256)
    shared = jnp.concatenate([state_sums, g_input_gain.reshape(-1, 256)], axis=0)
    n_core = per_core.shape[0]
    pack = jnp.concatenate([per_core, shared], axis=0)
    pack = pack + swap(pack, "x")
    pack = pack + swap(pack, "seq", 1)
    pack = pack + swap(pack, "seq", 2)
    other = swap(pack, "core")
    shared = pack[n_core:] + other[n_core:]
    shared = shared + swap(shared, "heads")
    both = ordered(ci, pack[:n_core].reshape(1, 8, cols), other[:n_core].reshape(1, 8, cols), 0)
    by_channel = jnp.transpose(both, (1, 0, 2)).reshape(8, 2 * cols)
    per_head = both[:, 7, :256].reshape(2, 2, 128)[:, :, :heads]
    input_gain_all = shared[8:].reshape(nx, 2, nz, rows)
    my_gain = at(at(at(input_gain_all, xi, 0), ci, 0), zi, 0)

    widths = lambda total: ordered(ci, *to_core(total), 1)
    small_mine, small_other = to_core(g_small)
    g_state = ordered(ci, small_mine[:, :STATE], small_other[:, :STATE], 1)
    g_state = g_state + swap(g_state, "heads")
    g_step = ordered(ci, small_mine[:, STATE : STATE + heads], small_other[:, STATE : STATE + heads], 1)
    return (
        block_output,
        grad_input,
        my_gain,
        widths(g_gate),
        widths(g_value),
        g_state,
        g_step,
        widths(g_out).T,
        by_channel[:5],
        shared[:5],
        per_head[:, 0].reshape(-1),
        per_head[:, 1].reshape(-1),
        jnp.sum(by_channel[5].reshape(2 * heads, -1), axis=1),
        by_channel[6],
    )


def solution(mesh):
    sizes = dict(mesh.shape)
    if sizes["seq"] == 2 * MB and sizes["dp"] == 4 and sizes["heads"] == 2:
        devices = mesh.devices.reshape(sizes["dp"] // 2, 2, sizes["seq"], sizes["heads"])
        mesh = jax.sharding.Mesh(devices, ("x", "core", "seq", "heads"))
        body, dp = whole_sequences, ("x", "core")
    else:
        body, dp = shards, ("dp",)
    tokens = P(None, dp, "seq", None)
    both = (*dp, "seq")
    return jax.shard_map(
        body,
        mesh=mesh,
        in_specs=(
            tokens,
            tokens,
            P(both),
            P(both, "heads"),
            P(both, "heads"),
            P(both, None),
            P(both, "heads"),
            P("heads", both),
            P(None, "heads"),
            P(),
            P("heads"),
            P("heads"),
            P("heads"),
            P("heads"),
        ),
        out_specs=(
            tokens,
            tokens,
            P(both),
            P(both, "heads"),
            P(both, "heads"),
            P(both, None),
            P(both, "heads"),
            P("heads", both),
            P(None, "heads"),
            P(),
            P("heads"),
            P("heads"),
            P("heads"),
            P("heads"),
        ),
        check_vma=False,
    )
```

```python
import functools

import jax
import jax.numpy as jnp
from jax import lax
from jax.experimental import pallas as pl
from jax.experimental.pallas import tpu as pltpu
from jax.sharding import PartitionSpec as P

STATE = 128
CONV = 4
MB = 2
INNER = 3072


EPS = 1e-05
HIGH = lax.Precision.HIGHEST


def shifted(block, axis, distance):
    devices = range(lax.axis_size(axis))
    route = [(i - distance, i) for i in devices if i - distance in devices]
    return lax.ppermute(block, axis, route)


def entering(x, axis, combine, identity, reverse):
    peers, index = (lax.axis_size(axis), lax.axis_index(axis))
    everything = jax.tree.map(lambda part: lax.all_gather(part, axis), x)
    start = jax.tree.map(
        lambda part, zero: jnp.broadcast_to(jnp.asarray(zero, part.dtype), part.shape), x, identity
    )

    def step(k, before):
        at = peers - 1 - k if reverse else k
        reached = at > index if reverse else at < index
        new = combine(before, jax.tree.map(lambda part: part[at], everything))
        return jax.tree.map(lambda a, b: jnp.where(reached, a, b), new, before)

    return lax.fori_loop(0, peers, step, start)


def norm_rows(values, gain):
    return values * lax.rsqrt(jnp.mean(values * values, axis=-1, keepdims=True) + EPS) * gain


def conv_silu(extended, taps):
    length = extended.shape[1] - (CONV - 1)
    total = jnp.zeros((extended.shape[0], length, extended.shape[2]), jnp.float32) + taps[CONV]
    for offset in range(CONV):
        total = total + extended[:, offset : offset + length] * taps[offset]
    return jax.nn.silu(total)


def local_parts(
    values_ext, states_ext, step_pre, value_taps, state_taps, step_bias, log_decay, skip_gain
):
    values_conv = conv_silu(values_ext, value_taps)
    states_conv = conv_silu(states_ext, state_taps)
    batch, length, channels = values_conv.shape
    heads_here = step_pre.shape[-1]
    values = values_conv.reshape(batch, length, heads_here, channels // heads_here)
    input_mat = states_conv[..., :STATE]
    output_mat = states_conv[..., STATE:]
    stepsize = jax.nn.softplus(step_pre + step_bias)
    cumulative = jnp.cumsum(-stepsize * jnp.exp(log_decay), axis=1)
    gaps = cumulative[:, :, None, :] - cumulative[:, None, :, :]
    causal = (jnp.arange(length)[:, None] >= jnp.arange(length)[None, :])[None, :, :, None]
    decays = jnp.where(causal, jnp.exp(jnp.where(causal, gaps, 0.0)), 0.0)
    scores = jnp.einsum("btn,bsn->bts", output_mat, input_mat, precision=HIGH)
    weights = decays * scores[..., None] * stepsize[:, None, :, :]
    within = (
        jnp.einsum("btsh,bshp->bthp", weights, values, precision=HIGH) + skip_gain[:, None] * values
    )
    final = cumulative[:, -1]
    ending = jnp.exp(final[:, None, :] - cumulative) * stepsize
    local_state = jnp.einsum("bth,btn,bthp->bhnp", ending, input_mat, values, precision=HIGH)
    return (within, local_state, jnp.exp(final), cumulative, output_mat)


def carried_part(cumulative, output_mat, state_in):
    return jnp.exp(cumulative)[..., None] * jnp.einsum(
        "btn,bhnp->bthp", output_mat, state_in, precision=HIGH
    )


def whole_block(
    values_ext,
    states_ext,
    step_pre,
    value_taps,
    state_taps,
    step_bias,
    log_decay,
    skip_gain,
    state_in,
):
    within, local_state, span_decay, cumulative, output_mat = local_parts(
        values_ext, states_ext, step_pre, value_taps, state_taps, step_bias, log_decay, skip_gain
    )
    result = within + carried_part(cumulative, output_mat, state_in)
    return (result.reshape(result.shape[0], result.shape[1], -1), local_state, span_decay)


def compose(earlier, later):
    return (earlier[0] * later[0], later[0][..., None, None] * earlier[1] + later[1])


def shards(
    block_input,
    output_grad,
    input_gain,
    gate_weight,
    value_weight,
    state_weight,
    step_weight,
    out_weight,
    value_taps,
    state_taps,
    step_bias,
    log_decay,
    skip_gain,
    mixer_gain,
):
    margin = CONV - 1
    width = block_input.shape[-1]
    inner_here = gate_weight.shape[1]
    state_cols = state_weight.shape[1]
    heads_here = step_weight.shape[1]
    acc_gain = jnp.zeros((width,), jnp.float32)
    acc_gate = jnp.zeros((width, inner_here), jnp.float32)
    acc_value = jnp.zeros((width, inner_here), jnp.float32)
    acc_state = jnp.zeros((width, state_cols), jnp.float32)
    acc_step = jnp.zeros((width, heads_here), jnp.float32)
    acc_out = jnp.zeros((inner_here, width), jnp.float32)
    acc_value_taps = jnp.zeros_like(value_taps)
    acc_state_taps = jnp.zeros_like(state_taps)
    acc_step_bias = jnp.zeros_like(step_bias)
    acc_log_decay = jnp.zeros_like(log_decay)
    acc_skip = jnp.zeros_like(skip_gain)
    acc_mixer_gain = jnp.zeros_like(mixer_gain)
    outputs = []
    input_grads = []
    for micro_batch in range(MB):
        weights_now = (
            lax.all_gather(input_gain, ("dp", "seq"), axis=0, tiled=True),
            lax.all_gather(gate_weight, ("dp", "seq"), axis=0, tiled=True),
            lax.all_gather(value_weight, ("dp", "seq"), axis=0, tiled=True),
            lax.all_gather(state_weight, ("dp", "seq"), axis=0, tiled=True),
            lax.all_gather(step_weight, ("dp", "seq"), axis=0, tiled=True),
            lax.all_gather(out_weight, ("dp", "seq"), axis=1, tiled=True),
        )
        gain_full, gate_full, value_full, state_full, step_full, out_full = weights_now
        tokens = block_input[micro_batch].astype(jnp.float32)
        normed = norm_rows(tokens, gain_full.astype(jnp.float32)).astype(jnp.bfloat16)
        gate_lin = jnp.einsum("btd,di->bti", normed, gate_full, preferred_element_type=jnp.float32)
        values_pre = jnp.einsum(
            "btd,di->bti", normed, value_full, preferred_element_type=jnp.float32
        )
        states_pre = jnp.einsum(
            "btd,di->bti", normed, state_full, preferred_element_type=jnp.float32
        )
        step_pre = jnp.einsum("btd,di->bti", normed, step_full, preferred_element_type=jnp.float32)
        outgoing = jnp.concatenate([values_pre[:, -margin:], states_pre[:, -margin:]], axis=2)
        incoming = shifted(outgoing, "seq", 1)
        values_ext = jnp.concatenate([incoming[..., :inner_here], values_pre], axis=1)
        states_ext = jnp.concatenate([incoming[..., inner_here:], states_pre], axis=1)
        within, local_state, span_decay, cumulative, output_mat = local_parts(
            values_ext,
            states_ext,
            step_pre,
            value_taps,
            state_taps,
            step_bias,
            log_decay,
            skip_gain,
        )
        prefix = entering(
            (span_decay, local_state),
            "seq",
            compose,
            (jnp.ones_like(span_decay), jnp.zeros_like(local_state)),
            False,
        )
        state_in = prefix[1]
        mixer = (within + carried_part(cumulative, output_mat, state_in)).reshape(gate_lin.shape)
        silu_gate = jax.nn.silu(gate_lin)
        gated = mixer * silu_gate
        total_sq = lax.psum(jnp.sum(gated * gated, axis=-1), "heads")
        inverse = lax.rsqrt(total_sq / INNER + EPS)[..., None]
        out_normed = (gated * inverse * mixer_gain).astype(jnp.bfloat16)
        partial_out = jnp.einsum(
            "bti,id->btd", out_normed, out_full, preferred_element_type=jnp.float32
        )
        branch = lax.psum(partial_out, "heads")
        outputs.append((tokens + branch).astype(jnp.bfloat16))
        weights_back = (
            lax.all_gather(input_gain, ("dp", "seq"), axis=0, tiled=True),
            lax.all_gather(gate_weight, ("dp", "seq"), axis=0, tiled=True),
            lax.all_gather(value_weight, ("dp", "seq"), axis=0, tiled=True),
            lax.all_gather(state_weight, ("dp", "seq"), axis=0, tiled=True),
            lax.all_gather(step_weight, ("dp", "seq"), axis=0, tiled=True),
            lax.all_gather(out_weight, ("dp", "seq"), axis=1, tiled=True),
        )
        gain_full, gate_full, value_full, state_full, step_full, out_full = weights_back
        grad_out = output_grad[micro_batch]
        d_out_normed = jnp.einsum(
            "btd,id->bti", grad_out, out_full, preferred_element_type=jnp.float32
        )
        acc_out = acc_out + jnp.einsum(
            "bti,btd->id", out_normed, grad_out, preferred_element_type=jnp.float32
        )
        acc_mixer_gain = acc_mixer_gain + jnp.sum(d_out_normed * gated * inverse, axis=(0, 1))
        weighted = d_out_normed * mixer_gain
        dot_total = lax.psum(jnp.sum(weighted * gated, axis=-1), "heads")
        d_gated = inverse * weighted - gated * (inverse * inverse * inverse) * (
            dot_total[..., None] / INNER
        )
        d_mixer = d_gated * silu_gate
        sigmoid_gate = jax.nn.sigmoid(gate_lin)
        d_gate_lin = d_gated * mixer * sigmoid_gate * (1.0 + gate_lin * (1.0 - sigmoid_gate))
        carry_grad = jnp.einsum(
            "bth,btn,bthp->bhnp",
            jnp.exp(cumulative),
            output_mat,
            d_mixer.reshape(within.shape),
            precision=HIGH,
        )
        suffix = entering(
            (span_decay, carry_grad),
            "seq",
            compose,
            (jnp.ones_like(span_decay), jnp.zeros_like(carry_grad)),
            True,
        )
        later_grad = suffix[1]
        d_decay = jnp.sum(later_grad * state_in, axis=(2, 3))
        ignored, pullback = jax.vjp(
            whole_block,
            values_ext,
            states_ext,
            step_pre,
            value_taps,
            state_taps,
            step_bias,
            log_decay,
            skip_gain,
            state_in,
        )
        (
            d_values_ext,
            d_states_ext,
            d_step_pre,
            g_value_taps,
            g_state_taps,
            g_step_bias,
            g_log_decay,
            g_skip,
            unused_state,
        ) = pullback((d_mixer, later_grad, d_decay))
        rim_grads = jnp.concatenate([d_values_ext[:, :margin], d_states_ext[:, :margin]], axis=2)
        returned = shifted(rim_grads, "seq", -1)
        d_values_pre = d_values_ext[:, margin:].at[:, -margin:].add(returned[..., :inner_here])
        d_states_pre = d_states_ext[:, margin:].at[:, -margin:].add(returned[..., inner_here:])
        gate_low = d_gate_lin.astype(jnp.bfloat16)
        values_low = d_values_pre.astype(jnp.bfloat16)
        step_low = d_step_pre.astype(jnp.bfloat16)
        d_normed_part = (
            jnp.einsum("bti,di->btd", gate_low, gate_full, preferred_element_type=jnp.float32)
            + jnp.einsum("bti,di->btd", values_low, value_full, preferred_element_type=jnp.float32)
            + jnp.einsum("bti,di->btd", step_low, step_full, preferred_element_type=jnp.float32)
        )
        d_normed_sum, d_states_total, state_taps_total = lax.psum(
            (d_normed_part, d_states_pre, g_state_taps), "heads"
        )
        states_low = d_states_total.astype(jnp.bfloat16)
        d_normed = d_normed_sum + jnp.einsum(
            "bti,di->btd", states_low, state_full, preferred_element_type=jnp.float32
        )
        acc_gate = acc_gate + jnp.einsum(
            "btd,bti->di", normed, gate_low, preferred_element_type=jnp.float32
        )
        acc_value = acc_value + jnp.einsum(
            "btd,bti->di", normed, values_low, preferred_element_type=jnp.float32
        )
        acc_state = acc_state + jnp.einsum(
            "btd,bti->di", normed, states_low, preferred_element_type=jnp.float32
        )
        acc_step = acc_step + jnp.einsum(
            "btd,bti->di", normed, step_low, preferred_element_type=jnp.float32
        )
        scaling = lax.rsqrt(jnp.mean(tokens * tokens, axis=-1, keepdims=True) + EPS)
        acc_gain = acc_gain + jnp.sum(d_normed * tokens * scaling, axis=(0, 1))
        pushed = d_normed * gain_full.astype(jnp.float32)
        d_tokens = scaling * pushed - tokens * (scaling * scaling * scaling) * jnp.mean(
            pushed * tokens, axis=-1, keepdims=True
        )
        input_grads.append((grad_out.astype(jnp.float32) + d_tokens).astype(jnp.bfloat16))
        acc_value_taps = acc_value_taps + g_value_taps
        acc_state_taps = acc_state_taps + state_taps_total
        acc_step_bias = acc_step_bias + g_step_bias
        acc_log_decay = acc_log_decay + g_log_decay
        acc_skip = acc_skip + g_skip
    summed = (
        lax.psum_scatter(acc_gain, ("dp", "seq"), scatter_dimension=0, tiled=True),
        lax.psum_scatter(acc_gate, ("dp", "seq"), scatter_dimension=0, tiled=True),
        lax.psum_scatter(acc_value, ("dp", "seq"), scatter_dimension=0, tiled=True),
        lax.psum_scatter(acc_state, ("dp", "seq"), scatter_dimension=0, tiled=True),
        lax.psum_scatter(acc_step, ("dp", "seq"), scatter_dimension=0, tiled=True),
        lax.psum_scatter(acc_out, ("dp", "seq"), scatter_dimension=1, tiled=True),
    )
    smalls = lax.psum(
        (acc_value_taps, acc_state_taps, acc_step_bias, acc_log_decay, acc_skip, acc_mixer_gain),
        ("dp", "seq"),
    )
    return (
        jnp.stack(outputs),
        jnp.stack(input_grads),
        summed[0],
        summed[1],
        summed[2],
        summed[3],
        summed[4],
        summed[5],
        smalls[0],
        smalls[1],
        smalls[2],
        smalls[3],
        smalls[4],
        smalls[5],
    )


BF = jnp.bfloat16
F32 = jnp.float32
CHUNK = 128
VMEM = 40 * 1024 * 1024


def halves(x):
    top = x.astype(BF)
    return top, (x - top.astype(F32)).astype(BF)


def mm(a, b):
    return lax.dot_general(a, b, (((1,), (0,)), ((), ())), preferred_element_type=F32)


def mm_nt(a, b):
    return lax.dot_general(a, b, (((1,), (1,)), ((), ())), preferred_element_type=F32)


def beside(pair):
    return jnp.concatenate(pair, axis=1)


def right_side(b):
    top, rest = b
    return jnp.concatenate([beside((top, rest)), beside((top, jnp.zeros_like(top)))], axis=0)


def right_side_nt(b):
    top, rest = b
    return jnp.concatenate([beside((top, top)), beside((rest, jnp.zeros_like(top)))], axis=0)


def folded(wide):
    n = wide.shape[1] // 2
    return wide[:, :n] + wide[:, n:]


def softplus(x):
    return jnp.maximum(x, 0.0) + jnp.log1p(jnp.exp(-jnp.abs(x)))


def taps_applied(extended, taps):
    total = taps[CONV : CONV + 1, :]
    for k in range(CONV):
        total = total + extended[5 + k : 5 + k + CHUNK] * taps[k : k + 1, :]
    return total


def square(which):
    return lax.broadcasted_iota(jnp.int32, (CHUNK, CHUNK), which)


def step_terms(step_ref, bias_ref, log_decay_ref):
    shifted_pre = step_ref[...] + bias_ref[...]
    step = softplus(shifted_pre)
    rates = jnp.exp(log_decay_ref[...])
    lower = jnp.where(square(0) >= square(1), 1.0, 0.0).astype(F32)
    cum = jnp.dot(lower, -step * rates, precision=HIGH, preferred_element_type=F32)
    return shifted_pre, step, rates, cum


def by_pair(q, p):
    left = lax.broadcasted_iota(jnp.int32, (1, 128), 1) < 64
    return jnp.where(left, q[:, 2 * p : 2 * p + 1], q[:, 2 * p + 1 : 2 * p + 2])


def forward_kernel(
    vpre, spre, spre_step, vtaps, staps, bias, log_decay, skip,
    mixer, starts, vtotal, stotal, state, vtail, stail,
):
    @pl.when(pl.program_id(0) == 0)
    def _():
        state[...] = jnp.zeros_like(state)
        vtail[...] = jnp.zeros_like(vtail)
        stail[...] = jnp.zeros_like(stail)

    sx = spre[...]
    total = taps_applied(jnp.concatenate([stail[...], sx], axis=0), staps[...])
    stotal[...] = total
    states = jax.nn.silu(total)
    stail[...] = sx[CHUNK - 8 :]
    b, c = states[:, :STATE], states[:, STATE:]
    shifted_pre, step, rates, cum = step_terms(spre_step, bias, log_decay)
    cum_t = cum.T
    final = cum[CHUNK - 1 :, :]
    grown, ending, whole = jnp.exp(cum), jnp.exp(final - cum), jnp.exp(final)
    c_left, bt_left = beside(halves(c)), beside(halves(b.T))
    scores = folded(mm_nt(c_left, right_side_nt(halves(b))))
    scores = jnp.where(square(0) >= square(1), scores, 0.0)
    left = lax.broadcasted_iota(jnp.int32, (1, 128), 1) < 64
    starts[0] = state[...]
    for p in range(vpre.shape[1] // 128):
        lanes = slice(128 * p, 128 * p + 128)
        vx = vpre[:, lanes]
        total = taps_applied(jnp.concatenate([vtail[:, lanes], vx], axis=0), vtaps[:, lanes])
        vtotal[:, lanes] = total
        vtail[:, lanes] = vx[CHUNK - 8 :]
        v = jax.nn.silu(total)
        weighted = v * by_pair(step, p)
        right = right_side(halves(weighted))
        parts = []
        for h in (2 * p, 2 * p + 1):
            decay = jnp.exp(jnp.minimum(cum[:, h : h + 1] - cum_t[h : h + 1, :], 0.0))
            parts.append(folded(mm(beside(halves(decay * scores)), right)))
        held = state[:, lanes]
        carried = by_pair(grown, p) * folded(mm(c_left, right_side(halves(held))))
        mixer[:, lanes] = jnp.where(left, parts[0], parts[1]) + carried + skip[:, lanes] * v
        entering_here = right_side(halves(weighted * by_pair(ending, p)))
        state[:, lanes] = held * by_pair(whole, p) + folded(mm(bt_left, entering_here))


def forward_scan(vpre, spre, step_pre, vtaps, staps, bias, log_decay, skip):
    tokens, width = vpre.shape
    chunks = tokens // CHUNK
    row = lambda n: pl.BlockSpec((CHUNK, n), lambda i: (i, 0))
    fixed = lambda x: pl.BlockSpec(x.shape, lambda i: (0, 0))
    return pl.pallas_call(
        forward_kernel,
        grid=(chunks,),
        in_specs=[row(width), row(2 * STATE), row(128)]
        + [fixed(x) for x in (vtaps, staps, bias, log_decay, skip)],
        out_specs=[
            row(width), pl.BlockSpec((1, STATE, width), lambda i: (i, 0, 0)), row(width), row(2 * STATE)
        ],
        out_shape=[
            jax.ShapeDtypeStruct((tokens, width), F32),
            jax.ShapeDtypeStruct((chunks, STATE, width), F32),
            jax.ShapeDtypeStruct((tokens, width), F32),
            jax.ShapeDtypeStruct((tokens, 2 * STATE), F32),
        ],
        scratch_shapes=[
            pltpu.VMEM((STATE, width), F32),
            pltpu.VMEM((8, width), F32),
            pltpu.VMEM((8, 2 * STATE), F32),
        ],
        compiler_params=pltpu.CompilerParams(vmem_limit_bytes=VMEM),
        cost_estimate=pl.CostEstimate(
            flops=tokens * width * 16 * 256,
            bytes_accessed=tokens * width * 20,
            transcendentals=tokens * width * 3,
        ),
        name="scan_forward",
    )(vpre, spre, step_pre, vtaps, staps, bias, log_decay, skip)


def taps_back(d_total, later, x, taps):
    extended = jnp.concatenate([d_total, later], axis=0)
    d_x, rows = 0.0, []
    for k in range(CONV):
        moved = extended[3 - k : 3 - k + CHUNK]
        d_x = d_x + moved * taps[k : k + 1, :]
        rows.append(jnp.sum(moved * x, axis=0, keepdims=True))
    return d_x, rows + [jnp.sum(d_total, axis=0, keepdims=True)]


def backward_kernel(
    vpre, vtotal, spre, stotal, spre_step, vtaps, staps, bias, log_decay, skip, chooser,
    mixer, d_mixer, starts,
    values_low, d_spre, step_low, value_sums, state_sums, step_sums,
    later_grad, later_state, vhead, shead,
):
    @pl.when(pl.program_id(0) == 0)
    def _():
        for ref in (later_grad, later_state, vhead, shead, value_sums, state_sums, step_sums):
            ref[...] = jnp.zeros_like(ref)

    stot = stotal[...]
    s_sigmoid = jax.nn.sigmoid(stot)
    states = stot * s_sigmoid
    b, c = states[:, :STATE], states[:, STATE:]
    shifted_pre, step, rates, cum = step_terms(spre_step, bias, log_decay)
    cum_t = cum.T
    final = cum[CHUNK - 1 :, :]
    grown, ending, whole = jnp.exp(cum), jnp.exp(final - cum), jnp.exp(final)
    b2, c2 = halves(b), halves(c)
    b_left, ct_left = beside(b2), beside(halves(c.T))
    causal = square(1) >= square(0)
    scores_t = jnp.where(causal, folded(mm_nt(b_left, right_side_nt(c2))), 0.0)
    left = lax.broadcasted_iota(jnp.int32, (1, 128), 1) < 64
    zero = jnp.zeros((CHUNK, 128), BF)
    d_scores_t = jnp.zeros((CHUNK, CHUNK), F32)
    d_b = jnp.zeros((CHUNK, STATE), F32)
    d_c = jnp.zeros((CHUNK, STATE), F32)
    reached = jnp.zeros((CHUNK, 128), F32)
    pulled = jnp.zeros((CHUNK, 128), F32)
    at_end = jnp.zeros((8, 128), F32)
    for p in range(vpre.shape[1] // 128):
        lanes = slice(128 * p, 128 * p + 128)
        pick = chooser[256 * p : 256 * p + 256, :]
        total, dy = vtotal[:, lanes], d_mixer[:, lanes]
        sigmoid = jax.nn.sigmoid(total)
        v = total * sigmoid
        steps = by_pair(step, p)
        weighted = v * steps
        w2, d2 = halves(weighted), halves(dy)
        d_right = right_side(d2)
        w_rest = pltpu.roll(weighted - w2[0].astype(F32), 64, 1).astype(BF)
        d_top = pltpu.roll(d2[0].astype(F32), 64, 1).astype(BF)
        parts = []
        for h, mine in ((2 * p, left), (2 * p + 1, ~left)):
            decay = jnp.exp(jnp.minimum(cum_t[h : h + 1, :] - cum[:, h : h + 1], 0.0))
            parts.append(folded(mm(beside(halves(decay * scores_t)), d_right)))
            one = beside((jnp.where(mine, w2[0], w_rest), jnp.where(mine, w2[0], zero)))
            other = beside((jnp.where(mine, d2[0], d_top), jnp.where(mine, d2[1], zero)))
            d_scores_t = d_scores_t + mm_nt(one, other) * decay
        held, after_here = starts[0, :, lanes], later_grad[:, lanes]
        after2 = halves(after_here)
        ends = by_pair(ending, p)
        d_weighted = jnp.where(left, parts[0], parts[1]) + ends * folded(
            mm(b_left, right_side(after2))
        )
        gain = skip[:, lanes]
        reached = reached + mm(beside(halves(dy * (mixer[:, lanes] - gain * v))), pick)
        pulled = pulled + mm(beside(halves(v * d_weighted)), pick)
        ended = jnp.sum(after_here * later_state[:, lanes], axis=0, keepdims=True)
        at_end = at_end + mm(beside(halves(jnp.broadcast_to(ended, (8, 128)))), pick)
        faded = halves(by_pair(grown, p) * dy)
        d_c = d_c + folded(mm_nt(beside(faded), right_side_nt(halves(held))))
        d_b = d_b + folded(mm_nt(beside(halves(weighted * ends)), right_side_nt(after2)))
        later_grad[:, lanes] = after_here * by_pair(whole, p) + folded(
            mm(ct_left, right_side(faded))
        )
        d_total = (steps * d_weighted + gain * dy) * (sigmoid * (1.0 + total * (1.0 - sigmoid)))
        d_x, rows = taps_back(d_total, vhead[:, lanes], vpre[:, lanes], vtaps[:, lanes])
        values_low[:, lanes] = d_x.astype(BF)
        rows += [jnp.sum(v * dy, axis=0, keepdims=True), jnp.zeros((2, 128), F32)]
        value_sums[:, lanes] += jnp.concatenate(rows, axis=0)
        vhead[:, lanes] = d_total[:8]
    later_state[...] = starts[0]
    d_scores_t = jnp.where(causal, d_scores_t, 0.0)
    d_b = d_b + folded(mm(beside(halves(d_scores_t)), right_side(c2)))
    d_c = d_c + folded(mm(beside(halves(d_scores_t.T)), right_side(b2)))
    last = lax.broadcasted_iota(jnp.int32, (CHUNK, 128), 0) == CHUNK - 1
    d_cum = reached - step * pulled + jnp.where(last, at_end[:1], 0.0)
    upper = jnp.where(causal, 1.0, 0.0).astype(F32)
    d_rate = jnp.dot(upper, d_cum, precision=HIGH, preferred_element_type=F32)
    d_shifted = (pulled - rates * d_rate) * jax.nn.sigmoid(shifted_pre)
    step_low[...] = d_shifted.astype(BF)
    step_sums[0:1, :] += jnp.sum(d_shifted, axis=0, keepdims=True)
    step_sums[1:2, :] -= jnp.sum(d_rate * step, axis=0, keepdims=True) * rates
    d_total = beside((d_b, d_c)) * (s_sigmoid * (1.0 + stot * (1.0 - s_sigmoid)))
    d_x, rows = taps_back(d_total, shead[...], spre[...], staps[...])
    d_spre[...] = d_x
    state_sums[...] += jnp.concatenate(rows + [jnp.zeros((3, 2 * STATE), F32)], axis=0)
    shead[...] = d_total[:8]


def backward_scan(
    vpre, vtotal, spre, stotal, step_pre, vtaps, staps, bias, log_decay, skip, mixer, d_mixer, starts
):
    tokens, width = vpre.shape
    chunks = tokens // CHUNK
    lane = jnp.arange(2 * width)
    heads = 2 * (lane // 256) + lane % 128 // 64
    chooser = (heads[:, None] == jnp.arange(128)[None, :]).astype(BF)
    row = lambda n: pl.BlockSpec((CHUNK, n), lambda i: (chunks - 1 - i, 0))
    fixed = lambda x: pl.BlockSpec(x.shape, lambda i: (0, 0))
    summed = lambda n: pl.BlockSpec((8, n), lambda i: (0, 0))
    return pl.pallas_call(
        backward_kernel,
        grid=(chunks,),
        in_specs=[row(width), row(width), row(2 * STATE), row(2 * STATE), row(128)]
        + [fixed(x) for x in (vtaps, staps, bias, log_decay, skip, chooser)]
        + [row(width), row(width), pl.BlockSpec((1, STATE, width), lambda i: (chunks - 1 - i, 0, 0))],
        out_specs=[
            row(width), row(2 * STATE), row(128), summed(width), summed(2 * STATE), summed(128),
        ],
        out_shape=[
            jax.ShapeDtypeStruct((tokens, width), BF),
            jax.ShapeDtypeStruct((tokens, 2 * STATE), F32),
            jax.ShapeDtypeStruct((tokens, 128), BF),
            jax.ShapeDtypeStruct((8, width), F32),
            jax.ShapeDtypeStruct((8, 2 * STATE), F32),
            jax.ShapeDtypeStruct((8, 128), F32),
        ],
        scratch_shapes=[
            pltpu.VMEM((STATE, width), F32),
            pltpu.VMEM((STATE, width), F32),
            pltpu.VMEM((8, width), F32),
            pltpu.VMEM((8, 2 * STATE), F32),
        ],
        compiler_params=pltpu.CompilerParams(vmem_limit_bytes=VMEM),
        cost_estimate=pl.CostEstimate(
            flops=tokens * width * 40 * 256,
            bytes_accessed=tokens * width * 24,
            transcendentals=tokens * width * 3,
        ),
        name="scan_backward",
    )(
        vpre, vtotal, spre, stotal, step_pre, vtaps, staps, bias, log_decay, skip, chooser,
        mixer, d_mixer, starts,
    )


def place(arrays, piece, targets, rows):
    count = sum(x.shape[0] // piece for x in arrays)
    assert count == len(targets)
    width, dtype = arrays[0].shape[1], arrays[0].dtype

    def kernel(at, *refs):
        sources, out, done = refs[: len(arrays)], refs[len(arrays)], refs[len(arrays) + 1]
        copies = []
        for source in sources:
            for j in range(source.shape[0] // piece):
                k = len(copies)
                start = pl.multiple_of(at[k], piece)
                copies.append(
                    pltpu.make_async_copy(
                        source.at[pl.ds(j * piece, piece)], out.at[pl.ds(start, piece)], done.at[k]
                    )
                )
        for copy in copies:
            copy.start()
        for copy in copies:
            copy.wait()

    return pl.pallas_call(
        kernel,
        grid_spec=pltpu.PrefetchScalarGridSpec(
            num_scalar_prefetch=1,
            grid=(1,),
            in_specs=[pl.BlockSpec(memory_space=pl.ANY)] * len(arrays),
            out_specs=pl.BlockSpec(memory_space=pltpu.VMEM),
            scratch_shapes=[pltpu.SemaphoreType.DMA((count,))],
        ),
        out_shape=jax.ShapeDtypeStruct((rows, width), dtype),
        compiler_params=pltpu.CompilerParams(vmem_limit_bytes=16 * 1024 * 1024),
        cost_estimate=pl.CostEstimate(
            flops=0, bytes_accessed=2 * rows * width * dtype.itemsize, transcendentals=0
        ),
        name="place",
    )(jnp.stack([jnp.asarray(t, jnp.int32) for t in targets]), *arrays)


def swap(x, axis, bit=1):
    return lax.ppermute(x, axis, [(i, i ^ bit) for i in range(lax.axis_size(axis))])


def turned(x, axis, distance):
    n = lax.axis_size(axis)
    return lax.ppermute(x, axis, [(i, (i + distance) % n) for i in range(n)])


def after(x, *earlier):
    return lax.optimization_barrier((x, *earlier))[0]


def at(x, index, axis):
    return lax.dynamic_index_in_dim(x, index, axis, keepdims=False)


def part(x, index, size, axis):
    return lax.dynamic_slice_in_dim(x, index * size, size, axis)


def ordered(flag, mine, other, axis):
    first = jnp.where(flag == 0, mine, other)
    second = jnp.where(flag == 0, other, mine)
    return jnp.concatenate([first, second], axis=axis)


def paired_kernel(count, core, *refs):
    lows, weights, outs = refs[:count], refs[count : 3 * count], refs[3 * count :]
    step, tiles = pl.program_id(0), pl.num_programs(0) // 2
    for j in range(2):

        @pl.when(step // tiles == j)
        def _(j=j):
            for out, which in zip(outs, (1 - core[0], core[0]), strict=True):
                total = 0.0
                for k, low in enumerate(lows):
                    block = low[:, which]
                    total = total + mm_nt(
                        block.reshape(-1, block.shape[-1]), weights[2 * k + j][...]
                    )
                out[...] = total


def paired_products(lows, weights, core, sub):
    tokens, n = lows[0].shape[0], weights[0][0].shape[0]
    groups = tokens // (4 * sub)
    split = [x.reshape(groups, 2, 2 * sub, x.shape[1]) for x in lows]
    tile = 256
    tiles = n // tile
    out = jax.ShapeDtypeStruct((tokens // 2, 2 * n), F32)
    first = lambda i, core: (jnp.minimum(i, tiles - 1), 0)
    second = lambda i, core: (jnp.maximum(i - tiles, 0), 0)
    return pl.pallas_call(
        functools.partial(paired_kernel, len(lows)),
        grid_spec=pltpu.PrefetchScalarGridSpec(
            num_scalar_prefetch=1,
            grid=(2 * tiles,),
            in_specs=[pl.BlockSpec(x.shape, lambda i, core: (0, 0, 0, 0)) for x in split]
            + [
                pl.BlockSpec((tile, w.shape[1]), where)
                for pair in weights
                for w, where in zip(pair, (first, second), strict=True)
            ],
            out_specs=[pl.BlockSpec((tokens // 2, tile), lambda i, core: (0, i))] * 2,
        ),
        out_shape=[out, out],
        compiler_params=pltpu.CompilerParams(vmem_limit_bytes=VMEM),
        cost_estimate=pl.CostEstimate(flops=1, bytes_accessed=1, transcendentals=0),
        name="paired_products",
    )(core[None], *split, *[w for pair in weights for w in pair])


def whole_sequences(
    block_input, output_grad, input_gain, gate_weight, value_weight, state_weight, step_weight,
    out_weight, value_taps, state_taps, step_bias, log_decay, skip_gain, mixer_gain,
):
    xi, ci, zi, yi = (lax.axis_index(n) for n in ("x", "core", "seq", "heads"))
    nz = lax.axis_size("seq")
    nx = lax.axis_size("x")
    d_model = block_input.shape[-1]
    half = d_model // 2
    group = block_input.shape[2]
    sub = group // 2
    tokens = group * nz
    own = sub * nz // 2
    rows = gate_weight.shape[0]
    cols = gate_weight.shape[1] // 2
    heads = step_weight.shape[1] // 2

    def turned_halves(x):
        return jnp.where(xi == 0, x, jnp.concatenate([x[:, half:], x[:, :half]], axis=1))

    def route(r):
        return [
            (c * nz + z, (z % 2) * nz + 2 * ((z // 2) ^ r) + c) for c in range(2) for z in range(nz)
        ]

    def tokens_in(x, *earlier):
        rounds = []
        for r in range(2):
            piece = lax.dynamic_slice(x, ((zi // 2) ^ r, 0, yi * sub, 0), (1, 1, sub, d_model))
            rounds.append(lax.ppermute(piece.reshape(sub, d_model), ("core", "seq"), route(r)))
        return ordered(zi // 2, after(rounds[0], *earlier), after(rounds[1], *earlier), 0)

    def tokens_back(x):
        pieces = [part(x, (zi // 2) ^ r, sub, 0) for r in range(2)]
        return [
            lax.ppermute(piece, ("core", "seq"), [(b, a) for a, b in route(r)])
            for r, piece in enumerate(pieces)
        ]

    def tokens_home(mine):
        targets = [(2 * ((zi // 2) ^ r) + y) * sub for y in (yi, 1 - yi) for r in range(2)]
        blocks = mine + [swap(x, "heads") for x in mine]
        return place(blocks, sub, targets, 2 * group).reshape(block_input.shape)

    def spread(x):
        by_y = swap(x, "heads")
        by_core = swap(x, "core")
        by_both = swap(by_y, "core")
        targets = [
            ((2 * k + c) * 2 + y) * sub
            for y, c in ((yi, ci), (1 - yi, ci), (yi, 1 - ci), (1 - yi, 1 - ci))
            for k in range(nz // 2)
        ]
        return place([x, by_y, by_core, by_both], sub, targets, tokens)

    def of_core(x, core):
        return at(x.reshape(nz // 2, 2, 2 * sub, -1), core, 1).reshape(tokens // 2, -1)

    def over_core(send, keep, link=BF):
        return core_sum(swap(send, "core"), keep, link)

    def core_sum(received, keep, link=BF):
        received = received.reshape(nz // 2, 2, sub, keep.shape[1])
        keep = keep.reshape(received.shape)
        goes = (at(keep, 1 - yi, 1) + at(received, 1 - yi, 1)).astype(link)
        return at(keep, yi, 1) + at(received, yi, 1), goes

    def over_y(stays, received):
        return (stays + received.astype(F32)).reshape(own, -1)

    def block_of(weight):
        width = weight.shape[1] // 2
        received = swap(part(weight, 1 - ci, width, 1), "core")
        return ordered(ci, part(weight, ci, width, 1), received, 0)

    def ring(block, *earlier):
        right = turned(block, "seq", 1)
        left = turned(block, "seq", -1)
        return [block, right, left, turned(after(right, left, *earlier), "seq", 1)]

    def stacked(blocks):
        targets = [
            (c * nz + z % nz) * rows for z in (zi, zi + nz - 1, zi + 1, zi + 2) for c in range(2)
        ]
        return place(blocks, rows, targets, half)

    def products(low, features):
        return transposed(features[:, half:], low).astype(BF), transposed(features[:, :half], low)

    def over_x(kept, received):
        return (kept + received.astype(F32)).reshape(2, nz, rows, -1)

    def far_pieces(summed):
        return part(summed, 1 - zi // 2, 2, summed.ndim - 3).astype(BF)

    def near_sum(summed, received):
        return part(summed, zi // 2, 2, summed.ndim - 3) + received.astype(F32)

    def near_pieces(summed):
        return at(summed, 1 - zi % 2, -3).astype(BF)

    def over_z(summed, received):
        return at(summed, zi % 2, -3) + received.astype(F32)

    def to_core(total):
        received = swap(at(total, 1 - ci, 0), "core")
        return at(total, ci, 0), received

    project = lambda a, b: jnp.dot(a, b, preferred_element_type=F32)
    transposed = lambda a, b: lax.dot_general(
        a, b, (((0,), (0,)), ((), ())), preferred_element_type=F32
    )
    back = lambda a, b: lax.dot_general(a, b, (((1,), (1,)), ((), ())), preferred_element_type=F32)

    pad = 128 - heads
    first = jnp.concatenate(
        [
            jnp.concatenate(
                [
                    value_weight[:, cols * k : cols * k + cols],
                    state_weight[:, STATE * k : STATE * k + STATE],
                    step_weight[:, heads * k : heads * k + heads],
                    jnp.broadcast_to(input_gain[:, None], (rows, pad)),
                ],
                axis=1,
            )
            for k in range(2)
        ],
        axis=1,
    )
    first_block = block_of(first)
    first_across = [swap(first_block, "x")]
    first_ring = ring(first_block, *first_across)
    first_across += [swap(x, "x") for x in first_ring[1:]]

    x_own = turned_halves(tokens_in(after(block_input, first_block)))

    pair_weight = after(
        jnp.concatenate(
            [gate_weight[:, :cols], out_weight[:cols].T, gate_weight[:, cols:], out_weight[cols:].T],
            axis=1,
        ),
        first_block,
    )
    pair_block = block_of(pair_weight)
    pair_across = [swap(after(pair_block, first_across[0]), "x")]
    x_all = spread(after(x_own, *pair_across))
    pair_ring = ring(after(pair_block, first_ring[3], first_across[1], first_across[2]))
    pair_across += [swap(after(x, first_across[3]), "x") for x in pair_ring[1:]]

    first_own = stacked(first_ring)
    first_other = stacked(first_across)
    def both_halves(a, w_own, w_other):
        return project(a[:, :half], w_own) + project(a[:, half:], w_other)

    split = lambda w: (w[:, :cols], w[:, cols : cols + STATE], w[:, cols + STATE :])
    value_own, state_own, step_own = split(first_own)
    value_other, state_other, step_other = split(first_other)
    gain = jnp.concatenate([step_own[:, -1], step_other[:, -1]])[None].astype(F32)
    blank = jnp.arange(128)[None, :] < heads
    step_own, step_other = jnp.where(blank, step_own, 0), jnp.where(blank, step_other, 0)

    x_wide = x_all.astype(F32)
    normed = (
        x_wide * lax.rsqrt(jnp.mean(x_wide * x_wide, axis=-1, keepdims=True) + EPS) * gain
    ).astype(BF)
    x_own = x_own.astype(F32)
    scaling = lax.rsqrt(jnp.mean(x_own * x_own, axis=-1, keepdims=True) + EPS)

    states_weights = jnp.concatenate([state_own, state_other], axis=0)
    states_received = swap(states_weights, "core")
    states_half = both_halves(normed, state_own, state_other)
    states_pre = ordered(ci, states_half, swap(states_half, "core"), 1)
    values_pre = both_halves(normed, value_own, value_other)
    step_pre = both_halves(normed, step_own, step_other)

    vtaps = part(value_taps, ci, cols, 1)
    lanes = lambda v: jnp.pad(part(v, ci, heads, 0), (0, pad))[None]
    bias, decays = lanes(step_bias), lanes(log_decay)
    skip = jnp.repeat(part(skip_gain, ci, heads, 0), cols // heads)[None]
    gain_mixer = part(mixer_gain, ci, cols, 0)[None]
    values_pre, states_received, *pair_across[1:3], pair_ring[3] = lax.optimization_barrier(
        (values_pre, states_received, *pair_across[1:3], pair_ring[3])
    )
    mixer, starts, values_total, states_total = forward_scan(
        values_pre, states_pre, step_pre, vtaps, state_taps, bias, decays, skip
    )
    og_own = turned_halves(tokens_in(after(output_grad, pair_ring[1], pair_ring[2]), mixer))
    og = spread(og_own)
    pair_own = stacked(pair_ring)
    pair_other = stacked(pair_across)
    gate_own, out_own = pair_own[:, :cols], pair_own[:, cols:]
    gate_other, out_other = pair_other[:, :cols], pair_other[:, cols:]
    gate_lin = both_halves(normed, gate_own, gate_other)
    d_out = both_halves(og, out_own, out_other)
    sigmoid_gate = jax.nn.sigmoid(gate_lin)
    silu_gate = gate_lin * sigmoid_gate
    gated = mixer * silu_gate
    weighted = d_out * gain_mixer
    sums = jnp.stack([jnp.sum(gated * gated, axis=1), jnp.sum(weighted * gated, axis=1)])
    sums = sums + swap(sums, "core")
    sums = sums + swap(sums, "heads")
    inverse = lax.rsqrt(sums[0] / INNER + EPS)[:, None]
    out_normed = (gated * inverse * gain_mixer).astype(BF)
    d_gated = inverse * weighted - gated * (inverse * inverse * inverse) * (sums[1][:, None] / INNER)
    d_mixer = d_gated * silu_gate
    gate_low = (d_gated * mixer * sigmoid_gate * (1.0 + gate_lin * (1.0 - sigmoid_gate))).astype(BF)
    g_mixer_gain = jnp.sum(d_out * gated * inverse, axis=0)

    branch_sends, branch_keeps = paired_products([out_normed], [(out_own, out_other)], ci, sub)
    then = after(out_normed, branch_sends)
    out_sum = jnp.stack([transposed(og[:, :half], then), transposed(og[:, half:], then)])
    out_sum = out_sum.reshape(2, 2, nz, rows, cols)
    out_pieces = far_pieces(out_sum)
    gate_sends, gate_keeps = products(after(gate_low, out_pieces), normed)
    branch_stays, branch_goes = over_core(branch_sends, branch_keeps)
    d_mixer = after(d_mixer, out_pieces, gate_sends, branch_goes)
    scanned = backward_scan(
        values_pre, values_total, states_pre, states_total, step_pre, vtaps, state_taps, bias, decays, skip,
        mixer, d_mixer, starts,
    )
    sent = (swap(out_pieces, "seq", 2), swap(gate_sends, "x"), swap(branch_goes, "heads"))
    sent, scanned = lax.optimization_barrier((sent, scanned))
    out_received, gate_received, branch_received = sent
    values_low, d_states, step_low, value_sums, state_sums, step_sums = scanned

    value_sends, value_keeps = products(values_low, normed)
    gate_sum = over_x(after(gate_keeps, value_sends), gate_received)
    gate_pieces = far_pieces(gate_sum)
    d_states = after(d_states, gate_pieces)
    states_stay, states_go = over_core(of_core(d_states, 1 - ci), of_core(d_states, ci), F32)
    dn_sends, dn_keeps = paired_products(
        [after(gate_low, value_sends, states_go), values_low, step_low],
        [(gate_own, gate_other), (value_own, value_other), (step_own, step_other)],
        ci,
        sub,
    )
    out_sum = near_sum(out_sum, after(out_received, dn_sends))
    out_pieces = near_pieces(out_sum)
    branch = over_y(branch_stays, after(branch_received, dn_sends))
    output_rows = turned_halves((x_own + branch).astype(BF))
    (
        value_received, gate_received, states_received_y, dn_received, dn_keeps, out_pieces, output_rows
    ) = lax.optimization_barrier(
        (
            swap(value_sends, "x"), swap(gate_pieces, "seq", 2), swap(states_go, "heads"),
            swap(dn_sends, "core"), dn_keeps, out_pieces, output_rows,
        )
    )

    dn_stays, dn_goes = core_sum(dn_received, dn_keeps)
    output_sent = tokens_back(output_rows)
    gate_sum = near_sum(gate_sum, gate_received)
    gate_pieces = near_pieces(gate_sum)
    states_low = over_y(states_stay, states_received_y).astype(BF)
    states_weights = ordered(ci, states_weights, states_received, 1)
    states_both = swap(states_low, "core").reshape(nz // 2, sub, -1), states_low.reshape(nz // 2, sub, -1)
    states_both = [part(x, ci, STATE, 2) for x in states_both]
    of_y = at(after(normed, dn_goes).reshape(nz // 2, 2, 2, sub, d_model), yi, 2)
    states_both = jnp.stack(
        [jnp.where(ci == k, states_both[1], states_both[0]) for k in range(2)], axis=1
    ).reshape(tokens // 2, STATE)
    parts = [
        products(states_both, of_y.reshape(tokens // 2, d_model)),
        products(after(step_low, dn_goes), normed),
    ]
    small_sends, small_keeps = (jnp.concatenate(p, axis=1) for p in zip(*parts, strict=True))
    value_sum = over_x(value_keeps, value_received)
    (
        dn_received, output_sent, gate_received, small_received, out_pieces, value_sum
    ) = lax.optimization_barrier(
        (
            swap(dn_goes, "heads"), output_sent, swap(gate_pieces, "seq", 1), swap(small_sends, "x"),
            out_pieces, value_sum,
        )
    )

    value_sum = jnp.concatenate([value_sum, over_x(small_keeps, small_received)], axis=-1)
    value_pieces = far_pieces(value_sum)
    d_normed = over_y(dn_stays, after(dn_received, value_pieces)) + back(states_low, states_weights)
    pushed = d_normed * gain
    d_tokens = scaling * pushed - x_own * (scaling * scaling * scaling) * jnp.mean(
        pushed * x_own, axis=-1, keepdims=True
    )
    input_rows = turned_halves((og_own.astype(F32) + d_tokens).astype(BF))
    block_output = tokens_home(output_sent)
    g_gate = over_z(gate_sum, gate_received)
    out_sum = over_z(out_sum, swap(out_pieces, "seq", 1))
    out_sum, input_sent = lax.optimization_barrier((out_sum, tokens_back(input_rows)))

    grad_input = tokens_home(input_sent)
    g_out = out_sum[0] + swap(out_sum[1].astype(BF), "x").astype(F32)
    value_sum = near_sum(value_sum, after(swap(value_pieces, "seq", 2), *input_sent))
    g_value = over_z(value_sum, swap(near_pieces(value_sum), "seq", 1))
    g_input_gain = turned_halves(jnp.sum(d_normed * x_own * scaling, axis=0)[None])

    per_core = jnp.concatenate(
        [value_sums[:6], g_mixer_gain[None], jnp.pad(step_sums[:2].reshape(1, -1), ((0, 0), (0, cols - 256)))],
        axis=0,
    ).reshape(-1, 256)
    shared = jnp.concatenate([state_sums, g_input_gain.reshape(-1, 256)], axis=0)
    shared = after(shared, *input_sent)
    shared = shared + swap(shared, "heads")
    received = swap(jnp.concatenate([per_core, shared], axis=0), "core")
    n_core = per_core.shape[0]
    pack = jnp.concatenate(
        [ordered(ci, per_core, received[:n_core], 0), shared + received[n_core:]], axis=0
    )
    pack = pack + swap(pack, "x")
    pack = pack + swap(pack, "seq", 1)
    pack = pack + swap(pack, "seq", 2)
    both, shared = pack[: 2 * n_core].reshape(2, 8, cols), pack[2 * n_core :]
    by_channel = jnp.transpose(both, (1, 0, 2)).reshape(8, 2 * cols)
    per_head = both[:, 7, :256].reshape(2, 2, 128)[:, :, :heads]
    input_gain_all = shared[8:].reshape(nx, 2, nz, rows)
    my_gain = at(at(at(input_gain_all, xi, 0), ci, 0), zi, 0)

    def widths(mine, received):
        return ordered(ci, mine, received, 1)

    value_mine, value_received = to_core(g_value)
    states_at, steps_at = slice(cols, cols + STATE), slice(cols + STATE, cols + STATE + heads)
    g_state = widths(value_mine[:, states_at], value_received[:, states_at])
    g_state = g_state + swap(g_state, "heads")
    return (
        block_output,
        grad_input,
        my_gain,
        widths(*to_core(g_gate)),
        widths(value_mine[:, :cols], value_received[:, :cols]),
        g_state,
        widths(value_mine[:, steps_at], value_received[:, steps_at]),
        widths(*to_core(g_out)).T,
        by_channel[:5],
        shared[:5],
        per_head[:, 0].reshape(-1),
        per_head[:, 1].reshape(-1),
        jnp.sum(by_channel[5].reshape(2 * heads, -1), axis=1),
        by_channel[6],
    )


def solution(mesh):
    sizes = dict(mesh.shape)
    if sizes["seq"] == 2 * MB and sizes["dp"] == 4 and sizes["heads"] == 2:
        devices = mesh.devices.reshape(sizes["dp"] // 2, 2, sizes["seq"], sizes["heads"])
        mesh = jax.sharding.Mesh(devices, ("x", "core", "seq", "heads"))
        body, dp = whole_sequences, ("x", "core")
    else:
        body, dp = shards, ("dp",)
    tokens = P(None, dp, "seq", None)
    both = (*dp, "seq")
    return jax.shard_map(
        body,
        mesh=mesh,
        in_specs=(
            tokens,
            tokens,
            P(both),
            P(both, "heads"),
            P(both, "heads"),
            P(both, None),
            P(both, "heads"),
            P("heads", both),
            P(None, "heads"),
            P(),
            P("heads"),
            P("heads"),
            P("heads"),
            P("heads"),
        ),
        out_specs=(
            tokens,
            tokens,
            P(both),
            P(both, "heads"),
            P(both, "heads"),
            P(both, None),
            P(both, "heads"),
            P("heads", both),
            P(None, "heads"),
            P(),
            P("heads"),
            P("heads"),
            P("heads"),
            P("heads"),
        ),
        check_vma=False,
    )
```

```python
import functools

import jax
import jax.numpy as jnp
from jax import lax
from jax.experimental import pallas as pl
from jax.experimental.pallas import tpu as pltpu
from jax.sharding import PartitionSpec as P

STATE = 128
CONV = 4
MB = 2
INNER = 3072


EPS = 1e-05
HIGH = lax.Precision.HIGHEST


def shifted(block, axis, distance):
    devices = range(lax.axis_size(axis))
    route = [(i - distance, i) for i in devices if i - distance in devices]
    return lax.ppermute(block, axis, route)


def entering(x, axis, combine, identity, reverse):
    peers, index = (lax.axis_size(axis), lax.axis_index(axis))
    everything = jax.tree.map(lambda part: lax.all_gather(part, axis), x)
    start = jax.tree.map(
        lambda part, zero: jnp.broadcast_to(jnp.asarray(zero, part.dtype), part.shape), x, identity
    )

    def step(k, before):
        at = peers - 1 - k if reverse else k
        reached = at > index if reverse else at < index
        new = combine(before, jax.tree.map(lambda part: part[at], everything))
        return jax.tree.map(lambda a, b: jnp.where(reached, a, b), new, before)

    return lax.fori_loop(0, peers, step, start)


def norm_rows(values, gain):
    return values * lax.rsqrt(jnp.mean(values * values, axis=-1, keepdims=True) + EPS) * gain


def conv_silu(extended, taps):
    length = extended.shape[1] - (CONV - 1)
    total = jnp.zeros((extended.shape[0], length, extended.shape[2]), jnp.float32) + taps[CONV]
    for offset in range(CONV):
        total = total + extended[:, offset : offset + length] * taps[offset]
    return jax.nn.silu(total)


def local_parts(
    values_ext, states_ext, step_pre, value_taps, state_taps, step_bias, log_decay, skip_gain
):
    values_conv = conv_silu(values_ext, value_taps)
    states_conv = conv_silu(states_ext, state_taps)
    batch, length, channels = values_conv.shape
    heads_here = step_pre.shape[-1]
    values = values_conv.reshape(batch, length, heads_here, channels // heads_here)
    input_mat = states_conv[..., :STATE]
    output_mat = states_conv[..., STATE:]
    stepsize = jax.nn.softplus(step_pre + step_bias)
    cumulative = jnp.cumsum(-stepsize * jnp.exp(log_decay), axis=1)
    gaps = cumulative[:, :, None, :] - cumulative[:, None, :, :]
    causal = (jnp.arange(length)[:, None] >= jnp.arange(length)[None, :])[None, :, :, None]
    decays = jnp.where(causal, jnp.exp(jnp.where(causal, gaps, 0.0)), 0.0)
    scores = jnp.einsum("btn,bsn->bts", output_mat, input_mat, precision=HIGH)
    weights = decays * scores[..., None] * stepsize[:, None, :, :]
    within = (
        jnp.einsum("btsh,bshp->bthp", weights, values, precision=HIGH) + skip_gain[:, None] * values
    )
    final = cumulative[:, -1]
    ending = jnp.exp(final[:, None, :] - cumulative) * stepsize
    local_state = jnp.einsum("bth,btn,bthp->bhnp", ending, input_mat, values, precision=HIGH)
    return (within, local_state, jnp.exp(final), cumulative, output_mat)


def carried_part(cumulative, output_mat, state_in):
    return jnp.exp(cumulative)[..., None] * jnp.einsum(
        "btn,bhnp->bthp", output_mat, state_in, precision=HIGH
    )


def whole_block(
    values_ext,
    states_ext,
    step_pre,
    value_taps,
    state_taps,
    step_bias,
    log_decay,
    skip_gain,
    state_in,
):
    within, local_state, span_decay, cumulative, output_mat = local_parts(
        values_ext, states_ext, step_pre, value_taps, state_taps, step_bias, log_decay, skip_gain
    )
    result = within + carried_part(cumulative, output_mat, state_in)
    return (result.reshape(result.shape[0], result.shape[1], -1), local_state, span_decay)


def compose(earlier, later):
    return (earlier[0] * later[0], later[0][..., None, None] * earlier[1] + later[1])


def shards(
    block_input,
    output_grad,
    input_gain,
    gate_weight,
    value_weight,
    state_weight,
    step_weight,
    out_weight,
    value_taps,
    state_taps,
    step_bias,
    log_decay,
    skip_gain,
    mixer_gain,
):
    margin = CONV - 1
    width = block_input.shape[-1]
    inner_here = gate_weight.shape[1]
    state_cols = state_weight.shape[1]
    heads_here = step_weight.shape[1]
    acc_gain = jnp.zeros((width,), jnp.float32)
    acc_gate = jnp.zeros((width, inner_here), jnp.float32)
    acc_value = jnp.zeros((width, inner_here), jnp.float32)
    acc_state = jnp.zeros((width, state_cols), jnp.float32)
    acc_step = jnp.zeros((width, heads_here), jnp.float32)
    acc_out = jnp.zeros((inner_here, width), jnp.float32)
    acc_value_taps = jnp.zeros_like(value_taps)
    acc_state_taps = jnp.zeros_like(state_taps)
    acc_step_bias = jnp.zeros_like(step_bias)
    acc_log_decay = jnp.zeros_like(log_decay)
    acc_skip = jnp.zeros_like(skip_gain)
    acc_mixer_gain = jnp.zeros_like(mixer_gain)
    outputs = []
    input_grads = []
    for micro_batch in range(MB):
        weights_now = (
            lax.all_gather(input_gain, ("dp", "seq"), axis=0, tiled=True),
            lax.all_gather(gate_weight, ("dp", "seq"), axis=0, tiled=True),
            lax.all_gather(value_weight, ("dp", "seq"), axis=0, tiled=True),
            lax.all_gather(state_weight, ("dp", "seq"), axis=0, tiled=True),
            lax.all_gather(step_weight, ("dp", "seq"), axis=0, tiled=True),
            lax.all_gather(out_weight, ("dp", "seq"), axis=1, tiled=True),
        )
        gain_full, gate_full, value_full, state_full, step_full, out_full = weights_now
        tokens = block_input[micro_batch].astype(jnp.float32)
        normed = norm_rows(tokens, gain_full.astype(jnp.float32)).astype(jnp.bfloat16)
        gate_lin = jnp.einsum("btd,di->bti", normed, gate_full, preferred_element_type=jnp.float32)
        values_pre = jnp.einsum(
            "btd,di->bti", normed, value_full, preferred_element_type=jnp.float32
        )
        states_pre = jnp.einsum(
            "btd,di->bti", normed, state_full, preferred_element_type=jnp.float32
        )
        step_pre = jnp.einsum("btd,di->bti", normed, step_full, preferred_element_type=jnp.float32)
        outgoing = jnp.concatenate([values_pre[:, -margin:], states_pre[:, -margin:]], axis=2)
        incoming = shifted(outgoing, "seq", 1)
        values_ext = jnp.concatenate([incoming[..., :inner_here], values_pre], axis=1)
        states_ext = jnp.concatenate([incoming[..., inner_here:], states_pre], axis=1)
        within, local_state, span_decay, cumulative, output_mat = local_parts(
            values_ext,
            states_ext,
            step_pre,
            value_taps,
            state_taps,
            step_bias,
            log_decay,
            skip_gain,
        )
        prefix = entering(
            (span_decay, local_state),
            "seq",
            compose,
            (jnp.ones_like(span_decay), jnp.zeros_like(local_state)),
            False,
        )
        state_in = prefix[1]
        mixer = (within + carried_part(cumulative, output_mat, state_in)).reshape(gate_lin.shape)
        silu_gate = jax.nn.silu(gate_lin)
        gated = mixer * silu_gate
        total_sq = lax.psum(jnp.sum(gated * gated, axis=-1), "heads")
        inverse = lax.rsqrt(total_sq / INNER + EPS)[..., None]
        out_normed = (gated * inverse * mixer_gain).astype(jnp.bfloat16)
        partial_out = jnp.einsum(
            "bti,id->btd", out_normed, out_full, preferred_element_type=jnp.float32
        )
        branch = lax.psum(partial_out, "heads")
        outputs.append((tokens + branch).astype(jnp.bfloat16))
        weights_back = (
            lax.all_gather(input_gain, ("dp", "seq"), axis=0, tiled=True),
            lax.all_gather(gate_weight, ("dp", "seq"), axis=0, tiled=True),
            lax.all_gather(value_weight, ("dp", "seq"), axis=0, tiled=True),
            lax.all_gather(state_weight, ("dp", "seq"), axis=0, tiled=True),
            lax.all_gather(step_weight, ("dp", "seq"), axis=0, tiled=True),
            lax.all_gather(out_weight, ("dp", "seq"), axis=1, tiled=True),
        )
        gain_full, gate_full, value_full, state_full, step_full, out_full = weights_back
        grad_out = output_grad[micro_batch]
        d_out_normed = jnp.einsum(
            "btd,id->bti", grad_out, out_full, preferred_element_type=jnp.float32
        )
        acc_out = acc_out + jnp.einsum(
            "bti,btd->id", out_normed, grad_out, preferred_element_type=jnp.float32
        )
        acc_mixer_gain = acc_mixer_gain + jnp.sum(d_out_normed * gated * inverse, axis=(0, 1))
        weighted = d_out_normed * mixer_gain
        dot_total = lax.psum(jnp.sum(weighted * gated, axis=-1), "heads")
        d_gated = inverse * weighted - gated * (inverse * inverse * inverse) * (
            dot_total[..., None] / INNER
        )
        d_mixer = d_gated * silu_gate
        sigmoid_gate = jax.nn.sigmoid(gate_lin)
        d_gate_lin = d_gated * mixer * sigmoid_gate * (1.0 + gate_lin * (1.0 - sigmoid_gate))
        carry_grad = jnp.einsum(
            "bth,btn,bthp->bhnp",
            jnp.exp(cumulative),
            output_mat,
            d_mixer.reshape(within.shape),
            precision=HIGH,
        )
        suffix = entering(
            (span_decay, carry_grad),
            "seq",
            compose,
            (jnp.ones_like(span_decay), jnp.zeros_like(carry_grad)),
            True,
        )
        later_grad = suffix[1]
        d_decay = jnp.sum(later_grad * state_in, axis=(2, 3))
        ignored, pullback = jax.vjp(
            whole_block,
            values_ext,
            states_ext,
            step_pre,
            value_taps,
            state_taps,
            step_bias,
            log_decay,
            skip_gain,
            state_in,
        )
        (
            d_values_ext,
            d_states_ext,
            d_step_pre,
            g_value_taps,
            g_state_taps,
            g_step_bias,
            g_log_decay,
            g_skip,
            unused_state,
        ) = pullback((d_mixer, later_grad, d_decay))
        rim_grads = jnp.concatenate([d_values_ext[:, :margin], d_states_ext[:, :margin]], axis=2)
        returned = shifted(rim_grads, "seq", -1)
        d_values_pre = d_values_ext[:, margin:].at[:, -margin:].add(returned[..., :inner_here])
        d_states_pre = d_states_ext[:, margin:].at[:, -margin:].add(returned[..., inner_here:])
        gate_low = d_gate_lin.astype(jnp.bfloat16)
        values_low = d_values_pre.astype(jnp.bfloat16)
        step_low = d_step_pre.astype(jnp.bfloat16)
        d_normed_part = (
            jnp.einsum("bti,di->btd", gate_low, gate_full, preferred_element_type=jnp.float32)
            + jnp.einsum("bti,di->btd", values_low, value_full, preferred_element_type=jnp.float32)
            + jnp.einsum("bti,di->btd", step_low, step_full, preferred_element_type=jnp.float32)
        )
        d_normed_sum, d_states_total, state_taps_total = lax.psum(
            (d_normed_part, d_states_pre, g_state_taps), "heads"
        )
        states_low = d_states_total.astype(jnp.bfloat16)
        d_normed = d_normed_sum + jnp.einsum(
            "bti,di->btd", states_low, state_full, preferred_element_type=jnp.float32
        )
        acc_gate = acc_gate + jnp.einsum(
            "btd,bti->di", normed, gate_low, preferred_element_type=jnp.float32
        )
        acc_value = acc_value + jnp.einsum(
            "btd,bti->di", normed, values_low, preferred_element_type=jnp.float32
        )
        acc_state = acc_state + jnp.einsum(
            "btd,bti->di", normed, states_low, preferred_element_type=jnp.float32
        )
        acc_step = acc_step + jnp.einsum(
            "btd,bti->di", normed, step_low, preferred_element_type=jnp.float32
        )
        scaling = lax.rsqrt(jnp.mean(tokens * tokens, axis=-1, keepdims=True) + EPS)
        acc_gain = acc_gain + jnp.sum(d_normed * tokens * scaling, axis=(0, 1))
        pushed = d_normed * gain_full.astype(jnp.float32)
        d_tokens = scaling * pushed - tokens * (scaling * scaling * scaling) * jnp.mean(
            pushed * tokens, axis=-1, keepdims=True
        )
        input_grads.append((grad_out.astype(jnp.float32) + d_tokens).astype(jnp.bfloat16))
        acc_value_taps = acc_value_taps + g_value_taps
        acc_state_taps = acc_state_taps + state_taps_total
        acc_step_bias = acc_step_bias + g_step_bias
        acc_log_decay = acc_log_decay + g_log_decay
        acc_skip = acc_skip + g_skip
    summed = (
        lax.psum_scatter(acc_gain, ("dp", "seq"), scatter_dimension=0, tiled=True),
        lax.psum_scatter(acc_gate, ("dp", "seq"), scatter_dimension=0, tiled=True),
        lax.psum_scatter(acc_value, ("dp", "seq"), scatter_dimension=0, tiled=True),
        lax.psum_scatter(acc_state, ("dp", "seq"), scatter_dimension=0, tiled=True),
        lax.psum_scatter(acc_step, ("dp", "seq"), scatter_dimension=0, tiled=True),
        lax.psum_scatter(acc_out, ("dp", "seq"), scatter_dimension=1, tiled=True),
    )
    smalls = lax.psum(
        (acc_value_taps, acc_state_taps, acc_step_bias, acc_log_decay, acc_skip, acc_mixer_gain),
        ("dp", "seq"),
    )
    return (
        jnp.stack(outputs),
        jnp.stack(input_grads),
        summed[0],
        summed[1],
        summed[2],
        summed[3],
        summed[4],
        summed[5],
        smalls[0],
        smalls[1],
        smalls[2],
        smalls[3],
        smalls[4],
        smalls[5],
    )


BF = jnp.bfloat16
F32 = jnp.float32
CHUNK = 256
HALF = 128
VMEM = 40 * 1024 * 1024


def halves(x):
    top = x.astype(BF)
    return top, (x - top.astype(F32)).astype(BF)


def mm(a, b):
    return lax.dot_general(a, b, (((1,), (0,)), ((), ())), preferred_element_type=F32)


def mm_nt(a, b):
    return lax.dot_general(a, b, (((1,), (1,)), ((), ())), preferred_element_type=F32)


def beside(pair):
    return jnp.concatenate(pair, axis=1)


def right_side(b):
    top, rest = b
    return jnp.concatenate([beside((top, rest)), beside((top, jnp.zeros_like(top)))], axis=0)


def right_side_nt(b):
    top, rest = b
    return jnp.concatenate([beside((top, top)), beside((rest, jnp.zeros_like(top)))], axis=0)


def folded(wide):
    n = wide.shape[1] // 2
    return wide[:, :n] + wide[:, n:]


def softplus(x):
    return jnp.maximum(x, 0.0) + jnp.log1p(jnp.exp(-jnp.abs(x)))


def taps_applied(x, before, taps, moved):
    moved[:8, :] = before
    moved[8:, :] = x
    total = taps[CONV : CONV + 1, :]
    for k in range(CONV - 1):
        total = total + moved[5 + k : 5 + k + CHUNK, :] * taps[k : k + 1, :]
    return total + x * taps[CONV - 1 : CONV, :]


def summed_by(ones, x):
    top, rest = halves(x)
    low = x - top.astype(F32) - rest.astype(F32)
    return folded(mm(ones, beside((top, rest)))) + mm(ones, low.astype(BF))


def square(which):
    return lax.broadcasted_iota(jnp.int32, (CHUNK, CHUNK), which)


def step_terms(step_ref, bias_ref, log_decay_ref):
    shifted_pre = step_ref[...] + bias_ref[...]
    step = softplus(shifted_pre)
    rates = jnp.exp(log_decay_ref[...])
    cum = summed_by(jnp.where(square(0) >= square(1), 1.0, 0.0).astype(BF), -step * rates)
    return shifted_pre, step, rates, cum


def by_pair(q, p):
    left = lax.broadcasted_iota(jnp.int32, (1, 128), 1) < 64
    return jnp.where(left, q[:, 2 * p : 2 * p + 1], q[:, 2 * p + 1 : 2 * p + 2])


def forward_kernel(
    vpre, spre, spre_step, vtaps, staps, bias, log_decay, skip,
    mixer, starts, values, vslope, states_ref, sslope, state, vtail, stail, vmoved, smoved,
):
    @pl.when(pl.program_id(0) == 0)
    def _():
        state[...] = jnp.zeros_like(state)
        vtail[...] = jnp.zeros_like(vtail)
        stail[...] = jnp.zeros_like(stail)

    sx = spre[...]
    total = taps_applied(sx, stail[...], staps[...], smoved)
    sigmoid = jax.nn.sigmoid(total)
    states = total * sigmoid
    states_ref[...] = states
    sslope[...] = sigmoid * (1.0 + total * (1.0 - sigmoid))
    stail[...] = sx[CHUNK - 8 :]
    b, c = states[:, :STATE], states[:, STATE:]
    shifted_pre, step, rates, cum = step_terms(spre_step, bias, log_decay)
    cum_t = cum.T
    final = cum[CHUNK - 1 :, :]
    grown, ending, whole = jnp.exp(cum), jnp.exp(final - cum), jnp.exp(final)
    c_left, bt2 = beside(halves(c)), halves(b.T)
    scores = folded(mm_nt(c_left, right_side_nt(halves(b))))
    scores = jnp.where(square(0) >= square(1), scores, 0.0)
    left = lax.broadcasted_iota(jnp.int32, (1, 128), 1) < 64
    starts[0] = state[...]
    for p in range(vpre.shape[1] // 128):
        lanes = slice(128 * p, 128 * p + 128)
        vx = vpre[:, lanes]
        total = taps_applied(vx, vtail[:, lanes], vtaps[:, lanes], vmoved.at[p])
        vtail[:, lanes] = vx[CHUNK - 8 :]
        sigmoid = jax.nn.sigmoid(total)
        v = total * sigmoid
        values[:, lanes] = v
        vslope[:, lanes] = sigmoid * (1.0 + total * (1.0 - sigmoid))
        weighted = v * by_pair(step, p)
        w2 = halves(weighted)
        early, late = [], []
        for h in (2 * p, 2 * p + 1):
            gap = cum[:HALF, h : h + 1] - cum_t[h : h + 1, :HALF]
            early.append(jnp.exp(jnp.minimum(gap, 0.0)) * scores[:HALF, :HALF])
            gap = cum[HALF:, h : h + 1] - cum_t[h : h + 1, :]
            late.append(jnp.exp(jnp.minimum(gap, 0.0)) * scores[HALF:, :])
        early = beside(halves(jnp.concatenate(early, axis=0)))
        early = folded(mm(early, right_side((w2[0][:HALF], w2[1][:HALF]))))
        late = halves(jnp.concatenate(late, axis=0))
        late = folded(mm(late[0], beside(w2))) + mm(late[1], w2[0])
        within = jnp.concatenate(
            [
                jnp.where(left, early[:HALF], early[HALF:]),
                jnp.where(left, late[:HALF], late[HALF:]),
            ],
            axis=0,
        )
        held = state[:, lanes]
        carried = by_pair(grown, p) * folded(mm(c_left, right_side(halves(held))))
        mixer[:, lanes] = within + carried + skip[:, lanes] * v
        ends = halves(weighted * by_pair(ending, p))
        added = folded(mm(bt2[0], beside(ends))) + mm(bt2[1], ends[0])
        state[:, lanes] = held * by_pair(whole, p) + added


def forward_scan(vpre, spre, step_pre, vtaps, staps, bias, log_decay, skip):
    tokens, width = vpre.shape
    chunks = tokens // CHUNK
    row = lambda n: pl.BlockSpec((CHUNK, n), lambda i: (i, 0))
    fixed = lambda x: pl.BlockSpec(x.shape, lambda i: (0, 0))
    return pl.pallas_call(
        forward_kernel,
        grid=(chunks,),
        in_specs=[row(width), row(2 * STATE), row(128)]
        + [fixed(x) for x in (vtaps, staps, bias, log_decay, skip)],
        out_specs=[
            row(width), pl.BlockSpec((1, STATE, width), lambda i: (i, 0, 0)),
            row(width), row(width), row(2 * STATE), row(2 * STATE),
        ],
        out_shape=[
            jax.ShapeDtypeStruct((tokens, width), F32),
            jax.ShapeDtypeStruct((chunks, STATE, width), F32),
            jax.ShapeDtypeStruct((tokens, width), F32),
            jax.ShapeDtypeStruct((tokens, width), F32),
            jax.ShapeDtypeStruct((tokens, 2 * STATE), F32),
            jax.ShapeDtypeStruct((tokens, 2 * STATE), F32),
        ],
        scratch_shapes=[
            pltpu.VMEM((STATE, width), F32),
            pltpu.VMEM((8, width), F32),
            pltpu.VMEM((8, 2 * STATE), F32),
            pltpu.VMEM((width // 128, CHUNK + 8, 128), F32),
            pltpu.VMEM((CHUNK + 8, 2 * STATE), F32),
        ],
        compiler_params=pltpu.CompilerParams(vmem_limit_bytes=VMEM),
        cost_estimate=pl.CostEstimate(
            flops=tokens * width * 16 * 256,
            bytes_accessed=tokens * width * 20,
            transcendentals=tokens * width * 3,
        ),
        name="scan_forward",
    )(vpre, spre, step_pre, vtaps, staps, bias, log_decay, skip)


def taps_back(d_total, later, x, taps, moved):
    moved[:CHUNK, :] = d_total
    moved[CHUNK:, :] = later
    d_x = d_total * taps[CONV - 1 : CONV, :]
    rows = []
    for k in range(CONV - 1):
        later_rows = moved[3 - k : 3 - k + CHUNK, :]
        d_x = d_x + later_rows * taps[k : k + 1, :]
        rows.append(jnp.sum(later_rows * x, axis=0, keepdims=True))
    rows.append(jnp.sum(d_total * x, axis=0, keepdims=True))
    return d_x, rows + [jnp.sum(d_total, axis=0, keepdims=True)]


def backward_kernel(
    vpre, values, vslope, spre, states_ref, sslope, spre_step, vtaps, staps, bias, log_decay, skip, chooser,
    mixer, d_mixer, starts,
    values_low, d_spre, step_low, value_sums, state_sums, step_sums,
    later_grad, later_state, vhead, shead, vmoved, smoved,
):
    @pl.when(pl.program_id(0) == 0)
    def _():
        for ref in (later_grad, later_state, vhead, shead, value_sums, state_sums, step_sums):
            ref[...] = jnp.zeros_like(ref)

    states = states_ref[...]
    b, c = states[:, :STATE], states[:, STATE:]
    shifted_pre, step, rates, cum = step_terms(spre_step, bias, log_decay)
    cum_t = cum.T
    final = cum[CHUNK - 1 :, :]
    grown, ending, whole = jnp.exp(cum), jnp.exp(final - cum), jnp.exp(final)
    b2, c2 = halves(b), halves(c)
    b_left, ct2 = beside(b2), halves(c.T)
    causal = square(1) >= square(0)
    scores_t = jnp.where(causal, folded(mm_nt(b_left, right_side_nt(c2))), 0.0)
    left = lax.broadcasted_iota(jnp.int32, (1, 128), 1) < 64
    zero = jnp.zeros((CHUNK, 128), BF)
    d_early = jnp.zeros((HALF, CHUNK), F32)
    d_late = jnp.zeros((HALF, HALF), F32)
    d_b = jnp.zeros((CHUNK, STATE), F32)
    d_c = jnp.zeros((CHUNK, STATE), F32)
    by_head = jnp.zeros((2 * CHUNK, 128), F32)
    at_end = jnp.zeros((8, 128), F32)
    for p in range(vpre.shape[1] // 128):
        lanes = slice(128 * p, 128 * p + 128)
        pick = chooser[256 * p : 256 * p + 256, :]
        v, dy = values[:, lanes], d_mixer[:, lanes]
        steps = by_pair(step, p)
        weighted = v * steps
        w2, d2 = halves(weighted), halves(dy)
        w_rest = pltpu.roll(weighted - w2[0].astype(F32), 64, 1).astype(BF)
        d_top = pltpu.roll(d2[0].astype(F32), 64, 1).astype(BF)
        early, late = [], []
        for h, mine in ((2 * p, left), (2 * p + 1, ~left)):
            gap = cum_t[h : h + 1, :] - cum[:HALF, h : h + 1]
            decay_early = jnp.exp(jnp.minimum(gap, 0.0))
            gap = cum_t[h : h + 1, HALF:] - cum[HALF:, h : h + 1]
            decay_late = jnp.exp(jnp.minimum(gap, 0.0))
            early.append(decay_early * scores_t[:HALF, :])
            late.append(decay_late * scores_t[HALF:, HALF:])
            one = beside((jnp.where(mine, w2[0], w_rest), jnp.where(mine, w2[0], zero)))
            other = beside((jnp.where(mine, d2[0], d_top), jnp.where(mine, d2[1], zero)))
            d_mix = mm_nt(one, other)
            d_early = d_early + d_mix[:HALF, :] * decay_early
            d_late = d_late + d_mix[HALF:, HALF:] * decay_late
        early = halves(jnp.concatenate(early, axis=0))
        early = folded(mm(early[0], beside(d2))) + mm(early[1], d2[0])
        late = beside(halves(jnp.concatenate(late, axis=0)))
        late = folded(mm(late, right_side((d2[0][HALF:], d2[1][HALF:]))))
        within = jnp.concatenate(
            [
                jnp.where(left, early[:HALF], early[HALF:]),
                jnp.where(left, late[:HALF], late[HALF:]),
            ],
            axis=0,
        )
        held, after_here = starts[0, :, lanes], later_grad[:, lanes]
        after2 = halves(after_here)
        ends = by_pair(ending, p)
        d_weighted = within + ends * folded(mm(b_left, right_side(after2)))
        gain = skip[:, lanes]
        both = jnp.concatenate([dy * (mixer[:, lanes] - gain * v), v * d_weighted], axis=0)
        by_head = by_head + mm(beside(halves(both)), pick)
        ended = jnp.sum(after_here * later_state[:, lanes], axis=0, keepdims=True)
        at_end = at_end + mm(beside(halves(jnp.broadcast_to(ended, (8, 128)))), pick)
        faded = halves(by_pair(grown, p) * dy)
        d_c = d_c + folded(mm_nt(beside(faded), right_side_nt(halves(held))))
        d_b = d_b + folded(mm_nt(beside(halves(weighted * ends)), right_side_nt(after2)))
        added = folded(mm(ct2[0], beside(faded))) + mm(ct2[1], faded[0])
        later_grad[:, lanes] = after_here * by_pair(whole, p) + added
        d_total = (steps * d_weighted + gain * dy) * vslope[:, lanes]
        d_x, rows = taps_back(
            d_total, vhead[:, lanes], vpre[:, lanes], vtaps[:, lanes], vmoved.at[p]
        )
        values_low[:, lanes] = d_x.astype(BF)
        rows += [jnp.sum(v * dy, axis=0, keepdims=True), jnp.zeros((2, 128), F32)]
        value_sums[:, lanes] += jnp.concatenate(rows, axis=0)
        vhead[:, lanes] = d_total[:8]
    later_state[...] = starts[0]
    d_late = jnp.concatenate([jnp.zeros((HALF, HALF), F32), d_late], axis=1)
    d_scores_t = jnp.where(causal, jnp.concatenate([d_early, d_late], axis=0), 0.0)
    top, rest = halves(d_scores_t)
    d_b = d_b + folded(mm(top, beside(c2))) + mm(rest, c2[0])
    top, rest = halves(d_scores_t.T)
    d_c = d_c + folded(mm(top, beside(b2))) + mm(rest, b2[0])
    reached, pulled = by_head[:CHUNK], by_head[CHUNK:]
    last = lax.broadcasted_iota(jnp.int32, (CHUNK, 128), 0) == CHUNK - 1
    d_cum = reached - step * pulled + jnp.where(last, at_end[:1], 0.0)
    d_rate = summed_by(jnp.where(causal, 1.0, 0.0).astype(BF), d_cum)
    d_shifted = (pulled - rates * d_rate) * jax.nn.sigmoid(shifted_pre)
    step_low[...] = d_shifted.astype(BF)
    step_sums[0:1, :] += jnp.sum(d_shifted, axis=0, keepdims=True)
    step_sums[1:2, :] -= jnp.sum(d_rate * step, axis=0, keepdims=True) * rates
    d_total = beside((d_b, d_c)) * sslope[...]
    d_x, rows = taps_back(d_total, shead[...], spre[...], staps[...], smoved)
    d_spre[...] = d_x
    state_sums[...] += jnp.concatenate(rows + [jnp.zeros((3, 2 * STATE), F32)], axis=0)
    shead[...] = d_total[:8]


def backward_scan(
    vpre, values, vslope, spre, states, sslope, step_pre, vtaps, staps, bias, log_decay, skip, mixer, d_mixer,
    starts,
):
    tokens, width = vpre.shape
    chunks = tokens // CHUNK
    lane = jnp.arange(2 * width)
    heads = 2 * (lane // 256) + lane % 128 // 64
    chooser = (heads[:, None] == jnp.arange(128)[None, :]).astype(BF)
    row = lambda n: pl.BlockSpec((CHUNK, n), lambda i: (chunks - 1 - i, 0))
    fixed = lambda x: pl.BlockSpec(x.shape, lambda i: (0, 0))
    summed = lambda n: pl.BlockSpec((8, n), lambda i: (0, 0))
    return pl.pallas_call(
        backward_kernel,
        grid=(chunks,),
        in_specs=[row(width)] * 3 + [row(2 * STATE)] * 3 + [row(128)]
        + [fixed(x) for x in (vtaps, staps, bias, log_decay, skip, chooser)]
        + [row(width), row(width), pl.BlockSpec((1, STATE, width), lambda i: (chunks - 1 - i, 0, 0))],
        out_specs=[
            row(width), row(2 * STATE), row(128), summed(width), summed(2 * STATE), summed(128),
        ],
        out_shape=[
            jax.ShapeDtypeStruct((tokens, width), BF),
            jax.ShapeDtypeStruct((tokens, 2 * STATE), F32),
            jax.ShapeDtypeStruct((tokens, 128), BF),
            jax.ShapeDtypeStruct((8, width), F32),
            jax.ShapeDtypeStruct((8, 2 * STATE), F32),
            jax.ShapeDtypeStruct((8, 128), F32),
        ],
        scratch_shapes=[
            pltpu.VMEM((STATE, width), F32),
            pltpu.VMEM((STATE, width), F32),
            pltpu.VMEM((8, width), F32),
            pltpu.VMEM((8, 2 * STATE), F32),
            pltpu.VMEM((width // 128, CHUNK + 8, 128), F32),
            pltpu.VMEM((CHUNK + 8, 2 * STATE), F32),
        ],
        compiler_params=pltpu.CompilerParams(vmem_limit_bytes=VMEM),
        cost_estimate=pl.CostEstimate(
            flops=tokens * width * 40 * 256,
            bytes_accessed=tokens * width * 24,
            transcendentals=tokens * width * 3,
        ),
        name="scan_backward",
    )(
        vpre, values, vslope, spre, states, sslope, step_pre, vtaps, staps, bias, log_decay, skip, chooser,
        mixer, d_mixer, starts,
    )


def place(arrays, piece, targets, rows):
    count = sum(x.shape[0] // piece for x in arrays)
    assert count == len(targets)
    width, dtype = arrays[0].shape[1], arrays[0].dtype

    def kernel(at, *refs):
        sources, out, done = refs[: len(arrays)], refs[len(arrays)], refs[len(arrays) + 1]
        copies = []
        for source in sources:
            for j in range(source.shape[0] // piece):
                k = len(copies)
                start = pl.multiple_of(at[k], piece)
                copies.append(
                    pltpu.make_async_copy(
                        source.at[pl.ds(j * piece, piece)], out.at[pl.ds(start, piece)], done.at[k]
                    )
                )
        for copy in copies:
            copy.start()
        for copy in copies:
            copy.wait()

    return pl.pallas_call(
        kernel,
        grid_spec=pltpu.PrefetchScalarGridSpec(
            num_scalar_prefetch=1,
            grid=(1,),
            in_specs=[pl.BlockSpec(memory_space=pl.ANY)] * len(arrays),
            out_specs=pl.BlockSpec(memory_space=pltpu.VMEM),
            scratch_shapes=[pltpu.SemaphoreType.DMA((count,))],
        ),
        out_shape=jax.ShapeDtypeStruct((rows, width), dtype),
        compiler_params=pltpu.CompilerParams(vmem_limit_bytes=16 * 1024 * 1024),
        cost_estimate=pl.CostEstimate(
            flops=0, bytes_accessed=2 * rows * width * dtype.itemsize, transcendentals=0
        ),
        name="place",
    )(jnp.stack([jnp.asarray(t, jnp.int32) for t in targets]), *arrays)


def swap(x, axis, bit=1):
    return lax.ppermute(x, axis, [(i, i ^ bit) for i in range(lax.axis_size(axis))])


def turned(x, axis, distance):
    n = lax.axis_size(axis)
    return lax.ppermute(x, axis, [(i, (i + distance) % n) for i in range(n)])


def after(x, *earlier):
    return lax.optimization_barrier((x, *earlier))[0]


def at(x, index, axis):
    return lax.dynamic_index_in_dim(x, index, axis, keepdims=False)


def part(x, index, size, axis):
    return lax.dynamic_slice_in_dim(x, index * size, size, axis)


def ordered(flag, mine, other, axis):
    first = jnp.where(flag == 0, mine, other)
    second = jnp.where(flag == 0, other, mine)
    return jnp.concatenate([first, second], axis=axis)


def paired_kernel(count, core, *refs):
    lows, weights, outs = refs[:count], refs[count : 3 * count], refs[3 * count :]
    step, tiles = pl.program_id(0), pl.num_programs(0) // 2
    for j in range(2):

        @pl.when(step // tiles == j)
        def _(j=j):
            for out, which in zip(outs, (1 - core[0], core[0]), strict=True):
                total = 0.0
                for k, low in enumerate(lows):
                    block = low[:, which]
                    total = total + mm_nt(
                        block.reshape(-1, block.shape[-1]), weights[2 * k + j][...]
                    )
                out[...] = total


def paired_products(lows, weights, core, sub):
    tokens, n = lows[0].shape[0], weights[0][0].shape[0]
    groups = tokens // (4 * sub)
    split = [x.reshape(groups, 2, 2 * sub, x.shape[1]) for x in lows]
    tile = n
    tiles = n // tile
    out = jax.ShapeDtypeStruct((tokens // 2, 2 * n), F32)
    first = lambda i, core: (jnp.minimum(i, tiles - 1), 0)
    second = lambda i, core: (jnp.maximum(i - tiles, 0), 0)
    return pl.pallas_call(
        functools.partial(paired_kernel, len(lows)),
        grid_spec=pltpu.PrefetchScalarGridSpec(
            num_scalar_prefetch=1,
            grid=(2 * tiles,),
            in_specs=[pl.BlockSpec(x.shape, lambda i, core: (0, 0, 0, 0)) for x in split]
            + [
                pl.BlockSpec((tile, w.shape[1]), where)
                for pair in weights
                for w, where in zip(pair, (first, second), strict=True)
            ],
            out_specs=[pl.BlockSpec((tokens // 2, tile), lambda i, core: (0, i))] * 2,
        ),
        out_shape=[out, out],
        compiler_params=pltpu.CompilerParams(vmem_limit_bytes=VMEM),
        cost_estimate=pl.CostEstimate(flops=1, bytes_accessed=1, transcendentals=0),
        name="paired_products",
    )(core[None], *split, *[w for pair in weights for w in pair])


def whole_sequences(
    block_input, output_grad, input_gain, gate_weight, value_weight, state_weight, step_weight,
    out_weight, value_taps, state_taps, step_bias, log_decay, skip_gain, mixer_gain,
):
    xi, ci, zi, yi = (lax.axis_index(n) for n in ("x", "core", "seq", "heads"))
    nz = lax.axis_size("seq")
    nx = lax.axis_size("x")
    d_model = block_input.shape[-1]
    half = d_model // 2
    group = block_input.shape[2]
    sub = group // 2
    tokens = group * nz
    own = sub * nz // 2
    rows = gate_weight.shape[0]
    cols = gate_weight.shape[1] // 2
    heads = step_weight.shape[1] // 2

    def turned_halves(x):
        return jnp.where(xi == 0, x, jnp.concatenate([x[:, half:], x[:, :half]], axis=1))

    def route(r):
        return [
            (c * nz + z, (z % 2) * nz + 2 * ((z // 2) ^ r) + c) for c in range(2) for z in range(nz)
        ]

    def tokens_in(x):
        rounds = []
        for r in range(2):
            piece = lax.dynamic_slice(x, ((zi // 2) ^ r, 0, yi * sub, 0), (1, 1, sub, d_model))
            rounds.append(lax.ppermute(piece.reshape(sub, d_model), ("core", "seq"), route(r)))
        return rounds

    def in_order(rounds):
        return turned_halves(ordered(zi // 2, *rounds, 0))

    def tokens_back(x):
        pieces = [part(x, (zi // 2) ^ r, sub, 0) for r in range(2)]
        return [
            lax.ppermute(piece, ("core", "seq"), [(b, a) for a, b in route(r)])
            for r, piece in enumerate(pieces)
        ]

    def tokens_home(mine, by_y):
        targets = [(2 * ((zi // 2) ^ r) + y) * sub for y in (yi, 1 - yi) for r in range(2)]
        return place([mine, by_y], sub, targets, 2 * group).reshape(block_input.shape)

    spread_targets = [
        ((2 * k + c) * 2 + y) * sub
        for y, c in ((yi, ci), (1 - yi, ci), (yi, 1 - ci), (1 - yi, 1 - ci))
        for k in range(nz // 2)
    ]

    def spread(x, by_y=None):
        by_y = swap(x, "heads") if by_y is None else by_y
        by_core = swap(x, "core")
        by_both = swap(by_y, "core")
        return place([x, by_y, by_core, by_both], sub, spread_targets, tokens)

    def of_core(x, core):
        return at(x.reshape(nz // 2, 2, 2 * sub, -1), core, 1).reshape(tokens // 2, -1)

    def over_core(send, keep, link=BF):
        return core_sum(swap(send, "core"), keep, link)

    def core_sum(received, keep, link=BF):
        received = received.reshape(nz // 2, 2, sub, keep.shape[1])
        keep = keep.reshape(received.shape)
        goes = (at(keep, 1 - yi, 1) + at(received, 1 - yi, 1)).astype(link)
        return at(keep, yi, 1) + at(received, yi, 1), goes

    def over_y(stays, received):
        return (stays + received.astype(F32)).reshape(own, -1)

    def block_of(weight):
        width = weight.shape[1] // 2
        received = swap(part(weight, 1 - ci, width, 1), "core")
        return ordered(ci, part(weight, ci, width, 1), received, 0)

    def ring(block, *earlier):
        right = turned(block, "seq", 1)
        left = turned(block, "seq", -1)
        return [block, right, left, turned(after(right, left, *earlier), "seq", 1)]

    def stacked(blocks):
        targets = [
            (c * nz + z % nz) * rows for z in (zi, zi + nz - 1, zi + 1, zi + 2) for c in range(2)
        ]
        return place(blocks, rows, targets, half)

    def products(low, features):
        return transposed(features[:, half:], low).astype(BF), transposed(features[:, :half], low)

    def over_x(kept, received):
        return (kept + received.astype(F32)).reshape(2, nz, rows, -1)

    def by_parity(summed, which):
        shape = summed.shape
        split = summed.reshape(*shape[:-3], nz // 2, 2, *shape[-2:])
        return at(split, which, split.ndim - 3)

    def first_pieces(summed):
        return by_parity(summed, 1 - zi % 2).astype(BF)

    def first_sum(summed, received):
        return by_parity(summed, zi % 2) + received.astype(F32)

    def second_pieces(summed):
        return at(summed, 1 - zi // 2, -3).astype(BF)

    def over_z(summed, received):
        return at(summed, zi // 2, -3) + received.astype(F32)

    def to_core(total):
        received = swap(at(total, 1 - ci, 0), "core")
        return at(total, ci, 0), received

    project = lambda a, b: jnp.dot(a, b, preferred_element_type=F32)
    transposed = lambda a, b: lax.dot_general(
        a, b, (((0,), (0,)), ((), ())), preferred_element_type=F32
    )
    back = lambda a, b: lax.dot_general(a, b, (((1,), (1,)), ((), ())), preferred_element_type=F32)

    pad = 128 - heads
    first = jnp.concatenate(
        [
            jnp.concatenate(
                [
                    value_weight[:, cols * k : cols * k + cols],
                    state_weight[:, STATE * k : STATE * k + STATE],
                    step_weight[:, heads * k : heads * k + heads],
                    jnp.broadcast_to(input_gain[:, None], (rows, pad)),
                ],
                axis=1,
            )
            for k in range(2)
        ],
        axis=1,
    )
    first_block = block_of(first)
    first_across = [swap(first_block, "x")]
    first_ring = ring(first_block, *first_across)
    first_across += [swap(x, "x") for x in first_ring[1:]]

    x_own = in_order(tokens_in(block_input))

    pair_weight = after(
        jnp.concatenate(
            [gate_weight[:, :cols], out_weight[:cols].T, gate_weight[:, cols:], out_weight[cols:].T],
            axis=1,
        ),
        first_block,
    )
    pair_block = block_of(pair_weight)
    pair_across = [swap(after(pair_block, first_across[0]), "x")]
    x_all = spread(after(x_own, *pair_across))
    pair_ring = ring(after(pair_block, first_ring[3]))
    pair_across += [swap(after(x, first_across[3]), "x") for x in pair_ring[1:3]] + [None]

    first_own = stacked(first_ring)
    first_other = stacked(first_across)
    def both_halves(a, w_own, w_other):
        return project(a[:, :half], w_own) + project(a[:, half:], w_other)

    split = lambda w: (w[:, :cols], w[:, cols : cols + STATE], w[:, cols + STATE :])
    value_own, state_own, step_own = split(first_own)
    value_other, state_other, step_other = split(first_other)
    gain = jnp.concatenate([step_own[:, -1], step_other[:, -1]])[None].astype(F32)
    blank = jnp.arange(128)[None, :] < heads
    step_own, step_other = jnp.where(blank, step_own, 0), jnp.where(blank, step_other, 0)

    x_wide = x_all.astype(F32)
    normed = (
        x_wide * lax.rsqrt(jnp.mean(x_wide * x_wide, axis=-1, keepdims=True) + EPS) * gain
    ).astype(BF)
    x_own = x_own.astype(F32)
    scaling = lax.rsqrt(jnp.mean(x_own * x_own, axis=-1, keepdims=True) + EPS)

    states_weights = jnp.concatenate([state_own, state_other], axis=0)
    states_received = swap(states_weights, "core")
    states_half = both_halves(normed, state_own, state_other)
    states_pre = ordered(ci, states_half, swap(states_half, "core"), 1)
    values_pre = both_halves(normed, value_own, value_other)
    step_pre = both_halves(normed, step_own, step_other)

    vtaps = part(value_taps, ci, cols, 1)
    lanes = lambda v: jnp.pad(part(v, ci, heads, 0), (0, pad))[None]
    bias, decays = lanes(step_bias), lanes(log_decay)
    skip = jnp.repeat(part(skip_gain, ci, heads, 0), cols // heads)[None]
    gain_mixer = part(mixer_gain, ci, cols, 0)[None]
    og_rounds = tokens_in(after(output_grad, pair_ring[1], pair_ring[2]))
    values_pre, states_received, *pair_across[1:3], pair_ring[3], og_rounds = lax.optimization_barrier(
        (values_pre, states_received, *pair_across[1:3], pair_ring[3], og_rounds)
    )
    og_own = in_order(og_rounds)
    og_own, values_pre = lax.optimization_barrier((og_own, values_pre))
    mixer, starts, *kept = forward_scan(
        values_pre, states_pre, step_pre, vtaps, state_taps, bias, decays, skip
    )
    pair_across[3], og_by_y, mixer = lax.optimization_barrier(
        (swap(pair_ring[3], "x"), swap(og_own, "heads"), mixer)
    )
    og = spread(og_own, og_by_y)
    pair_own = stacked(pair_ring)
    pair_other = stacked(pair_across)
    gate_own, out_own = pair_own[:, :cols], pair_own[:, cols:]
    gate_other, out_other = pair_other[:, :cols], pair_other[:, cols:]
    gate_lin = both_halves(normed, gate_own, gate_other)
    d_out = both_halves(og, out_own, out_other)
    sigmoid_gate = jax.nn.sigmoid(gate_lin)
    silu_gate = gate_lin * sigmoid_gate
    gated = mixer * silu_gate
    weighted = d_out * gain_mixer
    sums = jnp.stack([jnp.sum(gated * gated, axis=1), jnp.sum(weighted * gated, axis=1)])
    sums = sums + swap(sums, "core")
    sums = sums + swap(sums, "heads")
    inverse = lax.rsqrt(sums[0] / INNER + EPS)[:, None]
    out_normed = (gated * inverse * gain_mixer).astype(BF)
    d_gated = inverse * weighted - gated * (inverse * inverse * inverse) * (sums[1][:, None] / INNER)
    d_mixer = d_gated * silu_gate
    gate_low = (d_gated * mixer * sigmoid_gate * (1.0 + gate_lin * (1.0 - sigmoid_gate))).astype(BF)
    g_mixer_gain = jnp.sum(d_out * gated * inverse, axis=0)

    out_sum = jnp.stack(
        [transposed(og[:, :half], out_normed), transposed(og[:, half:], out_normed)]
    ).reshape(2, 2, nz, rows, cols)
    out_pieces = first_pieces(out_sum)
    branch_sends, branch_keeps = paired_products(
        [after(out_normed, out_pieces)], [(out_own, out_other)], ci, sub
    )
    gate_sends, gate_keeps = products(after(gate_low, branch_sends), normed)
    branch_stays, branch_goes = over_core(branch_sends, branch_keeps)
    d_mixer = after(d_mixer, out_pieces, gate_sends, branch_goes)
    scanned = backward_scan(
        values_pre, *kept[:2], states_pre, *kept[2:], step_pre, vtaps, state_taps, bias, decays, skip,
        mixer, d_mixer, starts,
    )
    sent = (swap(out_pieces, "seq", 1), swap(gate_sends, "x"), swap(branch_goes, "heads"))
    sent, scanned = lax.optimization_barrier((sent, scanned))
    out_received, gate_received, branch_received = sent
    values_low, d_states, step_low, value_sums, state_sums, step_sums = scanned

    out_sum = first_sum(out_sum, out_received)
    out_pieces = second_pieces(out_sum)
    gate_sum = over_x(gate_keeps, gate_received)
    gate_pieces = first_pieces(gate_sum)
    value_sends, value_keeps = products(after(values_low, out_pieces, gate_pieces), normed)
    d_states = after(d_states, gate_pieces)
    states_stay, states_go = over_core(of_core(d_states, 1 - ci), of_core(d_states, ci), F32)
    dn_sends, dn_keeps = paired_products(
        [after(gate_low, value_sends, states_go), values_low, step_low],
        [(gate_own, gate_other), (value_own, value_other), (step_own, step_other)],
        ci,
        sub,
    )
    states_low = over_y(states_stay, swap(states_go, "heads")).astype(BF)
    dn_sends = after(dn_sends, states_low)
    states_by_y = swap(states_low, "heads")
    states_by_core = swap(after(states_low, states_by_y), "core")
    states_by_both = swap(after(states_by_y, states_by_core), "core")
    states_all = place(
        [x.astype(F32) for x in (states_low, states_by_y, states_by_core, states_by_both)],
        sub,
        spread_targets,
        tokens,
    ).astype(BF)
    parts = [
        products(part(states_all, ci, STATE, 1), normed),
        products(step_low, normed),
    ]
    small_sends, small_keeps = (jnp.concatenate(p, axis=1) for p in zip(*parts, strict=True))
    branch = over_y(branch_stays, after(branch_received, dn_sends))
    output_rows = turned_halves((x_own + branch).astype(BF))
    (
        value_received, gate_received, small_sends, dn_received, dn_keeps, out_received, output_rows
    ) = lax.optimization_barrier(
        (
            swap(value_sends, "x"), swap(gate_pieces, "seq", 1), small_sends,
            swap(dn_sends, "core"), dn_keeps, swap(out_pieces, "seq", 2), output_rows,
        )
    )

    dn_stays, dn_goes = core_sum(dn_received, dn_keeps)
    output_sent = tokens_back(output_rows)
    gate_sum = first_sum(after(gate_sum, dn_goes), gate_received)
    gate_pieces = second_pieces(gate_sum)
    value_sum = over_x(after(value_keeps, dn_goes), value_received)
    value_pieces = first_pieces(value_sum)
    states_weights = ordered(ci, states_weights, states_received, 1)
    dn_received, output_sent, value_received, small_received = lax.optimization_barrier(
        (
            swap(dn_goes, "heads"), output_sent, swap(value_pieces, "seq", 1), swap(small_sends, "x"),
        )
    )

    d_normed = over_y(dn_stays, dn_received) + back(states_low, states_weights)
    pushed = d_normed * gain
    d_tokens = scaling * pushed - x_own * (scaling * scaling * scaling) * jnp.mean(
        pushed * x_own, axis=-1, keepdims=True
    )
    input_rows = turned_halves((og_own.astype(F32) + d_tokens).astype(BF))
    g_input_gain = turned_halves(jnp.sum(d_normed * x_own * scaling, axis=0)[None])
    per_core = jnp.concatenate(
        [value_sums[:6], g_mixer_gain[None], jnp.pad(step_sums[:2].reshape(1, -1), ((0, 0), (0, cols - 256)))],
        axis=0,
    ).reshape(-1, 256)
    shared = jnp.concatenate([state_sums, g_input_gain.reshape(-1, 256)], axis=0)
    shared = shared + swap(shared, "heads")
    received = swap(jnp.concatenate([per_core, shared], axis=0), "core")
    n_core = per_core.shape[0]
    pack = jnp.concatenate(
        [ordered(ci, per_core, received[:n_core], 0), shared + received[n_core:]], axis=0
    )
    output_sent = jnp.concatenate(after(output_sent, shared), axis=0)
    small_sum = over_x(small_keeps, after(small_received, input_rows))
    small_sum = first_sum(small_sum, swap(first_pieces(small_sum), "seq", 1))
    small_pieces = second_pieces(small_sum)
    input_sent, output_by_y, gate_received, small_pieces, pack = lax.optimization_barrier(
        (
            tokens_back(input_rows), swap(output_sent, "heads"), swap(gate_pieces, "seq", 2),
            small_pieces, pack,
        )
    )

    input_sent = jnp.concatenate(input_sent, axis=0)
    value_sum = first_sum(value_sum, value_received)
    value_pieces = second_pieces(value_sum)
    g_out = over_z(out_sum, out_received)
    pack = pack + swap(pack, "x")
    g_out = g_out[0] + swap(g_out[1].astype(BF), "x").astype(F32)
    out_mine, out_received = to_core(g_out)
    input_by_y, value_received, small_received, out_received, pack = lax.optimization_barrier(
        (
            swap(input_sent, "heads"), swap(value_pieces, "seq", 2), swap(small_pieces, "seq", 2),
            out_received, pack,
        )
    )
    pack = pack + swap(pack, "seq", 1)
    pack = pack + swap(pack, "seq", 2)
    g_gate = over_z(gate_sum, gate_received)
    g_value = over_z(value_sum, value_received)
    g_small = over_z(small_sum, small_received)
    block_output = tokens_home(output_sent, output_by_y)
    grad_input = tokens_home(input_sent, input_by_y)

    both, shared = pack[: 2 * n_core].reshape(2, 8, cols), pack[2 * n_core :]
    by_channel = jnp.transpose(both, (1, 0, 2)).reshape(8, 2 * cols)
    per_head = both[:, 7, :256].reshape(2, 2, 128)[:, :, :heads]
    input_gain_all = shared[8:].reshape(nx, 2, nz, rows)
    my_gain = at(at(at(input_gain_all, xi, 0), ci, 0), zi, 0)

    def widths(mine, received):
        return ordered(ci, mine, received, 1)

    small_mine, small_received = to_core(g_small)
    steps_at = slice(STATE, STATE + heads)
    return (
        block_output,
        grad_input,
        my_gain,
        widths(*to_core(g_gate)),
        widths(*to_core(g_value)),
        widths(small_mine[:, :STATE], small_received[:, :STATE]),
        widths(small_mine[:, steps_at], small_received[:, steps_at]),
        widths(out_mine, out_received).T,
        by_channel[:5],
        shared[:5],
        per_head[:, 0].reshape(-1),
        per_head[:, 1].reshape(-1),
        jnp.sum(by_channel[5].reshape(2 * heads, -1), axis=1),
        by_channel[6],
    )


def solution(mesh):
    sizes = dict(mesh.shape)
    if sizes["seq"] == 2 * MB and sizes["dp"] == 4 and sizes["heads"] == 2:
        devices = mesh.devices.reshape(sizes["dp"] // 2, 2, sizes["seq"], sizes["heads"])
        mesh = jax.sharding.Mesh(devices, ("x", "core", "seq", "heads"))
        body, dp = whole_sequences, ("x", "core")
    else:
        body, dp = shards, ("dp",)
    tokens = P(None, dp, "seq", None)
    both = (*dp, "seq")
    return jax.shard_map(
        body,
        mesh=mesh,
        in_specs=(
            tokens,
            tokens,
            P(both),
            P(both, "heads"),
            P(both, "heads"),
            P(both, None),
            P(both, "heads"),
            P("heads", both),
            P(None, "heads"),
            P(),
            P("heads"),
            P("heads"),
            P("heads"),
            P("heads"),
        ),
        out_specs=(
            tokens,
            tokens,
            P(both),
            P(both, "heads"),
            P(both, "heads"),
            P(both, None),
            P(both, "heads"),
            P("heads", both),
            P(None, "heads"),
            P(),
            P("heads"),
            P("heads"),
            P("heads"),
            P("heads"),
        ),
        check_vma=False,
    )
```

```python
import functools

import jax
import jax.numpy as jnp
from jax import lax
from jax.experimental import pallas as pl
from jax.experimental.pallas import tpu as pltpu
from jax.sharding import PartitionSpec as P

STATE = 128
CONV = 4
MB = 2
INNER = 3072


EPS = 1e-05
HIGH = lax.Precision.HIGHEST


def shifted(block, axis, distance):
    devices = range(lax.axis_size(axis))
    route = [(i - distance, i) for i in devices if i - distance in devices]
    return lax.ppermute(block, axis, route)


def entering(x, axis, combine, identity, reverse):
    peers, index = (lax.axis_size(axis), lax.axis_index(axis))
    everything = jax.tree.map(lambda part: lax.all_gather(part, axis), x)
    start = jax.tree.map(
        lambda part, zero: jnp.broadcast_to(jnp.asarray(zero, part.dtype), part.shape), x, identity
    )

    def step(k, before):
        at = peers - 1 - k if reverse else k
        reached = at > index if reverse else at < index
        new = combine(before, jax.tree.map(lambda part: part[at], everything))
        return jax.tree.map(lambda a, b: jnp.where(reached, a, b), new, before)

    return lax.fori_loop(0, peers, step, start)


def norm_rows(values, gain):
    return values * lax.rsqrt(jnp.mean(values * values, axis=-1, keepdims=True) + EPS) * gain


def conv_silu(extended, taps):
    length = extended.shape[1] - (CONV - 1)
    total = jnp.zeros((extended.shape[0], length, extended.shape[2]), jnp.float32) + taps[CONV]
    for offset in range(CONV):
        total = total + extended[:, offset : offset + length] * taps[offset]
    return jax.nn.silu(total)


def local_parts(
    values_ext, states_ext, step_pre, value_taps, state_taps, step_bias, log_decay, skip_gain
):
    values_conv = conv_silu(values_ext, value_taps)
    states_conv = conv_silu(states_ext, state_taps)
    batch, length, channels = values_conv.shape
    heads_here = step_pre.shape[-1]
    values = values_conv.reshape(batch, length, heads_here, channels // heads_here)
    input_mat = states_conv[..., :STATE]
    output_mat = states_conv[..., STATE:]
    stepsize = jax.nn.softplus(step_pre + step_bias)
    cumulative = jnp.cumsum(-stepsize * jnp.exp(log_decay), axis=1)
    gaps = cumulative[:, :, None, :] - cumulative[:, None, :, :]
    causal = (jnp.arange(length)[:, None] >= jnp.arange(length)[None, :])[None, :, :, None]
    decays = jnp.where(causal, jnp.exp(jnp.where(causal, gaps, 0.0)), 0.0)
    scores = jnp.einsum("btn,bsn->bts", output_mat, input_mat, precision=HIGH)
    weights = decays * scores[..., None] * stepsize[:, None, :, :]
    within = (
        jnp.einsum("btsh,bshp->bthp", weights, values, precision=HIGH) + skip_gain[:, None] * values
    )
    final = cumulative[:, -1]
    ending = jnp.exp(final[:, None, :] - cumulative) * stepsize
    local_state = jnp.einsum("bth,btn,bthp->bhnp", ending, input_mat, values, precision=HIGH)
    return (within, local_state, jnp.exp(final), cumulative, output_mat)


def carried_part(cumulative, output_mat, state_in):
    return jnp.exp(cumulative)[..., None] * jnp.einsum(
        "btn,bhnp->bthp", output_mat, state_in, precision=HIGH
    )


def whole_block(
    values_ext,
    states_ext,
    step_pre,
    value_taps,
    state_taps,
    step_bias,
    log_decay,
    skip_gain,
    state_in,
):
    within, local_state, span_decay, cumulative, output_mat = local_parts(
        values_ext, states_ext, step_pre, value_taps, state_taps, step_bias, log_decay, skip_gain
    )
    result = within + carried_part(cumulative, output_mat, state_in)
    return (result.reshape(result.shape[0], result.shape[1], -1), local_state, span_decay)


def compose(earlier, later):
    return (earlier[0] * later[0], later[0][..., None, None] * earlier[1] + later[1])


def shards(
    block_input,
    output_grad,
    input_gain,
    gate_weight,
    value_weight,
    state_weight,
    step_weight,
    out_weight,
    value_taps,
    state_taps,
    step_bias,
    log_decay,
    skip_gain,
    mixer_gain,
):
    margin = CONV - 1
    width = block_input.shape[-1]
    inner_here = gate_weight.shape[1]
    state_cols = state_weight.shape[1]
    heads_here = step_weight.shape[1]
    acc_gain = jnp.zeros((width,), jnp.float32)
    acc_gate = jnp.zeros((width, inner_here), jnp.float32)
    acc_value = jnp.zeros((width, inner_here), jnp.float32)
    acc_state = jnp.zeros((width, state_cols), jnp.float32)
    acc_step = jnp.zeros((width, heads_here), jnp.float32)
    acc_out = jnp.zeros((inner_here, width), jnp.float32)
    acc_value_taps = jnp.zeros_like(value_taps)
    acc_state_taps = jnp.zeros_like(state_taps)
    acc_step_bias = jnp.zeros_like(step_bias)
    acc_log_decay = jnp.zeros_like(log_decay)
    acc_skip = jnp.zeros_like(skip_gain)
    acc_mixer_gain = jnp.zeros_like(mixer_gain)
    outputs = []
    input_grads = []
    for micro_batch in range(MB):
        weights_now = (
            lax.all_gather(input_gain, ("dp", "seq"), axis=0, tiled=True),
            lax.all_gather(gate_weight, ("dp", "seq"), axis=0, tiled=True),
            lax.all_gather(value_weight, ("dp", "seq"), axis=0, tiled=True),
            lax.all_gather(state_weight, ("dp", "seq"), axis=0, tiled=True),
            lax.all_gather(step_weight, ("dp", "seq"), axis=0, tiled=True),
            lax.all_gather(out_weight, ("dp", "seq"), axis=1, tiled=True),
        )
        gain_full, gate_full, value_full, state_full, step_full, out_full = weights_now
        tokens = block_input[micro_batch].astype(jnp.float32)
        normed = norm_rows(tokens, gain_full.astype(jnp.float32)).astype(jnp.bfloat16)
        gate_lin = jnp.einsum("btd,di->bti", normed, gate_full, preferred_element_type=jnp.float32)
        values_pre = jnp.einsum(
            "btd,di->bti", normed, value_full, preferred_element_type=jnp.float32
        )
        states_pre = jnp.einsum(
            "btd,di->bti", normed, state_full, preferred_element_type=jnp.float32
        )
        step_pre = jnp.einsum("btd,di->bti", normed, step_full, preferred_element_type=jnp.float32)
        outgoing = jnp.concatenate([values_pre[:, -margin:], states_pre[:, -margin:]], axis=2)
        incoming = shifted(outgoing, "seq", 1)
        values_ext = jnp.concatenate([incoming[..., :inner_here], values_pre], axis=1)
        states_ext = jnp.concatenate([incoming[..., inner_here:], states_pre], axis=1)
        within, local_state, span_decay, cumulative, output_mat = local_parts(
            values_ext,
            states_ext,
            step_pre,
            value_taps,
            state_taps,
            step_bias,
            log_decay,
            skip_gain,
        )
        prefix = entering(
            (span_decay, local_state),
            "seq",
            compose,
            (jnp.ones_like(span_decay), jnp.zeros_like(local_state)),
            False,
        )
        state_in = prefix[1]
        mixer = (within + carried_part(cumulative, output_mat, state_in)).reshape(gate_lin.shape)
        silu_gate = jax.nn.silu(gate_lin)
        gated = mixer * silu_gate
        total_sq = lax.psum(jnp.sum(gated * gated, axis=-1), "heads")
        inverse = lax.rsqrt(total_sq / INNER + EPS)[..., None]
        out_normed = (gated * inverse * mixer_gain).astype(jnp.bfloat16)
        partial_out = jnp.einsum(
            "bti,id->btd", out_normed, out_full, preferred_element_type=jnp.float32
        )
        branch = lax.psum(partial_out, "heads")
        outputs.append((tokens + branch).astype(jnp.bfloat16))
        weights_back = (
            lax.all_gather(input_gain, ("dp", "seq"), axis=0, tiled=True),
            lax.all_gather(gate_weight, ("dp", "seq"), axis=0, tiled=True),
            lax.all_gather(value_weight, ("dp", "seq"), axis=0, tiled=True),
            lax.all_gather(state_weight, ("dp", "seq"), axis=0, tiled=True),
            lax.all_gather(step_weight, ("dp", "seq"), axis=0, tiled=True),
            lax.all_gather(out_weight, ("dp", "seq"), axis=1, tiled=True),
        )
        gain_full, gate_full, value_full, state_full, step_full, out_full = weights_back
        grad_out = output_grad[micro_batch]
        d_out_normed = jnp.einsum(
            "btd,id->bti", grad_out, out_full, preferred_element_type=jnp.float32
        )
        acc_out = acc_out + jnp.einsum(
            "bti,btd->id", out_normed, grad_out, preferred_element_type=jnp.float32
        )
        acc_mixer_gain = acc_mixer_gain + jnp.sum(d_out_normed * gated * inverse, axis=(0, 1))
        weighted = d_out_normed * mixer_gain
        dot_total = lax.psum(jnp.sum(weighted * gated, axis=-1), "heads")
        d_gated = inverse * weighted - gated * (inverse * inverse * inverse) * (
            dot_total[..., None] / INNER
        )
        d_mixer = d_gated * silu_gate
        sigmoid_gate = jax.nn.sigmoid(gate_lin)
        d_gate_lin = d_gated * mixer * sigmoid_gate * (1.0 + gate_lin * (1.0 - sigmoid_gate))
        carry_grad = jnp.einsum(
            "bth,btn,bthp->bhnp",
            jnp.exp(cumulative),
            output_mat,
            d_mixer.reshape(within.shape),
            precision=HIGH,
        )
        suffix = entering(
            (span_decay, carry_grad),
            "seq",
            compose,
            (jnp.ones_like(span_decay), jnp.zeros_like(carry_grad)),
            True,
        )
        later_grad = suffix[1]
        d_decay = jnp.sum(later_grad * state_in, axis=(2, 3))
        ignored, pullback = jax.vjp(
            whole_block,
            values_ext,
            states_ext,
            step_pre,
            value_taps,
            state_taps,
            step_bias,
            log_decay,
            skip_gain,
            state_in,
        )
        (
            d_values_ext,
            d_states_ext,
            d_step_pre,
            g_value_taps,
            g_state_taps,
            g_step_bias,
            g_log_decay,
            g_skip,
            unused_state,
        ) = pullback((d_mixer, later_grad, d_decay))
        rim_grads = jnp.concatenate([d_values_ext[:, :margin], d_states_ext[:, :margin]], axis=2)
        returned = shifted(rim_grads, "seq", -1)
        d_values_pre = d_values_ext[:, margin:].at[:, -margin:].add(returned[..., :inner_here])
        d_states_pre = d_states_ext[:, margin:].at[:, -margin:].add(returned[..., inner_here:])
        gate_low = d_gate_lin.astype(jnp.bfloat16)
        values_low = d_values_pre.astype(jnp.bfloat16)
        step_low = d_step_pre.astype(jnp.bfloat16)
        d_normed_part = (
            jnp.einsum("bti,di->btd", gate_low, gate_full, preferred_element_type=jnp.float32)
            + jnp.einsum("bti,di->btd", values_low, value_full, preferred_element_type=jnp.float32)
            + jnp.einsum("bti,di->btd", step_low, step_full, preferred_element_type=jnp.float32)
        )
        d_normed_sum, d_states_total, state_taps_total = lax.psum(
            (d_normed_part, d_states_pre, g_state_taps), "heads"
        )
        states_low = d_states_total.astype(jnp.bfloat16)
        d_normed = d_normed_sum + jnp.einsum(
            "bti,di->btd", states_low, state_full, preferred_element_type=jnp.float32
        )
        acc_gate = acc_gate + jnp.einsum(
            "btd,bti->di", normed, gate_low, preferred_element_type=jnp.float32
        )
        acc_value = acc_value + jnp.einsum(
            "btd,bti->di", normed, values_low, preferred_element_type=jnp.float32
        )
        acc_state = acc_state + jnp.einsum(
            "btd,bti->di", normed, states_low, preferred_element_type=jnp.float32
        )
        acc_step = acc_step + jnp.einsum(
            "btd,bti->di", normed, step_low, preferred_element_type=jnp.float32
        )
        scaling = lax.rsqrt(jnp.mean(tokens * tokens, axis=-1, keepdims=True) + EPS)
        acc_gain = acc_gain + jnp.sum(d_normed * tokens * scaling, axis=(0, 1))
        pushed = d_normed * gain_full.astype(jnp.float32)
        d_tokens = scaling * pushed - tokens * (scaling * scaling * scaling) * jnp.mean(
            pushed * tokens, axis=-1, keepdims=True
        )
        input_grads.append((grad_out.astype(jnp.float32) + d_tokens).astype(jnp.bfloat16))
        acc_value_taps = acc_value_taps + g_value_taps
        acc_state_taps = acc_state_taps + state_taps_total
        acc_step_bias = acc_step_bias + g_step_bias
        acc_log_decay = acc_log_decay + g_log_decay
        acc_skip = acc_skip + g_skip
    summed = (
        lax.psum_scatter(acc_gain, ("dp", "seq"), scatter_dimension=0, tiled=True),
        lax.psum_scatter(acc_gate, ("dp", "seq"), scatter_dimension=0, tiled=True),
        lax.psum_scatter(acc_value, ("dp", "seq"), scatter_dimension=0, tiled=True),
        lax.psum_scatter(acc_state, ("dp", "seq"), scatter_dimension=0, tiled=True),
        lax.psum_scatter(acc_step, ("dp", "seq"), scatter_dimension=0, tiled=True),
        lax.psum_scatter(acc_out, ("dp", "seq"), scatter_dimension=1, tiled=True),
    )
    smalls = lax.psum(
        (acc_value_taps, acc_state_taps, acc_step_bias, acc_log_decay, acc_skip, acc_mixer_gain),
        ("dp", "seq"),
    )
    return (
        jnp.stack(outputs),
        jnp.stack(input_grads),
        summed[0],
        summed[1],
        summed[2],
        summed[3],
        summed[4],
        summed[5],
        smalls[0],
        smalls[1],
        smalls[2],
        smalls[3],
        smalls[4],
        smalls[5],
    )


BF = jnp.bfloat16
F32 = jnp.float32
CHUNK = 256
HALF = 128
VMEM = 18 * 1024 * 1024


def halves(x):
    top = x.astype(BF)
    return top, (x - top.astype(F32)).astype(BF)


def mm(a, b):
    return lax.dot_general(a, b, (((1,), (0,)), ((), ())), preferred_element_type=F32)


def mm_nt(a, b):
    return lax.dot_general(a, b, (((1,), (1,)), ((), ())), preferred_element_type=F32)


def beside(pair):
    return jnp.concatenate(pair, axis=1)


def right_side(b):
    top, rest = b
    return jnp.concatenate([beside((top, rest)), beside((top, jnp.zeros_like(top)))], axis=0)


def right_side_nt(b):
    top, rest = b
    return jnp.concatenate([beside((top, top)), beside((rest, jnp.zeros_like(top)))], axis=0)


def folded(wide):
    n = wide.shape[1] // 2
    return wide[:, :n] + wide[:, n:]


def softplus(x):
    return jnp.maximum(x, 0.0) + jnp.log1p(jnp.exp(-jnp.abs(x)))


def taps_applied(x, before, taps, moved):
    moved[:8, :] = before
    moved[8:, :] = x
    total = taps[CONV : CONV + 1, :]
    for k in range(CONV - 1):
        total = total + moved[5 + k : 5 + k + CHUNK, :] * taps[k : k + 1, :]
    return total + x * taps[CONV - 1 : CONV, :]


def summed_by(ones, x):
    top, rest = halves(x)
    low = x - top.astype(F32) - rest.astype(F32)
    return folded(mm(ones, beside((top, rest)))) + mm(ones, low.astype(BF))


def square(which):
    return lax.broadcasted_iota(jnp.int32, (CHUNK, CHUNK), which)


def step_terms(step_ref, bias_ref, log_decay_ref):
    shifted_pre = step_ref[...] + bias_ref[...]
    step = softplus(shifted_pre)
    rates = jnp.exp(log_decay_ref[...])
    cum = summed_by(jnp.where(square(0) >= square(1), 1.0, 0.0).astype(BF), -step * rates)
    return shifted_pre, step, rates, cum


def by_pair(q, p):
    left = lax.broadcasted_iota(jnp.int32, (1, 128), 1) < 64
    return jnp.where(left, q[:, 2 * p : 2 * p + 1], q[:, 2 * p + 1 : 2 * p + 2])


def forward_kernel(
    vpre, spre, spre_step, vtaps, staps, bias, log_decay, skip,
    mixer, starts, values, vslope, states_ref, sslope, state, vtail, stail, vmoved, smoved,
):
    @pl.when(pl.program_id(0) == 0)
    def _():
        state[...] = jnp.zeros_like(state)
        vtail[...] = jnp.zeros_like(vtail)
        stail[...] = jnp.zeros_like(stail)

    sx = spre[...]
    total = taps_applied(sx, stail[...], staps[...], smoved)
    sigmoid = jax.nn.sigmoid(total)
    states = total * sigmoid
    states_ref[...] = states
    sslope[...] = sigmoid * (1.0 + total * (1.0 - sigmoid))
    stail[...] = sx[CHUNK - 8 :]
    b, c = states[:, :STATE], states[:, STATE:]
    shifted_pre, step, rates, cum = step_terms(spre_step, bias, log_decay)
    cum_t = cum.T
    final = cum[CHUNK - 1 :, :]
    grown, ending, whole = jnp.exp(cum), jnp.exp(final - cum), jnp.exp(final)
    c_left, bt2 = beside(halves(c)), halves(b.T)
    scores = folded(mm_nt(c_left, right_side_nt(halves(b))))
    scores = jnp.where(square(0) >= square(1), scores, 0.0)
    left = lax.broadcasted_iota(jnp.int32, (1, 128), 1) < 64
    starts[0] = state[...]
    for p in range(vpre.shape[1] // 128):
        lanes = slice(128 * p, 128 * p + 128)
        vx = vpre[:, lanes]
        total = taps_applied(vx, vtail[:, lanes], vtaps[:, lanes], vmoved.at[p])
        vtail[:, lanes] = vx[CHUNK - 8 :]
        sigmoid = jax.nn.sigmoid(total)
        v = total * sigmoid
        values[:, lanes] = v
        vslope[:, lanes] = sigmoid * (1.0 + total * (1.0 - sigmoid))
        weighted = v * by_pair(step, p)
        w2 = halves(weighted)
        early, late = [], []
        for h in (2 * p, 2 * p + 1):
            gap = cum[:HALF, h : h + 1] - cum_t[h : h + 1, :HALF]
            early.append(jnp.exp(jnp.minimum(gap, 0.0)) * scores[:HALF, :HALF])
            gap = cum[HALF:, h : h + 1] - cum_t[h : h + 1, :]
            late.append(jnp.exp(jnp.minimum(gap, 0.0)) * scores[HALF:, :])
        early = beside(halves(jnp.concatenate(early, axis=0)))
        early = folded(mm(early, right_side((w2[0][:HALF], w2[1][:HALF]))))
        late = halves(jnp.concatenate(late, axis=0))
        late = folded(mm(late[0], beside(w2))) + mm(late[1], w2[0])
        within = jnp.concatenate(
            [
                jnp.where(left, early[:HALF], early[HALF:]),
                jnp.where(left, late[:HALF], late[HALF:]),
            ],
            axis=0,
        )
        held = state[:, lanes]
        carried = by_pair(grown, p) * folded(mm(c_left, right_side(halves(held))))
        mixer[:, lanes] = within + carried + skip[:, lanes] * v
        ends = halves(weighted * by_pair(ending, p))
        added = folded(mm(bt2[0], beside(ends))) + mm(bt2[1], ends[0])
        state[:, lanes] = held * by_pair(whole, p) + added


def forward_scan(vpre, spre, step_pre, vtaps, staps, bias, log_decay, skip):
    tokens, width = vpre.shape
    chunks = tokens // CHUNK
    row = lambda n: pl.BlockSpec((CHUNK, n), lambda i: (i, 0))
    fixed = lambda x: pl.BlockSpec(x.shape, lambda i: (0, 0))
    return pl.pallas_call(
        forward_kernel,
        grid=(chunks,),
        in_specs=[row(width), row(2 * STATE), row(128)]
        + [fixed(x) for x in (vtaps, staps, bias, log_decay, skip)],
        out_specs=[
            row(width), pl.BlockSpec((1, STATE, width), lambda i: (i, 0, 0)),
            row(width), row(width), row(2 * STATE), row(2 * STATE),
        ],
        out_shape=[
            jax.ShapeDtypeStruct((tokens, width), F32),
            jax.ShapeDtypeStruct((chunks, STATE, width), F32),
            jax.ShapeDtypeStruct((tokens, width), F32),
            jax.ShapeDtypeStruct((tokens, width), F32),
            jax.ShapeDtypeStruct((tokens, 2 * STATE), F32),
            jax.ShapeDtypeStruct((tokens, 2 * STATE), F32),
        ],
        scratch_shapes=[
            pltpu.VMEM((STATE, width), F32),
            pltpu.VMEM((8, width), F32),
            pltpu.VMEM((8, 2 * STATE), F32),
            pltpu.VMEM((width // 128, CHUNK + 8, 128), F32),
            pltpu.VMEM((CHUNK + 8, 2 * STATE), F32),
        ],
        compiler_params=pltpu.CompilerParams(vmem_limit_bytes=VMEM),
        cost_estimate=pl.CostEstimate(
            flops=tokens * width * 16 * 256,
            bytes_accessed=tokens * width * 20,
            transcendentals=tokens * width * 3,
        ),
        name="scan_forward",
    )(vpre, spre, step_pre, vtaps, staps, bias, log_decay, skip)


def taps_back(d_total, later, x, taps, moved):
    moved[:CHUNK, :] = d_total
    moved[CHUNK:, :] = later
    d_x = d_total * taps[CONV - 1 : CONV, :]
    rows = []
    for k in range(CONV - 1):
        later_rows = moved[3 - k : 3 - k + CHUNK, :]
        d_x = d_x + later_rows * taps[k : k + 1, :]
        rows.append(jnp.sum(later_rows * x, axis=0, keepdims=True))
    rows.append(jnp.sum(d_total * x, axis=0, keepdims=True))
    return d_x, rows + [jnp.sum(d_total, axis=0, keepdims=True)]


def backward_kernel(
    vpre, values, vslope, spre, states_ref, sslope, spre_step, vtaps, staps, bias, log_decay, skip, chooser,
    mixer, d_mixer, starts,
    values_low, d_spre, step_low, value_sums, state_sums, step_sums,
    later_grad, later_state, vhead, shead, vmoved, smoved,
):
    @pl.when(pl.program_id(0) == 0)
    def _():
        for ref in (later_grad, later_state, vhead, shead, value_sums, state_sums, step_sums):
            ref[...] = jnp.zeros_like(ref)

    states = states_ref[...]
    b, c = states[:, :STATE], states[:, STATE:]
    shifted_pre, step, rates, cum = step_terms(spre_step, bias, log_decay)
    cum_t = cum.T
    final = cum[CHUNK - 1 :, :]
    grown, ending, whole = jnp.exp(cum), jnp.exp(final - cum), jnp.exp(final)
    b2, c2 = halves(b), halves(c)
    b_left, ct2 = beside(b2), halves(c.T)
    causal = square(1) >= square(0)
    scores_t = jnp.where(causal, folded(mm_nt(b_left, right_side_nt(c2))), 0.0)
    left = lax.broadcasted_iota(jnp.int32, (1, 128), 1) < 64
    zero = jnp.zeros((CHUNK, 128), BF)
    d_early = jnp.zeros((HALF, CHUNK), F32)
    d_late = jnp.zeros((HALF, HALF), F32)
    d_b = jnp.zeros((CHUNK, STATE), F32)
    d_c = jnp.zeros((CHUNK, STATE), F32)
    by_head = jnp.zeros((2 * CHUNK, 128), F32)
    at_end = jnp.zeros((8, 128), F32)
    for p in range(vpre.shape[1] // 128):
        lanes = slice(128 * p, 128 * p + 128)
        pick = chooser[256 * p : 256 * p + 256, :]
        v, dy = values[:, lanes], d_mixer[:, lanes]
        steps = by_pair(step, p)
        weighted = v * steps
        w2, d2 = halves(weighted), halves(dy)
        w_rest = pltpu.roll(weighted - w2[0].astype(F32), 64, 1).astype(BF)
        d_top = pltpu.roll(d2[0].astype(F32), 64, 1).astype(BF)
        early, late = [], []
        for h, mine in ((2 * p, left), (2 * p + 1, ~left)):
            gap = cum_t[h : h + 1, :] - cum[:HALF, h : h + 1]
            decay_early = jnp.exp(jnp.minimum(gap, 0.0))
            gap = cum_t[h : h + 1, HALF:] - cum[HALF:, h : h + 1]
            decay_late = jnp.exp(jnp.minimum(gap, 0.0))
            early.append(decay_early * scores_t[:HALF, :])
            late.append(decay_late * scores_t[HALF:, HALF:])
            one = beside((jnp.where(mine, w2[0], w_rest), jnp.where(mine, w2[0], zero)))
            other = beside((jnp.where(mine, d2[0], d_top), jnp.where(mine, d2[1], zero)))
            d_mix = mm_nt(one, other)
            d_early = d_early + d_mix[:HALF, :] * decay_early
            d_late = d_late + d_mix[HALF:, HALF:] * decay_late
        early = halves(jnp.concatenate(early, axis=0))
        early = folded(mm(early[0], beside(d2))) + mm(early[1], d2[0])
        late = beside(halves(jnp.concatenate(late, axis=0)))
        late = folded(mm(late, right_side((d2[0][HALF:], d2[1][HALF:]))))
        within = jnp.concatenate(
            [
                jnp.where(left, early[:HALF], early[HALF:]),
                jnp.where(left, late[:HALF], late[HALF:]),
            ],
            axis=0,
        )
        held, after_here = starts[0, :, lanes], later_grad[:, lanes]
        after2 = halves(after_here)
        ends = by_pair(ending, p)
        d_weighted = within + ends * folded(mm(b_left, right_side(after2)))
        gain = skip[:, lanes]
        both = jnp.concatenate([dy * (mixer[:, lanes] - gain * v), v * d_weighted], axis=0)
        by_head = by_head + mm(beside(halves(both)), pick)
        ended = jnp.sum(after_here * later_state[:, lanes], axis=0, keepdims=True)
        at_end = at_end + mm(beside(halves(jnp.broadcast_to(ended, (8, 128)))), pick)
        faded = halves(by_pair(grown, p) * dy)
        d_c = d_c + folded(mm_nt(beside(faded), right_side_nt(halves(held))))
        d_b = d_b + folded(mm_nt(beside(halves(weighted * ends)), right_side_nt(after2)))
        added = folded(mm(ct2[0], beside(faded))) + mm(ct2[1], faded[0])
        later_grad[:, lanes] = after_here * by_pair(whole, p) + added
        d_total = (steps * d_weighted + gain * dy) * vslope[:, lanes]
        d_x, rows = taps_back(
            d_total, vhead[:, lanes], vpre[:, lanes], vtaps[:, lanes], vmoved.at[p]
        )
        values_low[:, lanes] = d_x.astype(BF)
        rows += [jnp.sum(v * dy, axis=0, keepdims=True), jnp.zeros((2, 128), F32)]
        value_sums[:, lanes] += jnp.concatenate(rows, axis=0)
        vhead[:, lanes] = d_total[:8]
    later_state[...] = starts[0]
    d_late = jnp.concatenate([jnp.zeros((HALF, HALF), F32), d_late], axis=1)
    d_scores_t = jnp.where(causal, jnp.concatenate([d_early, d_late], axis=0), 0.0)
    top, rest = halves(d_scores_t)
    d_b = d_b + folded(mm(top, beside(c2))) + mm(rest, c2[0])
    top, rest = halves(d_scores_t.T)
    d_c = d_c + folded(mm(top, beside(b2))) + mm(rest, b2[0])
    reached, pulled = by_head[:CHUNK], by_head[CHUNK:]
    last = lax.broadcasted_iota(jnp.int32, (CHUNK, 128), 0) == CHUNK - 1
    d_cum = reached - step * pulled + jnp.where(last, at_end[:1], 0.0)
    d_rate = summed_by(jnp.where(causal, 1.0, 0.0).astype(BF), d_cum)
    d_shifted = (pulled - rates * d_rate) * jax.nn.sigmoid(shifted_pre)
    step_low[...] = d_shifted.astype(BF)
    step_sums[0:1, :] += jnp.sum(d_shifted, axis=0, keepdims=True)
    step_sums[1:2, :] -= jnp.sum(d_rate * step, axis=0, keepdims=True) * rates
    d_total = beside((d_b, d_c)) * sslope[...]
    d_x, rows = taps_back(d_total, shead[...], spre[...], staps[...], smoved)
    d_spre[...] = d_x
    state_sums[...] += jnp.concatenate(rows + [jnp.zeros((3, 2 * STATE), F32)], axis=0)
    shead[...] = d_total[:8]


def backward_scan(
    vpre, values, vslope, spre, states, sslope, step_pre, vtaps, staps, bias, log_decay, skip, mixer, d_mixer,
    starts,
):
    tokens, width = vpre.shape
    chunks = tokens // CHUNK
    lane = jnp.arange(2 * width)
    heads = 2 * (lane // 256) + lane % 128 // 64
    chooser = (heads[:, None] == jnp.arange(128)[None, :]).astype(BF)
    row = lambda n: pl.BlockSpec((CHUNK, n), lambda i: (chunks - 1 - i, 0))
    fixed = lambda x: pl.BlockSpec(x.shape, lambda i: (0, 0))
    summed = lambda n: pl.BlockSpec((8, n), lambda i: (0, 0))
    return pl.pallas_call(
        backward_kernel,
        grid=(chunks,),
        in_specs=[row(width)] * 3 + [row(2 * STATE)] * 3 + [row(128)]
        + [fixed(x) for x in (vtaps, staps, bias, log_decay, skip, chooser)]
        + [row(width), row(width), pl.BlockSpec((1, STATE, width), lambda i: (chunks - 1 - i, 0, 0))],
        out_specs=[
            row(width), row(2 * STATE), row(128), summed(width), summed(2 * STATE), summed(128),
        ],
        out_shape=[
            jax.ShapeDtypeStruct((tokens, width), BF),
            jax.ShapeDtypeStruct((tokens, 2 * STATE), F32),
            jax.ShapeDtypeStruct((tokens, 128), BF),
            jax.ShapeDtypeStruct((8, width), F32),
            jax.ShapeDtypeStruct((8, 2 * STATE), F32),
            jax.ShapeDtypeStruct((8, 128), F32),
        ],
        scratch_shapes=[
            pltpu.VMEM((STATE, width), F32),
            pltpu.VMEM((STATE, width), F32),
            pltpu.VMEM((8, width), F32),
            pltpu.VMEM((8, 2 * STATE), F32),
            pltpu.VMEM((width // 128, CHUNK + 8, 128), F32),
            pltpu.VMEM((CHUNK + 8, 2 * STATE), F32),
        ],
        compiler_params=pltpu.CompilerParams(vmem_limit_bytes=VMEM),
        cost_estimate=pl.CostEstimate(
            flops=tokens * width * 40 * 256,
            bytes_accessed=tokens * width * 24,
            transcendentals=tokens * width * 3,
        ),
        name="scan_backward",
    )(
        vpre, values, vslope, spre, states, sslope, step_pre, vtaps, staps, bias, log_decay, skip, chooser,
        mixer, d_mixer, starts,
    )


def place(arrays, piece, targets, rows):
    count = sum(x.shape[0] // piece for x in arrays)
    assert count == len(targets)
    width, dtype = arrays[0].shape[1], arrays[0].dtype

    def kernel(at, *refs):
        sources, out, done = refs[: len(arrays)], refs[len(arrays)], refs[len(arrays) + 1]
        copies = []
        for source in sources:
            for j in range(source.shape[0] // piece):
                k = len(copies)
                start = pl.multiple_of(at[k], piece)
                copies.append(
                    pltpu.make_async_copy(
                        source.at[pl.ds(j * piece, piece)], out.at[pl.ds(start, piece)], done.at[k]
                    )
                )
        for copy in copies:
            copy.start()
        for copy in copies:
            copy.wait()

    return pl.pallas_call(
        kernel,
        grid_spec=pltpu.PrefetchScalarGridSpec(
            num_scalar_prefetch=1,
            grid=(1,),
            in_specs=[pl.BlockSpec(memory_space=pl.ANY)] * len(arrays),
            out_specs=pl.BlockSpec(memory_space=pltpu.VMEM),
            scratch_shapes=[pltpu.SemaphoreType.DMA((count,))],
        ),
        out_shape=jax.ShapeDtypeStruct((rows, width), dtype),
        compiler_params=pltpu.CompilerParams(vmem_limit_bytes=16 * 1024 * 1024),
        cost_estimate=pl.CostEstimate(
            flops=0, bytes_accessed=2 * rows * width * dtype.itemsize, transcendentals=0
        ),
        name="place",
    )(jnp.stack([jnp.asarray(t, jnp.int32) for t in targets]), *arrays)


def swap(x, axis, bit=1):
    return lax.ppermute(x, axis, [(i, i ^ bit) for i in range(lax.axis_size(axis))])


def turned(x, axis, distance):
    n = lax.axis_size(axis)
    return lax.ppermute(x, axis, [(i, (i + distance) % n) for i in range(n)])


def after(x, *earlier):
    return lax.optimization_barrier((x, *earlier))[0]


def at(x, index, axis):
    return lax.dynamic_index_in_dim(x, index, axis, keepdims=False)


def part(x, index, size, axis):
    return lax.dynamic_slice_in_dim(x, index * size, size, axis)


def ordered(flag, mine, other, axis):
    first = jnp.where(flag == 0, mine, other)
    second = jnp.where(flag == 0, other, mine)
    return jnp.concatenate([first, second], axis=axis)


def paired_kernel(count, core, *refs):
    lows, weights, outs = refs[:count], refs[count : 3 * count], refs[3 * count :]
    step, tiles = pl.program_id(0), pl.num_programs(0) // 2
    for j in range(2):

        @pl.when(step // tiles == j)
        def _(j=j):
            for out, which in zip(outs, (1 - core[0], core[0]), strict=True):
                total = 0.0
                for k, low in enumerate(lows):
                    block = low[:, which]
                    total = total + mm_nt(
                        block.reshape(-1, block.shape[-1]), weights[2 * k + j][...]
                    )
                out[...] = total.astype(out.dtype)


def paired_products(lows, weights, core, sub):
    tokens, n = lows[0].shape[0], weights[0][0].shape[0]
    groups = tokens // (4 * sub)
    split = [x.reshape(groups, 2, 2 * sub, x.shape[1]) for x in lows]
    tile = n
    tiles = n // tile
    outs = [jax.ShapeDtypeStruct((tokens // 2, 2 * n), dtype) for dtype in (BF, F32)]
    first = lambda i, core: (jnp.minimum(i, tiles - 1), 0)
    second = lambda i, core: (jnp.maximum(i - tiles, 0), 0)
    return pl.pallas_call(
        functools.partial(paired_kernel, len(lows)),
        grid_spec=pltpu.PrefetchScalarGridSpec(
            num_scalar_prefetch=1,
            grid=(2 * tiles,),
            in_specs=[pl.BlockSpec(x.shape, lambda i, core: (0, 0, 0, 0)) for x in split]
            + [
                pl.BlockSpec((tile, w.shape[1]), where)
                for pair in weights
                for w, where in zip(pair, (first, second), strict=True)
            ],
            out_specs=[pl.BlockSpec((tokens // 2, tile), lambda i, core: (0, i))] * 2,
        ),
        out_shape=outs,
        compiler_params=pltpu.CompilerParams(vmem_limit_bytes=26 * 1024 * 1024),
        cost_estimate=pl.CostEstimate(flops=1, bytes_accessed=1, transcendentals=0),
        name="paired_products",
    )(core[None], *split, *[w for pair in weights for w in pair])


def whole_sequences(
    block_input, output_grad, input_gain, gate_weight, value_weight, state_weight, step_weight,
    out_weight, value_taps, state_taps, step_bias, log_decay, skip_gain, mixer_gain,
):
    xi, ci, zi, yi = (lax.axis_index(n) for n in ("x", "core", "seq", "heads"))
    nz = lax.axis_size("seq")
    nx = lax.axis_size("x")
    d_model = block_input.shape[-1]
    half = d_model // 2
    group = block_input.shape[2]
    sub = group // 2
    tokens = group * nz
    own = sub * nz // 2
    rows = gate_weight.shape[0]
    cols = gate_weight.shape[1] // 2
    heads = step_weight.shape[1] // 2

    def turned_halves(x):
        return jnp.where(xi == 0, x, jnp.concatenate([x[:, half:], x[:, :half]], axis=1))

    def route(r):
        return [
            (c * nz + z, (z % 2) * nz + 2 * ((z // 2) ^ r) + c) for c in range(2) for z in range(nz)
        ]

    def tokens_in(x):
        rounds = []
        for r in range(2):
            piece = lax.dynamic_slice(x, ((zi // 2) ^ r, 0, yi * sub, 0), (1, 1, sub, d_model))
            rounds.append(lax.ppermute(piece.reshape(sub, d_model), ("core", "seq"), route(r)))
        return rounds

    def in_order(rounds):
        return turned_halves(ordered(zi // 2, *rounds, 0))

    def tokens_back(x):
        pieces = [part(x, (zi // 2) ^ r, sub, 0) for r in range(2)]
        return [
            lax.ppermute(piece, ("core", "seq"), [(b, a) for a, b in route(r)])
            for r, piece in enumerate(pieces)
        ]

    def tokens_home(mine, by_y):
        targets = [(2 * ((zi // 2) ^ r) + y) * sub for y in (yi, 1 - yi) for r in range(2)]
        return place([mine, by_y], sub, targets, 2 * group).reshape(block_input.shape)

    spread_targets = [
        ((2 * k + c) * 2 + y) * sub
        for y, c in ((yi, ci), (1 - yi, ci), (yi, 1 - ci), (1 - yi, 1 - ci))
        for k in range(nz // 2)
    ]

    def spread(x, by_y=None):
        by_y = swap(x, "heads") if by_y is None else by_y
        by_core = swap(x, "core")
        by_both = swap(by_y, "core")
        return place([x, by_y, by_core, by_both], sub, spread_targets, tokens)

    def of_core(x, core):
        return at(x.reshape(nz // 2, 2, 2 * sub, -1), core, 1).reshape(tokens // 2, -1)

    def over_core(send, keep, link=BF):
        return core_sum(swap(send, "core"), keep, link)

    def core_sum(received, keep, link=BF):
        received = received.reshape(nz // 2, 2, sub, keep.shape[1]).astype(F32)
        keep = keep.reshape(received.shape)
        goes = (at(keep, 1 - yi, 1) + at(received, 1 - yi, 1)).astype(link)
        return at(keep, yi, 1) + at(received, yi, 1), goes

    def over_y(stays, received):
        return (stays + received.astype(F32)).reshape(own, -1)

    def block_of(weight):
        width = weight.shape[1] // 2
        received = swap(part(weight, 1 - ci, width, 1), "core")
        return ordered(ci, part(weight, ci, width, 1), received, 0)

    def ring(block, *earlier):
        right = turned(block, "seq", 1)
        left = turned(block, "seq", -1)
        return [block, right, left, turned(after(right, left, *earlier), "seq", 1)]

    def stacked(blocks):
        targets = [
            (c * nz + z % nz) * rows for z in (zi, zi + nz - 1, zi + 1, zi + 2) for c in range(2)
        ]
        return place(blocks, rows, targets, half)

    def products(low, features):
        return transposed(features[:, half:], low).astype(BF), transposed(features[:, :half], low)

    def over_x(kept, received):
        return (kept + received.astype(F32)).reshape(2, nz, rows, -1)

    def by_parity(summed, which):
        shape = summed.shape
        split = summed.reshape(*shape[:-3], nz // 2, 2, *shape[-2:])
        return at(split, which, split.ndim - 3)

    def first_pieces(summed):
        return by_parity(summed, 1 - zi % 2).astype(BF)

    def first_sum(summed, received):
        return by_parity(summed, zi % 2) + received.astype(F32)

    def second_pieces(summed):
        return at(summed, 1 - zi // 2, -3).astype(BF)

    def over_z(summed, received):
        return at(summed, zi // 2, -3) + received.astype(F32)

    def to_core(total):
        received = swap(at(total, 1 - ci, 0), "core")
        return at(total, ci, 0), received

    project = lambda a, b: jnp.dot(a, b, preferred_element_type=F32)
    transposed = lambda a, b: lax.dot_general(
        a, b, (((0,), (0,)), ((), ())), preferred_element_type=F32
    )
    back = lambda a, b: lax.dot_general(a, b, (((1,), (1,)), ((), ())), preferred_element_type=F32)

    pad = 128 - heads
    first = jnp.concatenate(
        [
            jnp.concatenate(
                [
                    value_weight[:, cols * k : cols * k + cols],
                    state_weight[:, STATE * k : STATE * k + STATE],
                    step_weight[:, heads * k : heads * k + heads],
                    jnp.broadcast_to(input_gain[:, None], (rows, pad)),
                ],
                axis=1,
            )
            for k in range(2)
        ],
        axis=1,
    )
    first_block = block_of(first)
    first_across = [swap(first_block, "x")]
    first_ring = ring(first_block, *first_across)
    first_across += [swap(x, "x") for x in first_ring[1:]]

    x_own = in_order(tokens_in(block_input))

    pair_weight = after(
        jnp.concatenate(
            [gate_weight[:, :cols], out_weight[:cols].T, gate_weight[:, cols:], out_weight[cols:].T],
            axis=1,
        ),
        first_block,
    )
    pair_block = block_of(pair_weight)
    pair_across = [swap(after(pair_block, first_across[0]), "x")]
    x_all = spread(after(x_own, *pair_across))
    pair_ring = ring(after(pair_block, first_ring[3]))
    pair_across += [swap(after(x, first_across[3]), "x") for x in pair_ring[1:3]] + [None]

    first_own = stacked(first_ring)
    first_other = stacked(first_across)
    def both_halves(a, w_own, w_other):
        return project(a[:, :half], w_own) + project(a[:, half:], w_other)

    split = lambda w: (w[:, :cols], w[:, cols : cols + STATE], w[:, cols + STATE :])
    value_own, state_own, step_own = split(first_own)
    value_other, state_other, step_other = split(first_other)
    gain = jnp.concatenate([step_own[:, -1], step_other[:, -1]])[None].astype(F32)
    blank = jnp.arange(128)[None, :] < heads
    step_own, step_other = jnp.where(blank, step_own, 0), jnp.where(blank, step_other, 0)

    x_wide = x_all.astype(F32)
    normed = (
        x_wide * lax.rsqrt(jnp.mean(x_wide * x_wide, axis=-1, keepdims=True) + EPS) * gain
    ).astype(BF)
    x_own = x_own.astype(F32)
    scaling = lax.rsqrt(jnp.mean(x_own * x_own, axis=-1, keepdims=True) + EPS)

    states_weights = jnp.concatenate([state_own, state_other], axis=0)
    states_received = swap(states_weights, "core")
    states_half = both_halves(normed, state_own, state_other)
    states_pre = ordered(ci, states_half, swap(states_half, "core"), 1)
    values_pre = both_halves(normed, value_own, value_other)
    step_pre = both_halves(normed, step_own, step_other)

    vtaps = part(value_taps, ci, cols, 1)
    lanes = lambda v: jnp.pad(part(v, ci, heads, 0), (0, pad))[None]
    bias, decays = lanes(step_bias), lanes(log_decay)
    skip = jnp.repeat(part(skip_gain, ci, heads, 0), cols // heads)[None]
    gain_mixer = part(mixer_gain, ci, cols, 0)[None]
    og_rounds = tokens_in(after(output_grad, pair_ring[1], pair_ring[2]))
    values_pre, states_received, *pair_across[1:3], pair_ring[3], og_rounds = lax.optimization_barrier(
        (values_pre, states_received, *pair_across[1:3], pair_ring[3], og_rounds)
    )
    og_own = in_order(og_rounds)
    og_own, values_pre = lax.optimization_barrier((og_own, values_pre))
    mixer, starts, *kept = forward_scan(
        values_pre, states_pre, step_pre, vtaps, state_taps, bias, decays, skip
    )
    pair_across[3], og_by_y, mixer = lax.optimization_barrier(
        (swap(pair_ring[3], "x"), swap(og_own, "heads"), mixer)
    )
    og = spread(og_own, og_by_y)
    pair_own = stacked(pair_ring)
    pair_other = stacked(pair_across)
    gate_own, out_own = pair_own[:, :cols], pair_own[:, cols:]
    gate_other, out_other = pair_other[:, :cols], pair_other[:, cols:]
    gate_lin = both_halves(normed, gate_own, gate_other)
    d_out = both_halves(og, out_own, out_other)
    sigmoid_gate = jax.nn.sigmoid(gate_lin)
    silu_gate = gate_lin * sigmoid_gate
    gated = mixer * silu_gate
    weighted = d_out * gain_mixer
    sums = jnp.stack([jnp.sum(gated * gated, axis=1), jnp.sum(weighted * gated, axis=1)])
    sums = sums + swap(sums, "core")
    sums = sums + swap(sums, "heads")
    inverse = lax.rsqrt(sums[0] / INNER + EPS)[:, None]
    out_normed = (gated * inverse * gain_mixer).astype(BF)
    d_gated = inverse * weighted - gated * (inverse * inverse * inverse) * (sums[1][:, None] / INNER)
    d_mixer = d_gated * silu_gate
    gate_low = (d_gated * mixer * sigmoid_gate * (1.0 + gate_lin * (1.0 - sigmoid_gate))).astype(BF)
    g_mixer_gain = jnp.sum(d_out * gated * inverse, axis=0)

    out_sum = jnp.stack(
        [transposed(og[:, :half], out_normed), transposed(og[:, half:], out_normed)]
    ).reshape(2, 2, nz, rows, cols)
    out_pieces = first_pieces(out_sum)
    branch_sends, branch_keeps = paired_products(
        [after(out_normed, out_pieces)], [(out_own, out_other)], ci, sub
    )
    gate_sends, gate_keeps = products(after(gate_low, branch_sends), normed)
    branch_stays, branch_goes = over_core(branch_sends, branch_keeps)
    d_mixer = after(d_mixer, out_pieces, gate_sends, branch_goes)
    scanned = backward_scan(
        values_pre, *kept[:2], states_pre, *kept[2:], step_pre, vtaps, state_taps, bias, decays, skip,
        mixer, d_mixer, starts,
    )
    sent = (swap(out_pieces, "seq", 1), swap(gate_sends, "x"), swap(branch_goes, "heads"))
    sent, scanned = lax.optimization_barrier((sent, scanned))
    out_received, gate_received, branch_received = sent
    values_low, d_states, step_low, value_sums, state_sums, step_sums = scanned

    out_sum = first_sum(out_sum, out_received)
    out_pieces = second_pieces(out_sum)
    value_sends, value_keeps = products(after(values_low, out_pieces), normed)
    gate_sum = over_x(after(gate_keeps, value_sends), gate_received)
    gate_pieces = first_pieces(gate_sum)
    d_states = after(d_states, gate_pieces)
    states_stay, states_go = over_core(of_core(d_states, 1 - ci), of_core(d_states, ci), F32)
    dn_sends, dn_keeps = paired_products(
        [after(gate_low, value_sends, states_go), values_low, step_low],
        [(gate_own, gate_other), (value_own, value_other), (step_own, step_other)],
        ci,
        sub,
    )
    states_low = over_y(states_stay, swap(states_go, "heads")).astype(BF)
    dn_sends = after(dn_sends, states_low)
    states_by_y = swap(states_low, "heads")
    states_by_core = swap(after(states_low, states_by_y), "core")
    states_by_both = swap(after(states_by_y, states_by_core), "core")
    states_all = place(
        [x.astype(F32) for x in (states_low, states_by_y, states_by_core, states_by_both)],
        sub,
        spread_targets,
        tokens,
    ).astype(BF)
    parts = [
        products(part(states_all, ci, STATE, 1), normed),
        products(step_low, normed),
    ]
    small_sends, small_keeps = (jnp.concatenate(p, axis=1) for p in zip(*parts, strict=True))
    branch = over_y(branch_stays, after(branch_received, dn_sends))
    output_rows = turned_halves((x_own + branch).astype(BF))
    (
        value_received, gate_received, small_sends, dn_received, dn_keeps, out_received, output_rows
    ) = lax.optimization_barrier(
        (
            swap(value_sends, "x"), swap(gate_pieces, "seq", 1), small_sends,
            swap(dn_sends, "core"), dn_keeps, swap(out_pieces, "seq", 2), output_rows,
        )
    )

    dn_stays, dn_goes = core_sum(dn_received, dn_keeps)
    output_sent = tokens_back(output_rows)
    gate_sum = first_sum(after(gate_sum, dn_goes), gate_received)
    gate_pieces = second_pieces(gate_sum)
    value_sum = over_x(after(value_keeps, dn_goes), value_received)
    value_pieces = first_pieces(value_sum)
    states_weights = ordered(ci, states_weights, states_received, 1)
    dn_received, output_sent, value_received, small_received = lax.optimization_barrier(
        (
            swap(dn_goes, "heads"), output_sent, swap(value_pieces, "seq", 1), swap(small_sends, "x"),
        )
    )

    d_normed = over_y(dn_stays, dn_received) + back(states_low, states_weights)
    pushed = d_normed * gain
    d_tokens = scaling * pushed - x_own * (scaling * scaling * scaling) * jnp.mean(
        pushed * x_own, axis=-1, keepdims=True
    )
    input_rows = turned_halves((og_own.astype(F32) + d_tokens).astype(BF))
    g_input_gain = turned_halves(jnp.sum(d_normed * x_own * scaling, axis=0)[None])
    per_core = jnp.concatenate(
        [value_sums[:6], g_mixer_gain[None], jnp.pad(step_sums[:2].reshape(1, -1), ((0, 0), (0, cols - 256)))],
        axis=0,
    ).reshape(-1, 256)
    shared = jnp.concatenate([state_sums, g_input_gain.reshape(-1, 256)], axis=0)
    shared = shared + swap(shared, "heads")
    received = swap(jnp.concatenate([per_core, shared], axis=0), "core")
    n_core = per_core.shape[0]
    pack = jnp.concatenate(
        [ordered(ci, per_core, received[:n_core], 0), shared + received[n_core:]], axis=0
    )
    output_sent = jnp.concatenate(after(output_sent, shared), axis=0)
    small_sum = over_x(small_keeps, after(small_received, input_rows))
    small_sum = first_sum(small_sum, swap(first_pieces(small_sum), "seq", 1))
    small_pieces = second_pieces(small_sum)
    input_sent, output_by_y, gate_received, small_pieces, pack = lax.optimization_barrier(
        (
            tokens_back(input_rows), swap(output_sent, "heads"), swap(gate_pieces, "seq", 2),
            small_pieces, pack,
        )
    )

    input_sent = jnp.concatenate(input_sent, axis=0)
    value_sum = first_sum(value_sum, value_received)
    value_pieces = second_pieces(value_sum)
    g_out = over_z(out_sum, out_received)
    pack = pack + swap(pack, "x")
    pack = pack + swap(pack, "seq", 1)
    g_out = g_out[0] + swap(g_out[1].astype(BF), "x").astype(F32)
    out_mine, out_received = to_core(g_out)
    input_by_y, value_received, small_received, out_received, pack = lax.optimization_barrier(
        (
            swap(input_sent, "heads"), swap(value_pieces, "seq", 2), swap(small_pieces, "seq", 2),
            out_received, pack,
        )
    )
    pack = pack + swap(pack, "seq", 2)
    g_gate = over_z(gate_sum, gate_received)
    g_value = over_z(value_sum, value_received)
    g_small = over_z(small_sum, small_received)
    block_output = tokens_home(output_sent, output_by_y)
    grad_input = tokens_home(input_sent, input_by_y)

    both, shared = pack[: 2 * n_core].reshape(2, 8, cols), pack[2 * n_core :]
    by_channel = jnp.transpose(both, (1, 0, 2)).reshape(8, 2 * cols)
    per_head = both[:, 7, :256].reshape(2, 2, 128)[:, :, :heads]
    input_gain_all = shared[8:].reshape(nx, 2, nz, rows)
    my_gain = at(at(at(input_gain_all, xi, 0), ci, 0), zi, 0)

    def widths(mine, received):
        return ordered(ci, mine, received, 1)

    small_mine, small_received = to_core(g_small)
    steps_at = slice(STATE, STATE + heads)
    return (
        block_output,
        grad_input,
        my_gain,
        widths(*to_core(g_gate)),
        widths(*to_core(g_value)),
        widths(small_mine[:, :STATE], small_received[:, :STATE]),
        widths(small_mine[:, steps_at], small_received[:, steps_at]),
        widths(out_mine, out_received).T,
        by_channel[:5],
        shared[:5],
        per_head[:, 0].reshape(-1),
        per_head[:, 1].reshape(-1),
        jnp.sum(by_channel[5].reshape(2 * heads, -1), axis=1),
        by_channel[6],
    )


def solution(mesh):
    sizes = dict(mesh.shape)
    if sizes["seq"] == 2 * MB and sizes["dp"] == 4 and sizes["heads"] == 2:
        devices = mesh.devices.reshape(sizes["dp"] // 2, 2, sizes["seq"], sizes["heads"])
        mesh = jax.sharding.Mesh(devices, ("x", "core", "seq", "heads"))
        body, dp = whole_sequences, ("x", "core")
    else:
        body, dp = shards, ("dp",)
    tokens = P(None, dp, "seq", None)
    both = (*dp, "seq")
    return jax.shard_map(
        body,
        mesh=mesh,
        in_specs=(
            tokens,
            tokens,
            P(both),
            P(both, "heads"),
            P(both, "heads"),
            P(both, None),
            P(both, "heads"),
            P("heads", both),
            P(None, "heads"),
            P(),
            P("heads"),
            P("heads"),
            P("heads"),
            P("heads"),
        ),
        out_specs=(
            tokens,
            tokens,
            P(both),
            P(both, "heads"),
            P(both, "heads"),
            P(both, None),
            P(both, "heads"),
            P("heads", both),
            P(None, "heads"),
            P(),
            P("heads"),
            P("heads"),
            P("heads"),
            P("heads"),
        ),
        check_vma=False,
    )
```

```python
import functools

import jax
import jax.numpy as jnp
from jax import lax
from jax.experimental import pallas as pl
from jax.experimental.pallas import tpu as pltpu
from jax.sharding import PartitionSpec as P

STATE = 128
CONV = 4
MB = 2
INNER = 3072


EPS = 1e-05
HIGH = lax.Precision.HIGHEST


def shifted(block, axis, distance):
    devices = range(lax.axis_size(axis))
    route = [(i - distance, i) for i in devices if i - distance in devices]
    return lax.ppermute(block, axis, route)


def entering(x, axis, combine, identity, reverse):
    peers, index = (lax.axis_size(axis), lax.axis_index(axis))
    everything = jax.tree.map(lambda part: lax.all_gather(part, axis), x)
    start = jax.tree.map(
        lambda part, zero: jnp.broadcast_to(jnp.asarray(zero, part.dtype), part.shape), x, identity
    )

    def step(k, before):
        at = peers - 1 - k if reverse else k
        reached = at > index if reverse else at < index
        new = combine(before, jax.tree.map(lambda part: part[at], everything))
        return jax.tree.map(lambda a, b: jnp.where(reached, a, b), new, before)

    return lax.fori_loop(0, peers, step, start)


def norm_rows(values, gain):
    return values * lax.rsqrt(jnp.mean(values * values, axis=-1, keepdims=True) + EPS) * gain


def conv_silu(extended, taps):
    length = extended.shape[1] - (CONV - 1)
    total = jnp.zeros((extended.shape[0], length, extended.shape[2]), jnp.float32) + taps[CONV]
    for offset in range(CONV):
        total = total + extended[:, offset : offset + length] * taps[offset]
    return jax.nn.silu(total)


def local_parts(
    values_ext, states_ext, step_pre, value_taps, state_taps, step_bias, log_decay, skip_gain
):
    values_conv = conv_silu(values_ext, value_taps)
    states_conv = conv_silu(states_ext, state_taps)
    batch, length, channels = values_conv.shape
    heads_here = step_pre.shape[-1]
    values = values_conv.reshape(batch, length, heads_here, channels // heads_here)
    input_mat = states_conv[..., :STATE]
    output_mat = states_conv[..., STATE:]
    stepsize = jax.nn.softplus(step_pre + step_bias)
    cumulative = jnp.cumsum(-stepsize * jnp.exp(log_decay), axis=1)
    gaps = cumulative[:, :, None, :] - cumulative[:, None, :, :]
    causal = (jnp.arange(length)[:, None] >= jnp.arange(length)[None, :])[None, :, :, None]
    decays = jnp.where(causal, jnp.exp(jnp.where(causal, gaps, 0.0)), 0.0)
    scores = jnp.einsum("btn,bsn->bts", output_mat, input_mat, precision=HIGH)
    weights = decays * scores[..., None] * stepsize[:, None, :, :]
    within = (
        jnp.einsum("btsh,bshp->bthp", weights, values, precision=HIGH) + skip_gain[:, None] * values
    )
    final = cumulative[:, -1]
    ending = jnp.exp(final[:, None, :] - cumulative) * stepsize
    local_state = jnp.einsum("bth,btn,bthp->bhnp", ending, input_mat, values, precision=HIGH)
    return (within, local_state, jnp.exp(final), cumulative, output_mat)


def carried_part(cumulative, output_mat, state_in):
    return jnp.exp(cumulative)[..., None] * jnp.einsum(
        "btn,bhnp->bthp", output_mat, state_in, precision=HIGH
    )


def whole_block(
    values_ext,
    states_ext,
    step_pre,
    value_taps,
    state_taps,
    step_bias,
    log_decay,
    skip_gain,
    state_in,
):
    within, local_state, span_decay, cumulative, output_mat = local_parts(
        values_ext, states_ext, step_pre, value_taps, state_taps, step_bias, log_decay, skip_gain
    )
    result = within + carried_part(cumulative, output_mat, state_in)
    return (result.reshape(result.shape[0], result.shape[1], -1), local_state, span_decay)


def compose(earlier, later):
    return (earlier[0] * later[0], later[0][..., None, None] * earlier[1] + later[1])


def shards(
    block_input,
    output_grad,
    input_gain,
    gate_weight,
    value_weight,
    state_weight,
    step_weight,
    out_weight,
    value_taps,
    state_taps,
    step_bias,
    log_decay,
    skip_gain,
    mixer_gain,
):
    margin = CONV - 1
    width = block_input.shape[-1]
    inner_here = gate_weight.shape[1]
    state_cols = state_weight.shape[1]
    heads_here = step_weight.shape[1]
    acc_gain = jnp.zeros((width,), jnp.float32)
    acc_gate = jnp.zeros((width, inner_here), jnp.float32)
    acc_value = jnp.zeros((width, inner_here), jnp.float32)
    acc_state = jnp.zeros((width, state_cols), jnp.float32)
    acc_step = jnp.zeros((width, heads_here), jnp.float32)
    acc_out = jnp.zeros((inner_here, width), jnp.float32)
    acc_value_taps = jnp.zeros_like(value_taps)
    acc_state_taps = jnp.zeros_like(state_taps)
    acc_step_bias = jnp.zeros_like(step_bias)
    acc_log_decay = jnp.zeros_like(log_decay)
    acc_skip = jnp.zeros_like(skip_gain)
    acc_mixer_gain = jnp.zeros_like(mixer_gain)
    outputs = []
    input_grads = []
    for micro_batch in range(MB):
        weights_now = (
            lax.all_gather(input_gain, ("dp", "seq"), axis=0, tiled=True),
            lax.all_gather(gate_weight, ("dp", "seq"), axis=0, tiled=True),
            lax.all_gather(value_weight, ("dp", "seq"), axis=0, tiled=True),
            lax.all_gather(state_weight, ("dp", "seq"), axis=0, tiled=True),
            lax.all_gather(step_weight, ("dp", "seq"), axis=0, tiled=True),
            lax.all_gather(out_weight, ("dp", "seq"), axis=1, tiled=True),
        )
        gain_full, gate_full, value_full, state_full, step_full, out_full = weights_now
        tokens = block_input[micro_batch].astype(jnp.float32)
        normed = norm_rows(tokens, gain_full.astype(jnp.float32)).astype(jnp.bfloat16)
        gate_lin = jnp.einsum("btd,di->bti", normed, gate_full, preferred_element_type=jnp.float32)
        values_pre = jnp.einsum(
            "btd,di->bti", normed, value_full, preferred_element_type=jnp.float32
        )
        states_pre = jnp.einsum(
            "btd,di->bti", normed, state_full, preferred_element_type=jnp.float32
        )
        step_pre = jnp.einsum("btd,di->bti", normed, step_full, preferred_element_type=jnp.float32)
        outgoing = jnp.concatenate([values_pre[:, -margin:], states_pre[:, -margin:]], axis=2)
        incoming = shifted(outgoing, "seq", 1)
        values_ext = jnp.concatenate([incoming[..., :inner_here], values_pre], axis=1)
        states_ext = jnp.concatenate([incoming[..., inner_here:], states_pre], axis=1)
        within, local_state, span_decay, cumulative, output_mat = local_parts(
            values_ext,
            states_ext,
            step_pre,
            value_taps,
            state_taps,
            step_bias,
            log_decay,
            skip_gain,
        )
        prefix = entering(
            (span_decay, local_state),
            "seq",
            compose,
            (jnp.ones_like(span_decay), jnp.zeros_like(local_state)),
            False,
        )
        state_in = prefix[1]
        mixer = (within + carried_part(cumulative, output_mat, state_in)).reshape(gate_lin.shape)
        silu_gate = jax.nn.silu(gate_lin)
        gated = mixer * silu_gate
        total_sq = lax.psum(jnp.sum(gated * gated, axis=-1), "heads")
        inverse = lax.rsqrt(total_sq / INNER + EPS)[..., None]
        out_normed = (gated * inverse * mixer_gain).astype(jnp.bfloat16)
        partial_out = jnp.einsum(
            "bti,id->btd", out_normed, out_full, preferred_element_type=jnp.float32
        )
        branch = lax.psum(partial_out, "heads")
        outputs.append((tokens + branch).astype(jnp.bfloat16))
        weights_back = (
            lax.all_gather(input_gain, ("dp", "seq"), axis=0, tiled=True),
            lax.all_gather(gate_weight, ("dp", "seq"), axis=0, tiled=True),
            lax.all_gather(value_weight, ("dp", "seq"), axis=0, tiled=True),
            lax.all_gather(state_weight, ("dp", "seq"), axis=0, tiled=True),
            lax.all_gather(step_weight, ("dp", "seq"), axis=0, tiled=True),
            lax.all_gather(out_weight, ("dp", "seq"), axis=1, tiled=True),
        )
        gain_full, gate_full, value_full, state_full, step_full, out_full = weights_back
        grad_out = output_grad[micro_batch]
        d_out_normed = jnp.einsum(
            "btd,id->bti", grad_out, out_full, preferred_element_type=jnp.float32
        )
        acc_out = acc_out + jnp.einsum(
            "bti,btd->id", out_normed, grad_out, preferred_element_type=jnp.float32
        )
        acc_mixer_gain = acc_mixer_gain + jnp.sum(d_out_normed * gated * inverse, axis=(0, 1))
        weighted = d_out_normed * mixer_gain
        dot_total = lax.psum(jnp.sum(weighted * gated, axis=-1), "heads")
        d_gated = inverse * weighted - gated * (inverse * inverse * inverse) * (
            dot_total[..., None] / INNER
        )
        d_mixer = d_gated * silu_gate
        sigmoid_gate = jax.nn.sigmoid(gate_lin)
        d_gate_lin = d_gated * mixer * sigmoid_gate * (1.0 + gate_lin * (1.0 - sigmoid_gate))
        carry_grad = jnp.einsum(
            "bth,btn,bthp->bhnp",
            jnp.exp(cumulative),
            output_mat,
            d_mixer.reshape(within.shape),
            precision=HIGH,
        )
        suffix = entering(
            (span_decay, carry_grad),
            "seq",
            compose,
            (jnp.ones_like(span_decay), jnp.zeros_like(carry_grad)),
            True,
        )
        later_grad = suffix[1]
        d_decay = jnp.sum(later_grad * state_in, axis=(2, 3))
        ignored, pullback = jax.vjp(
            whole_block,
            values_ext,
            states_ext,
            step_pre,
            value_taps,
            state_taps,
            step_bias,
            log_decay,
            skip_gain,
            state_in,
        )
        (
            d_values_ext,
            d_states_ext,
            d_step_pre,
            g_value_taps,
            g_state_taps,
            g_step_bias,
            g_log_decay,
            g_skip,
            unused_state,
        ) = pullback((d_mixer, later_grad, d_decay))
        rim_grads = jnp.concatenate([d_values_ext[:, :margin], d_states_ext[:, :margin]], axis=2)
        returned = shifted(rim_grads, "seq", -1)
        d_values_pre = d_values_ext[:, margin:].at[:, -margin:].add(returned[..., :inner_here])
        d_states_pre = d_states_ext[:, margin:].at[:, -margin:].add(returned[..., inner_here:])
        gate_low = d_gate_lin.astype(jnp.bfloat16)
        values_low = d_values_pre.astype(jnp.bfloat16)
        step_low = d_step_pre.astype(jnp.bfloat16)
        d_normed_part = (
            jnp.einsum("bti,di->btd", gate_low, gate_full, preferred_element_type=jnp.float32)
            + jnp.einsum("bti,di->btd", values_low, value_full, preferred_element_type=jnp.float32)
            + jnp.einsum("bti,di->btd", step_low, step_full, preferred_element_type=jnp.float32)
        )
        d_normed_sum, d_states_total, state_taps_total = lax.psum(
            (d_normed_part, d_states_pre, g_state_taps), "heads"
        )
        states_low = d_states_total.astype(jnp.bfloat16)
        d_normed = d_normed_sum + jnp.einsum(
            "bti,di->btd", states_low, state_full, preferred_element_type=jnp.float32
        )
        acc_gate = acc_gate + jnp.einsum(
            "btd,bti->di", normed, gate_low, preferred_element_type=jnp.float32
        )
        acc_value = acc_value + jnp.einsum(
            "btd,bti->di", normed, values_low, preferred_element_type=jnp.float32
        )
        acc_state = acc_state + jnp.einsum(
            "btd,bti->di", normed, states_low, preferred_element_type=jnp.float32
        )
        acc_step = acc_step + jnp.einsum(
            "btd,bti->di", normed, step_low, preferred_element_type=jnp.float32
        )
        scaling = lax.rsqrt(jnp.mean(tokens * tokens, axis=-1, keepdims=True) + EPS)
        acc_gain = acc_gain + jnp.sum(d_normed * tokens * scaling, axis=(0, 1))
        pushed = d_normed * gain_full.astype(jnp.float32)
        d_tokens = scaling * pushed - tokens * (scaling * scaling * scaling) * jnp.mean(
            pushed * tokens, axis=-1, keepdims=True
        )
        input_grads.append((grad_out.astype(jnp.float32) + d_tokens).astype(jnp.bfloat16))
        acc_value_taps = acc_value_taps + g_value_taps
        acc_state_taps = acc_state_taps + state_taps_total
        acc_step_bias = acc_step_bias + g_step_bias
        acc_log_decay = acc_log_decay + g_log_decay
        acc_skip = acc_skip + g_skip
    summed = (
        lax.psum_scatter(acc_gain, ("dp", "seq"), scatter_dimension=0, tiled=True),
        lax.psum_scatter(acc_gate, ("dp", "seq"), scatter_dimension=0, tiled=True),
        lax.psum_scatter(acc_value, ("dp", "seq"), scatter_dimension=0, tiled=True),
        lax.psum_scatter(acc_state, ("dp", "seq"), scatter_dimension=0, tiled=True),
        lax.psum_scatter(acc_step, ("dp", "seq"), scatter_dimension=0, tiled=True),
        lax.psum_scatter(acc_out, ("dp", "seq"), scatter_dimension=1, tiled=True),
    )
    smalls = lax.psum(
        (acc_value_taps, acc_state_taps, acc_step_bias, acc_log_decay, acc_skip, acc_mixer_gain),
        ("dp", "seq"),
    )
    return (
        jnp.stack(outputs),
        jnp.stack(input_grads),
        summed[0],
        summed[1],
        summed[2],
        summed[3],
        summed[4],
        summed[5],
        smalls[0],
        smalls[1],
        smalls[2],
        smalls[3],
        smalls[4],
        smalls[5],
    )


BF = jnp.bfloat16
F32 = jnp.float32
CHUNK = 256
HALF = 128
VMEM = 18 * 1024 * 1024


def halves(x):
    top = x.astype(BF)
    return top, (x - top.astype(F32)).astype(BF)


def mm(a, b):
    return lax.dot_general(a, b, (((1,), (0,)), ((), ())), preferred_element_type=F32)


def mm_nt(a, b):
    return lax.dot_general(a, b, (((1,), (1,)), ((), ())), preferred_element_type=F32)


def beside(pair):
    return jnp.concatenate(pair, axis=1)


def right_side(b):
    top, rest = b
    return jnp.concatenate([beside((top, rest)), beside((top, jnp.zeros_like(top)))], axis=0)


def right_side_nt(b):
    top, rest = b
    return jnp.concatenate([beside((top, top)), beside((rest, jnp.zeros_like(top)))], axis=0)


def folded(wide):
    n = wide.shape[1] // 2
    return wide[:, :n] + wide[:, n:]


def softplus(x):
    return jnp.maximum(x, 0.0) + jnp.log1p(jnp.exp(-jnp.abs(x)))


def taps_applied(x, before, taps, moved):
    moved[:8, :] = before
    moved[8:, :] = x
    total = taps[CONV : CONV + 1, :]
    for k in range(CONV - 1):
        total = total + moved[5 + k : 5 + k + CHUNK, :] * taps[k : k + 1, :]
    return total + x * taps[CONV - 1 : CONV, :]


def summed_by(ones, x):
    top, rest = halves(x)
    low = x - top.astype(F32) - rest.astype(F32)
    return folded(mm(ones, beside((top, rest)))) + mm(ones, low.astype(BF))


def square(which):
    return lax.broadcasted_iota(jnp.int32, (CHUNK, CHUNK), which)


def step_terms(step_ref, bias_ref, log_decay_ref):
    shifted_pre = step_ref[...] + bias_ref[...]
    step = softplus(shifted_pre)
    rates = jnp.exp(log_decay_ref[...])
    cum = summed_by(jnp.where(square(0) >= square(1), 1.0, 0.0).astype(BF), -step * rates)
    return shifted_pre, step, rates, cum


def by_pair(q, p):
    left = lax.broadcasted_iota(jnp.int32, (1, 128), 1) < 64
    return jnp.where(left, q[:, 2 * p : 2 * p + 1], q[:, 2 * p + 1 : 2 * p + 2])


def forward_kernel(
    vpre, spre, spre_step, vtaps, staps, bias, log_decay, skip,
    mixer, starts, values, vslope, states_ref, sslope, state, vtail, stail, vmoved, smoved,
):
    @pl.when(pl.program_id(0) == 0)
    def _():
        state[...] = jnp.zeros_like(state)
        vtail[...] = jnp.zeros_like(vtail)
        stail[...] = jnp.zeros_like(stail)

    sx = spre[...]
    total = taps_applied(sx, stail[...], staps[...], smoved)
    sigmoid = jax.nn.sigmoid(total)
    states = total * sigmoid
    states_ref[...] = states
    sslope[...] = sigmoid * (1.0 + total * (1.0 - sigmoid))
    stail[...] = sx[CHUNK - 8 :]
    b, c = states[:, :STATE], states[:, STATE:]
    shifted_pre, step, rates, cum = step_terms(spre_step, bias, log_decay)
    cum_t = cum.T
    final = cum[CHUNK - 1 :, :]
    grown, ending, whole = jnp.exp(cum), jnp.exp(final - cum), jnp.exp(final)
    c_left, bt2 = beside(halves(c)), halves(b.T)
    scores = folded(mm_nt(c_left, right_side_nt(halves(b))))
    scores = jnp.where(square(0) >= square(1), scores, 0.0)
    left = lax.broadcasted_iota(jnp.int32, (1, 128), 1) < 64
    starts[0] = state[...]
    for p in range(vpre.shape[1] // 128):
        lanes = slice(128 * p, 128 * p + 128)
        vx = vpre[:, lanes]
        total = taps_applied(vx, vtail[:, lanes], vtaps[:, lanes], vmoved.at[p])
        vtail[:, lanes] = vx[CHUNK - 8 :]
        sigmoid = jax.nn.sigmoid(total)
        v = total * sigmoid
        values[:, lanes] = v
        vslope[:, lanes] = sigmoid * (1.0 + total * (1.0 - sigmoid))
        weighted = v * by_pair(step, p)
        w2 = halves(weighted)
        early, late = [], []
        for h in (2 * p, 2 * p + 1):
            gap = cum[:HALF, h : h + 1] - cum_t[h : h + 1, :HALF]
            early.append(jnp.exp(jnp.minimum(gap, 0.0)) * scores[:HALF, :HALF])
            gap = cum[HALF:, h : h + 1] - cum_t[h : h + 1, :]
            late.append(jnp.exp(jnp.minimum(gap, 0.0)) * scores[HALF:, :])
        early = beside(halves(jnp.concatenate(early, axis=0)))
        early = folded(mm(early, right_side((w2[0][:HALF], w2[1][:HALF]))))
        late = halves(jnp.concatenate(late, axis=0))
        late = folded(mm(late[0], beside(w2))) + mm(late[1], w2[0])
        within = jnp.concatenate(
            [
                jnp.where(left, early[:HALF], early[HALF:]),
                jnp.where(left, late[:HALF], late[HALF:]),
            ],
            axis=0,
        )
        held = state[:, lanes]
        carried = by_pair(grown, p) * folded(mm(c_left, right_side(halves(held))))
        mixer[:, lanes] = within + carried + skip[:, lanes] * v
        ends = halves(weighted * by_pair(ending, p))
        added = folded(mm(bt2[0], beside(ends))) + mm(bt2[1], ends[0])
        state[:, lanes] = held * by_pair(whole, p) + added


def forward_scan(vpre, spre, step_pre, vtaps, staps, bias, log_decay, skip):
    tokens, width = vpre.shape
    chunks = tokens // CHUNK
    row = lambda n: pl.BlockSpec((CHUNK, n), lambda i: (i, 0))
    fixed = lambda x: pl.BlockSpec(x.shape, lambda i: (0, 0))
    return pl.pallas_call(
        forward_kernel,
        grid=(chunks,),
        in_specs=[row(width), row(2 * STATE), row(128)]
        + [fixed(x) for x in (vtaps, staps, bias, log_decay, skip)],
        out_specs=[
            row(width), pl.BlockSpec((1, STATE, width), lambda i: (i, 0, 0)),
            row(width), row(width), row(2 * STATE), row(2 * STATE),
        ],
        out_shape=[
            jax.ShapeDtypeStruct((tokens, width), F32),
            jax.ShapeDtypeStruct((chunks, STATE, width), F32),
            jax.ShapeDtypeStruct((tokens, width), F32),
            jax.ShapeDtypeStruct((tokens, width), F32),
            jax.ShapeDtypeStruct((tokens, 2 * STATE), F32),
            jax.ShapeDtypeStruct((tokens, 2 * STATE), F32),
        ],
        scratch_shapes=[
            pltpu.VMEM((STATE, width), F32),
            pltpu.VMEM((8, width), F32),
            pltpu.VMEM((8, 2 * STATE), F32),
            pltpu.VMEM((width // 128, CHUNK + 8, 128), F32),
            pltpu.VMEM((CHUNK + 8, 2 * STATE), F32),
        ],
        compiler_params=pltpu.CompilerParams(vmem_limit_bytes=VMEM),
        cost_estimate=pl.CostEstimate(
            flops=tokens * width * 16 * 256,
            bytes_accessed=tokens * width * 20,
            transcendentals=tokens * width * 3,
        ),
        name="scan_forward",
    )(vpre, spre, step_pre, vtaps, staps, bias, log_decay, skip)


def taps_back(d_total, later, x, taps, moved):
    moved[:CHUNK, :] = d_total
    moved[CHUNK:, :] = later
    d_x = d_total * taps[CONV - 1 : CONV, :]
    rows = []
    for k in range(CONV - 1):
        later_rows = moved[3 - k : 3 - k + CHUNK, :]
        d_x = d_x + later_rows * taps[k : k + 1, :]
        rows.append(jnp.sum(later_rows * x, axis=0, keepdims=True))
    rows.append(jnp.sum(d_total * x, axis=0, keepdims=True))
    return d_x, rows + [jnp.sum(d_total, axis=0, keepdims=True)]


def backward_kernel(
    vpre, values, vslope, spre, states_ref, sslope, spre_step, vtaps, staps, bias, log_decay, skip, chooser,
    mixer, d_mixer, starts,
    values_low, d_spre, step_low, value_sums, state_sums, step_sums,
    later_grad, later_state, vhead, shead, vmoved, smoved,
):
    @pl.when(pl.program_id(0) == 0)
    def _():
        for ref in (later_grad, later_state, vhead, shead, value_sums, state_sums, step_sums):
            ref[...] = jnp.zeros_like(ref)

    states = states_ref[...]
    b, c = states[:, :STATE], states[:, STATE:]
    shifted_pre, step, rates, cum = step_terms(spre_step, bias, log_decay)
    cum_t = cum.T
    final = cum[CHUNK - 1 :, :]
    grown, ending, whole = jnp.exp(cum), jnp.exp(final - cum), jnp.exp(final)
    b2, c2 = halves(b), halves(c)
    b_left, ct2 = beside(b2), halves(c.T)
    causal = square(1) >= square(0)
    scores_t = jnp.where(causal, folded(mm_nt(b_left, right_side_nt(c2))), 0.0)
    left = lax.broadcasted_iota(jnp.int32, (1, 128), 1) < 64
    zero = jnp.zeros((CHUNK, 128), BF)
    d_early = jnp.zeros((HALF, CHUNK), F32)
    d_late = jnp.zeros((HALF, HALF), F32)
    d_b = jnp.zeros((CHUNK, STATE), F32)
    d_c = jnp.zeros((CHUNK, STATE), F32)
    by_head = jnp.zeros((2 * CHUNK, 128), F32)
    at_end = jnp.zeros((8, 128), F32)
    for p in range(vpre.shape[1] // 128):
        lanes = slice(128 * p, 128 * p + 128)
        pick = chooser[256 * p : 256 * p + 256, :]
        v, dy = values[:, lanes], d_mixer[:, lanes]
        steps = by_pair(step, p)
        weighted = v * steps
        w2, d2 = halves(weighted), halves(dy)
        w_rest = pltpu.roll(weighted - w2[0].astype(F32), 64, 1).astype(BF)
        d_top = pltpu.roll(d2[0].astype(F32), 64, 1).astype(BF)
        early, late = [], []
        for h, mine in ((2 * p, left), (2 * p + 1, ~left)):
            gap = cum_t[h : h + 1, :] - cum[:HALF, h : h + 1]
            decay_early = jnp.exp(jnp.minimum(gap, 0.0))
            gap = cum_t[h : h + 1, HALF:] - cum[HALF:, h : h + 1]
            decay_late = jnp.exp(jnp.minimum(gap, 0.0))
            early.append(decay_early * scores_t[:HALF, :])
            late.append(decay_late * scores_t[HALF:, HALF:])
            one = beside((jnp.where(mine, w2[0], w_rest), jnp.where(mine, w2[0], zero)))
            other = beside((jnp.where(mine, d2[0], d_top), jnp.where(mine, d2[1], zero)))
            d_mix = mm_nt(one, other)
            d_early = d_early + d_mix[:HALF, :] * decay_early
            d_late = d_late + d_mix[HALF:, HALF:] * decay_late
        early = halves(jnp.concatenate(early, axis=0))
        early = folded(mm(early[0], beside(d2))) + mm(early[1], d2[0])
        late = beside(halves(jnp.concatenate(late, axis=0)))
        late = folded(mm(late, right_side((d2[0][HALF:], d2[1][HALF:]))))
        within = jnp.concatenate(
            [
                jnp.where(left, early[:HALF], early[HALF:]),
                jnp.where(left, late[:HALF], late[HALF:]),
            ],
            axis=0,
        )
        held, after_here = starts[0, :, lanes], later_grad[:, lanes]
        after2 = halves(after_here)
        ends = by_pair(ending, p)
        d_weighted = within + ends * folded(mm(b_left, right_side(after2)))
        gain = skip[:, lanes]
        both = jnp.concatenate([dy * (mixer[:, lanes] - gain * v), v * d_weighted], axis=0)
        by_head = by_head + mm(beside(halves(both)), pick)
        ended = jnp.sum(after_here * later_state[:, lanes], axis=0, keepdims=True)
        at_end = at_end + mm(beside(halves(jnp.broadcast_to(ended, (8, 128)))), pick)
        faded = halves(by_pair(grown, p) * dy)
        d_c = d_c + folded(mm_nt(beside(faded), right_side_nt(halves(held))))
        d_b = d_b + folded(mm_nt(beside(halves(weighted * ends)), right_side_nt(after2)))
        added = folded(mm(ct2[0], beside(faded))) + mm(ct2[1], faded[0])
        later_grad[:, lanes] = after_here * by_pair(whole, p) + added
        d_total = (steps * d_weighted + gain * dy) * vslope[:, lanes]
        d_x, rows = taps_back(
            d_total, vhead[:, lanes], vpre[:, lanes], vtaps[:, lanes], vmoved.at[p]
        )
        values_low[:, lanes] = d_x.astype(BF)
        rows += [jnp.sum(v * dy, axis=0, keepdims=True), jnp.zeros((2, 128), F32)]
        value_sums[:, lanes] += jnp.concatenate(rows, axis=0)
        vhead[:, lanes] = d_total[:8]
    later_state[...] = starts[0]
    d_late = jnp.concatenate([jnp.zeros((HALF, HALF), F32), d_late], axis=1)
    d_scores_t = jnp.where(causal, jnp.concatenate([d_early, d_late], axis=0), 0.0)
    top, rest = halves(d_scores_t)
    d_b = d_b + folded(mm(top, beside(c2))) + mm(rest, c2[0])
    top, rest = halves(d_scores_t.T)
    d_c = d_c + folded(mm(top, beside(b2))) + mm(rest, b2[0])
    reached, pulled = by_head[:CHUNK], by_head[CHUNK:]
    last = lax.broadcasted_iota(jnp.int32, (CHUNK, 128), 0) == CHUNK - 1
    d_cum = reached - step * pulled + jnp.where(last, at_end[:1], 0.0)
    d_rate = summed_by(jnp.where(causal, 1.0, 0.0).astype(BF), d_cum)
    d_shifted = (pulled - rates * d_rate) * jax.nn.sigmoid(shifted_pre)
    step_low[...] = d_shifted.astype(BF)
    step_sums[0:1, :] += jnp.sum(d_shifted, axis=0, keepdims=True)
    step_sums[1:2, :] -= jnp.sum(d_rate * step, axis=0, keepdims=True) * rates
    d_total = beside((d_b, d_c)) * sslope[...]
    d_x, rows = taps_back(d_total, shead[...], spre[...], staps[...], smoved)
    d_spre[...] = d_x
    state_sums[...] += jnp.concatenate(rows + [jnp.zeros((3, 2 * STATE), F32)], axis=0)
    shead[...] = d_total[:8]


def backward_scan(
    vpre, values, vslope, spre, states, sslope, step_pre, vtaps, staps, bias, log_decay, skip, mixer, d_mixer,
    starts,
):
    tokens, width = vpre.shape
    chunks = tokens // CHUNK
    lane = jnp.arange(2 * width)
    heads = 2 * (lane // 256) + lane % 128 // 64
    chooser = (heads[:, None] == jnp.arange(128)[None, :]).astype(BF)
    row = lambda n: pl.BlockSpec((CHUNK, n), lambda i: (chunks - 1 - i, 0))
    fixed = lambda x: pl.BlockSpec(x.shape, lambda i: (0, 0))
    summed = lambda n: pl.BlockSpec((8, n), lambda i: (0, 0))
    return pl.pallas_call(
        backward_kernel,
        grid=(chunks,),
        in_specs=[row(width)] * 3 + [row(2 * STATE)] * 3 + [row(128)]
        + [fixed(x) for x in (vtaps, staps, bias, log_decay, skip, chooser)]
        + [row(width), row(width), pl.BlockSpec((1, STATE, width), lambda i: (chunks - 1 - i, 0, 0))],
        out_specs=[
            row(width), row(2 * STATE), row(128), summed(width), summed(2 * STATE), summed(128),
        ],
        out_shape=[
            jax.ShapeDtypeStruct((tokens, width), BF),
            jax.ShapeDtypeStruct((tokens, 2 * STATE), F32),
            jax.ShapeDtypeStruct((tokens, 128), BF),
            jax.ShapeDtypeStruct((8, width), F32),
            jax.ShapeDtypeStruct((8, 2 * STATE), F32),
            jax.ShapeDtypeStruct((8, 128), F32),
        ],
        scratch_shapes=[
            pltpu.VMEM((STATE, width), F32),
            pltpu.VMEM((STATE, width), F32),
            pltpu.VMEM((8, width), F32),
            pltpu.VMEM((8, 2 * STATE), F32),
            pltpu.VMEM((width // 128, CHUNK + 8, 128), F32),
            pltpu.VMEM((CHUNK + 8, 2 * STATE), F32),
        ],
        compiler_params=pltpu.CompilerParams(vmem_limit_bytes=VMEM),
        cost_estimate=pl.CostEstimate(
            flops=tokens * width * 40 * 256,
            bytes_accessed=tokens * width * 24,
            transcendentals=tokens * width * 3,
        ),
        name="scan_backward",
    )(
        vpre, values, vslope, spre, states, sslope, step_pre, vtaps, staps, bias, log_decay, skip, chooser,
        mixer, d_mixer, starts,
    )


def place(arrays, piece, targets, rows):
    count = sum(x.shape[0] // piece for x in arrays)
    assert count == len(targets)
    width, dtype = arrays[0].shape[1], arrays[0].dtype

    def kernel(at, *refs):
        sources, out, done = refs[: len(arrays)], refs[len(arrays)], refs[len(arrays) + 1]
        copies = []
        for source in sources:
            for j in range(source.shape[0] // piece):
                k = len(copies)
                start = pl.multiple_of(at[k], piece)
                copies.append(
                    pltpu.make_async_copy(
                        source.at[pl.ds(j * piece, piece)], out.at[pl.ds(start, piece)], done.at[k]
                    )
                )
        for copy in copies:
            copy.start()
        for copy in copies:
            copy.wait()

    return pl.pallas_call(
        kernel,
        grid_spec=pltpu.PrefetchScalarGridSpec(
            num_scalar_prefetch=1,
            grid=(1,),
            in_specs=[pl.BlockSpec(memory_space=pl.ANY)] * len(arrays),
            out_specs=pl.BlockSpec(memory_space=pltpu.VMEM),
            scratch_shapes=[pltpu.SemaphoreType.DMA((count,))],
        ),
        out_shape=jax.ShapeDtypeStruct((rows, width), dtype),
        compiler_params=pltpu.CompilerParams(vmem_limit_bytes=16 * 1024 * 1024),
        cost_estimate=pl.CostEstimate(
            flops=0, bytes_accessed=2 * rows * width * dtype.itemsize, transcendentals=0
        ),
        name="place",
    )(jnp.stack([jnp.asarray(t, jnp.int32) for t in targets]), *arrays)


def swap(x, axis, bit=1):
    return lax.ppermute(x, axis, [(i, i ^ bit) for i in range(lax.axis_size(axis))])


def turned(x, axis, distance):
    n = lax.axis_size(axis)
    return lax.ppermute(x, axis, [(i, (i + distance) % n) for i in range(n)])


def after(x, *earlier):
    return lax.optimization_barrier((x, *earlier))[0]


def at(x, index, axis):
    return lax.dynamic_index_in_dim(x, index, axis, keepdims=False)


def part(x, index, size, axis):
    return lax.dynamic_slice_in_dim(x, index * size, size, axis)


def ordered(flag, mine, other, axis):
    first = jnp.where(flag == 0, mine, other)
    second = jnp.where(flag == 0, other, mine)
    return jnp.concatenate([first, second], axis=axis)


def paired_kernel(count, core, *refs):
    lows, weights, outs = refs[:count], refs[count : 3 * count], refs[3 * count :]
    step, tiles = pl.program_id(0), pl.num_programs(0) // 2
    for j in range(2):

        @pl.when(step // tiles == j)
        def _(j=j):
            for out, which in zip(outs, (1 - core[0], core[0]), strict=True):
                total = 0.0
                for k, low in enumerate(lows):
                    block = low[:, which]
                    total = total + mm_nt(
                        block.reshape(-1, block.shape[-1]), weights[2 * k + j][...]
                    )
                out[...] = total.astype(out.dtype)


def paired_products(lows, weights, core, sub):
    tokens, n = lows[0].shape[0], weights[0][0].shape[0]
    groups = tokens // (4 * sub)
    split = [x.reshape(groups, 2, 2 * sub, x.shape[1]) for x in lows]
    tile = n
    tiles = n // tile
    outs = [jax.ShapeDtypeStruct((tokens // 2, 2 * n), dtype) for dtype in (BF, F32)]
    first = lambda i, core: (jnp.minimum(i, tiles - 1), 0)
    second = lambda i, core: (jnp.maximum(i - tiles, 0), 0)
    return pl.pallas_call(
        functools.partial(paired_kernel, len(lows)),
        grid_spec=pltpu.PrefetchScalarGridSpec(
            num_scalar_prefetch=1,
            grid=(2 * tiles,),
            in_specs=[pl.BlockSpec(x.shape, lambda i, core: (0, 0, 0, 0)) for x in split]
            + [
                pl.BlockSpec((tile, w.shape[1]), where)
                for pair in weights
                for w, where in zip(pair, (first, second), strict=True)
            ],
            out_specs=[pl.BlockSpec((tokens // 2, tile), lambda i, core: (0, i))] * 2,
        ),
        out_shape=outs,
        compiler_params=pltpu.CompilerParams(vmem_limit_bytes=26 * 1024 * 1024),
        cost_estimate=pl.CostEstimate(flops=1, bytes_accessed=1, transcendentals=0),
        name="paired_products",
    )(core[None], *split, *[w for pair in weights for w in pair])


def whole_sequences(
    block_input, output_grad, input_gain, gate_weight, value_weight, state_weight, step_weight,
    out_weight, value_taps, state_taps, step_bias, log_decay, skip_gain, mixer_gain,
):
    xi, ci, zi, yi = (lax.axis_index(n) for n in ("x", "core", "seq", "heads"))
    nz = lax.axis_size("seq")
    nx = lax.axis_size("x")
    d_model = block_input.shape[-1]
    half = d_model // 2
    group = block_input.shape[2]
    sub = group // 2
    tokens = group * nz
    own = sub * nz // 2
    rows = gate_weight.shape[0]
    cols = gate_weight.shape[1] // 2
    heads = step_weight.shape[1] // 2

    def turned_halves(x):
        return jnp.where(xi == 0, x, jnp.concatenate([x[:, half:], x[:, :half]], axis=1))

    def route(r):
        return [
            (c * nz + z, (z % 2) * nz + 2 * ((z // 2) ^ r) + c) for c in range(2) for z in range(nz)
        ]

    def tokens_in(x):
        rounds = []
        for r in range(2):
            piece = lax.dynamic_slice(x, ((zi // 2) ^ r, 0, yi * sub, 0), (1, 1, sub, d_model))
            rounds.append(lax.ppermute(piece.reshape(sub, d_model), ("core", "seq"), route(r)))
        return rounds

    def in_order(rounds):
        return turned_halves(ordered(zi // 2, *rounds, 0))

    def tokens_back(x):
        pieces = [part(x, (zi // 2) ^ r, sub, 0) for r in range(2)]
        return [
            lax.ppermute(piece, ("core", "seq"), [(b, a) for a, b in route(r)])
            for r, piece in enumerate(pieces)
        ]

    def tokens_home(mine, by_y):
        targets = [(2 * ((zi // 2) ^ r) + y) * sub for y in (yi, 1 - yi) for r in range(2)]
        return place([mine, by_y], sub, targets, 2 * group).reshape(block_input.shape)

    spread_targets = [
        ((2 * k + c) * 2 + y) * sub
        for y, c in ((yi, ci), (1 - yi, ci), (yi, 1 - ci), (1 - yi, 1 - ci))
        for k in range(nz // 2)
    ]

    def spread(x, by_y=None):
        by_y = swap(x, "heads") if by_y is None else by_y
        by_core = swap(x, "core")
        by_both = swap(by_y, "core")
        return place([x, by_y, by_core, by_both], sub, spread_targets, tokens)

    def of_core(x, core):
        return at(x.reshape(nz // 2, 2, 2 * sub, -1), core, 1).reshape(tokens // 2, -1)

    def over_core(send, keep, link=BF):
        return core_sum(swap(send, "core"), keep, link)

    def core_sum(received, keep, link=BF):
        received = received.reshape(nz // 2, 2, sub, keep.shape[1])
        keep = keep.reshape(received.shape)
        goes = (at(keep, 1 - yi, 1) + at(received, 1 - yi, 1).astype(F32)).astype(link)
        return at(keep, yi, 1) + at(received, yi, 1).astype(F32), goes

    def over_y(stays, received):
        return (stays + received.astype(F32)).reshape(own, -1)

    def block_of(weight):
        width = weight.shape[1] // 2
        received = swap(part(weight, 1 - ci, width, 1), "core")
        return ordered(ci, part(weight, ci, width, 1), received, 0)

    def ring(block, *earlier):
        right = turned(block, "seq", 1)
        left = turned(block, "seq", -1)
        return [block, right, left, turned(after(right, left, *earlier), "seq", 1)]

    def stacked(blocks):
        targets = [
            (c * nz + z % nz) * rows for z in (zi, zi + nz - 1, zi + 1, zi + 2) for c in range(2)
        ]
        return place(blocks, rows, targets, half)

    def products(low, features):
        return transposed(features[:, half:], low).astype(BF), transposed(features[:, :half], low)

    def over_x(kept, received):
        return (kept + received.astype(F32)).reshape(2, nz, rows, -1)

    def by_parity(summed, which):
        shape = summed.shape
        split = summed.reshape(*shape[:-3], nz // 2, 2, *shape[-2:])
        return at(split, which, split.ndim - 3)

    def first_pieces(summed):
        return by_parity(summed, 1 - zi % 2).astype(BF)

    def first_sum(summed, received):
        return by_parity(summed, zi % 2) + received.astype(F32)

    def second_pieces(summed):
        return at(summed, 1 - zi // 2, -3).astype(BF)

    def over_z(summed, received):
        return at(summed, zi // 2, -3) + received.astype(F32)

    def to_core(total):
        received = swap(at(total, 1 - ci, 0), "core")
        return at(total, ci, 0), received

    project = lambda a, b: jnp.dot(a, b, preferred_element_type=F32)
    transposed = lambda a, b: lax.dot_general(
        a, b, (((0,), (0,)), ((), ())), preferred_element_type=F32
    )
    back = lambda a, b: lax.dot_general(a, b, (((1,), (1,)), ((), ())), preferred_element_type=F32)

    pad = 128 - heads
    first = jnp.concatenate(
        [
            jnp.concatenate(
                [
                    value_weight[:, cols * k : cols * k + cols],
                    state_weight[:, STATE * k : STATE * k + STATE],
                    step_weight[:, heads * k : heads * k + heads],
                    jnp.broadcast_to(input_gain[:, None], (rows, pad)),
                ],
                axis=1,
            )
            for k in range(2)
        ],
        axis=1,
    )
    first_block = block_of(first)
    first_across = [swap(first_block, "x")]
    first_ring = ring(first_block, *first_across)
    first_across += [swap(x, "x") for x in first_ring[1:]]

    x_own = in_order(tokens_in(block_input))

    pair_weight = after(
        jnp.concatenate(
            [gate_weight[:, :cols], out_weight[:cols].T, gate_weight[:, cols:], out_weight[cols:].T],
            axis=1,
        ),
        first_block,
    )
    pair_block = block_of(pair_weight)
    pair_across = [swap(after(pair_block, first_across[0]), "x")]
    x_all = spread(after(x_own, *pair_across))
    pair_ring = ring(after(pair_block, first_ring[3]))
    pair_across += [swap(after(x, first_across[3]), "x") for x in pair_ring[1:3]] + [None]

    first_own = stacked(first_ring)
    first_other = stacked(first_across)
    def both_halves(a, w_own, w_other):
        return project(a[:, :half], w_own) + project(a[:, half:], w_other)

    split = lambda w: (w[:, :cols], w[:, cols : cols + STATE], w[:, cols + STATE :])
    value_own, state_own, step_own = split(first_own)
    value_other, state_other, step_other = split(first_other)
    gain = jnp.concatenate([step_own[:, -1], step_other[:, -1]])[None].astype(F32)
    blank = jnp.arange(128)[None, :] < heads
    step_own, step_other = jnp.where(blank, step_own, 0), jnp.where(blank, step_other, 0)

    x_wide = x_all.astype(F32)
    normed = (
        x_wide * lax.rsqrt(jnp.mean(x_wide * x_wide, axis=-1, keepdims=True) + EPS) * gain
    ).astype(BF)
    x_own = x_own.astype(F32)
    scaling = lax.rsqrt(jnp.mean(x_own * x_own, axis=-1, keepdims=True) + EPS)

    states_weights = jnp.concatenate([state_own, state_other], axis=0)
    states_received = swap(states_weights, "core")
    states_half = both_halves(normed, state_own, state_other)
    states_pre = ordered(ci, states_half, swap(states_half, "core"), 1)
    values_pre = both_halves(normed, value_own, value_other)
    step_pre = both_halves(normed, step_own, step_other)

    vtaps = part(value_taps, ci, cols, 1)
    lanes = lambda v: jnp.pad(part(v, ci, heads, 0), (0, pad))[None]
    bias, decays = lanes(step_bias), lanes(log_decay)
    skip = jnp.repeat(part(skip_gain, ci, heads, 0), cols // heads)[None]
    gain_mixer = part(mixer_gain, ci, cols, 0)[None]
    og_rounds = tokens_in(after(output_grad, pair_ring[1], pair_ring[2]))
    values_pre, states_received, *pair_across[1:3], pair_ring[3], og_rounds = lax.optimization_barrier(
        (values_pre, states_received, *pair_across[1:3], pair_ring[3], og_rounds)
    )
    og_own = in_order(og_rounds)
    og_own, values_pre = lax.optimization_barrier((og_own, values_pre))
    mixer, starts, *kept = forward_scan(
        values_pre, states_pre, step_pre, vtaps, state_taps, bias, decays, skip
    )
    pair_across[3], og_by_y, mixer = lax.optimization_barrier(
        (swap(pair_ring[3], "x"), swap(og_own, "heads"), mixer)
    )
    og = spread(og_own, og_by_y)
    pair_own = stacked(pair_ring)
    pair_other = stacked(pair_across)
    gate_own, out_own = pair_own[:, :cols], pair_own[:, cols:]
    gate_other, out_other = pair_other[:, :cols], pair_other[:, cols:]
    gate_lin = both_halves(normed, gate_own, gate_other)
    d_out = both_halves(og, out_own, out_other)
    sigmoid_gate = jax.nn.sigmoid(gate_lin)
    silu_gate = gate_lin * sigmoid_gate
    gated = mixer * silu_gate
    weighted = d_out * gain_mixer
    sums = jnp.stack([jnp.sum(gated * gated, axis=1), jnp.sum(weighted * gated, axis=1)])
    sums = sums + swap(sums, "core")
    sums = sums + swap(sums, "heads")
    inverse = lax.rsqrt(sums[0] / INNER + EPS)[:, None]
    out_normed = (gated * inverse * gain_mixer).astype(BF)
    d_gated = inverse * weighted - gated * (inverse * inverse * inverse) * (sums[1][:, None] / INNER)
    d_mixer = d_gated * silu_gate
    gate_low = (d_gated * mixer * sigmoid_gate * (1.0 + gate_lin * (1.0 - sigmoid_gate))).astype(BF)
    g_mixer_gain = jnp.sum(d_out * gated * inverse, axis=0)

    out_sum = jnp.stack(
        [transposed(og[:, :half], out_normed), transposed(og[:, half:], out_normed)]
    ).reshape(2, 2, nz, rows, cols)
    out_pieces = first_pieces(out_sum)
    branch_sends, branch_keeps = paired_products(
        [after(out_normed, out_pieces)], [(out_own, out_other)], ci, sub
    )
    gate_sends, gate_keeps = products(after(gate_low, branch_sends), normed)
    branch_stays, branch_goes = over_core(branch_sends, branch_keeps)
    d_mixer = after(d_mixer, out_pieces, gate_sends, branch_goes)
    scanned = backward_scan(
        values_pre, *kept[:2], states_pre, *kept[2:], step_pre, vtaps, state_taps, bias, decays, skip,
        mixer, d_mixer, starts,
    )
    sent = (swap(out_pieces, "seq", 1), swap(gate_sends, "x"), swap(branch_goes, "heads"))
    sent, scanned = lax.optimization_barrier((sent, scanned))
    out_received, gate_received, branch_received = sent
    values_low, d_states, step_low, value_sums, state_sums, step_sums = scanned

    out_sum = first_sum(out_sum, out_received)
    out_pieces = second_pieces(out_sum)
    value_sends, value_keeps = products(after(values_low, out_pieces), normed)
    gate_sum = over_x(after(gate_keeps, value_sends), gate_received)
    gate_pieces = first_pieces(gate_sum)
    d_states = after(d_states, gate_pieces)
    states_stay, states_go = over_core(of_core(d_states, 1 - ci), of_core(d_states, ci), F32)
    dn_sends, dn_keeps = paired_products(
        [after(gate_low, value_sends, states_go), values_low, step_low],
        [(gate_own, gate_other), (value_own, value_other), (step_own, step_other)],
        ci,
        sub,
    )
    states_low = over_y(states_stay, swap(states_go, "heads")).astype(BF)
    dn_sends = after(dn_sends, states_low)
    states_by_y = swap(states_low, "heads")
    states_by_core = swap(after(states_low, states_by_y), "core")
    states_by_both = swap(after(states_by_y, states_by_core), "core")
    states_all = place(
        [x.astype(F32) for x in (states_low, states_by_y, states_by_core, states_by_both)],
        sub,
        spread_targets,
        tokens,
    ).astype(BF)
    parts = [
        products(part(states_all, ci, STATE, 1), normed),
        products(step_low, normed),
    ]
    small_sends, small_keeps = (jnp.concatenate(p, axis=1) for p in zip(*parts, strict=True))
    branch = over_y(branch_stays, after(branch_received, dn_sends))
    output_rows = turned_halves((x_own + branch).astype(BF))
    (
        value_received, gate_received, small_sends, dn_received, dn_keeps, out_received, output_rows
    ) = lax.optimization_barrier(
        (
            swap(value_sends, "x"), swap(gate_pieces, "seq", 1), small_sends,
            swap(dn_sends, "core"), dn_keeps, swap(out_pieces, "seq", 2), output_rows,
        )
    )

    dn_stays, dn_goes = core_sum(dn_received, dn_keeps)
    output_sent = tokens_back(output_rows)
    gate_sum = first_sum(after(gate_sum, dn_goes), gate_received)
    gate_pieces = second_pieces(gate_sum)
    value_sum = over_x(after(value_keeps, dn_goes), value_received)
    value_pieces = first_pieces(value_sum)
    states_weights = ordered(ci, states_weights, states_received, 1)
    dn_received, output_sent, value_received, small_received = lax.optimization_barrier(
        (
            swap(dn_goes, "heads"), output_sent, swap(value_pieces, "seq", 1), swap(small_sends, "x"),
        )
    )

    d_normed = over_y(dn_stays, dn_received) + back(states_low, states_weights)
    pushed = d_normed * gain
    d_tokens = scaling * pushed - x_own * (scaling * scaling * scaling) * jnp.mean(
        pushed * x_own, axis=-1, keepdims=True
    )
    input_rows = turned_halves((og_own.astype(F32) + d_tokens).astype(BF))
    g_input_gain = turned_halves(jnp.sum(d_normed * x_own * scaling, axis=0)[None])
    per_core = jnp.concatenate(
        [value_sums[:6], g_mixer_gain[None], jnp.pad(step_sums[:2].reshape(1, -1), ((0, 0), (0, cols - 256)))],
        axis=0,
    ).reshape(-1, 256)
    shared = jnp.concatenate([state_sums, g_input_gain.reshape(-1, 256)], axis=0)
    shared = shared + swap(shared, "heads")
    received = swap(jnp.concatenate([per_core, shared], axis=0), "core")
    n_core = per_core.shape[0]
    pack = jnp.concatenate(
        [ordered(ci, per_core, received[:n_core], 0), shared + received[n_core:]], axis=0
    )
    output_sent = jnp.concatenate(after(output_sent, shared), axis=0)
    small_sum = over_x(small_keeps, after(small_received, input_rows))
    small_sum = first_sum(small_sum, swap(first_pieces(small_sum), "seq", 1))
    small_pieces = second_pieces(small_sum)
    input_sent, output_by_y, gate_received, small_pieces, pack = lax.optimization_barrier(
        (
            tokens_back(input_rows), swap(output_sent, "heads"), swap(gate_pieces, "seq", 2),
            small_pieces, pack,
        )
    )

    input_sent = jnp.concatenate(input_sent, axis=0)
    value_sum = first_sum(value_sum, value_received)
    value_pieces = second_pieces(value_sum)
    g_out = over_z(out_sum, out_received)
    pack = pack + swap(pack, "x")
    pack = pack + swap(pack, "seq", 1)
    g_out = g_out[0] + swap(g_out[1].astype(BF), "x").astype(F32)
    out_mine, out_received = to_core(g_out)
    input_by_y, value_received, small_received, out_received, pack = lax.optimization_barrier(
        (
            swap(input_sent, "heads"), swap(value_pieces, "seq", 2), swap(small_pieces, "seq", 2),
            out_received, pack,
        )
    )
    pack = pack + swap(pack, "seq", 2)
    g_gate = over_z(gate_sum, gate_received)
    g_value = over_z(value_sum, value_received)
    g_small = over_z(small_sum, small_received)
    block_output = tokens_home(output_sent, output_by_y)
    grad_input = tokens_home(input_sent, input_by_y)

    both, shared = pack[: 2 * n_core].reshape(2, 8, cols), pack[2 * n_core :]
    by_channel = jnp.transpose(both, (1, 0, 2)).reshape(8, 2 * cols)
    per_head = both[:, 7, :256].reshape(2, 2, 128)[:, :, :heads]
    input_gain_all = shared[8:].reshape(nx, 2, nz, rows)
    my_gain = at(at(at(input_gain_all, xi, 0), ci, 0), zi, 0)

    def widths(mine, received):
        return ordered(ci, mine, received, 1)

    small_mine, small_received = to_core(g_small)
    steps_at = slice(STATE, STATE + heads)
    return (
        block_output,
        grad_input,
        my_gain,
        widths(*to_core(g_gate)),
        widths(*to_core(g_value)),
        widths(small_mine[:, :STATE], small_received[:, :STATE]),
        widths(small_mine[:, steps_at], small_received[:, steps_at]),
        widths(out_mine, out_received).T,
        by_channel[:5],
        shared[:5],
        per_head[:, 0].reshape(-1),
        per_head[:, 1].reshape(-1),
        jnp.sum(by_channel[5].reshape(2 * heads, -1), axis=1),
        by_channel[6],
    )


def solution(mesh):
    sizes = dict(mesh.shape)
    if sizes["seq"] == 2 * MB and sizes["dp"] == 4 and sizes["heads"] == 2:
        devices = mesh.devices.reshape(sizes["dp"] // 2, 2, sizes["seq"], sizes["heads"])
        mesh = jax.sharding.Mesh(devices, ("x", "core", "seq", "heads"))
        body, dp = whole_sequences, ("x", "core")
    else:
        body, dp = shards, ("dp",)
    tokens = P(None, dp, "seq", None)
    both = (*dp, "seq")
    return jax.shard_map(
        body,
        mesh=mesh,
        in_specs=(
            tokens,
            tokens,
            P(both),
            P(both, "heads"),
            P(both, "heads"),
            P(both, None),
            P(both, "heads"),
            P("heads", both),
            P(None, "heads"),
            P(),
            P("heads"),
            P("heads"),
            P("heads"),
            P("heads"),
        ),
        out_specs=(
            tokens,
            tokens,
            P(both),
            P(both, "heads"),
            P(both, "heads"),
            P(both, None),
            P(both, "heads"),
            P("heads", both),
            P(None, "heads"),
            P(),
            P("heads"),
            P("heads"),
            P("heads"),
            P("heads"),
        ),
        check_vma=False,
    )
```

```python
import functools

import jax
import jax.numpy as jnp
from jax import lax
from jax.experimental import pallas as pl
from jax.experimental.pallas import tpu as pltpu
from jax.sharding import PartitionSpec as P

STATE = 128
CONV = 4
MB = 2
INNER = 3072


EPS = 1e-05
HIGH = lax.Precision.HIGHEST


def shifted(block, axis, distance):
    devices = range(lax.axis_size(axis))
    route = [(i - distance, i) for i in devices if i - distance in devices]
    return lax.ppermute(block, axis, route)


def entering(x, axis, combine, identity, reverse):
    peers, index = (lax.axis_size(axis), lax.axis_index(axis))
    everything = jax.tree.map(lambda part: lax.all_gather(part, axis), x)
    start = jax.tree.map(
        lambda part, zero: jnp.broadcast_to(jnp.asarray(zero, part.dtype), part.shape), x, identity
    )

    def step(k, before):
        at = peers - 1 - k if reverse else k
        reached = at > index if reverse else at < index
        new = combine(before, jax.tree.map(lambda part: part[at], everything))
        return jax.tree.map(lambda a, b: jnp.where(reached, a, b), new, before)

    return lax.fori_loop(0, peers, step, start)


def norm_rows(values, gain):
    return values * lax.rsqrt(jnp.mean(values * values, axis=-1, keepdims=True) + EPS) * gain


def conv_silu(extended, taps):
    length = extended.shape[1] - (CONV - 1)
    total = jnp.zeros((extended.shape[0], length, extended.shape[2]), jnp.float32) + taps[CONV]
    for offset in range(CONV):
        total = total + extended[:, offset : offset + length] * taps[offset]
    return jax.nn.silu(total)


def local_parts(
    values_ext, states_ext, step_pre, value_taps, state_taps, step_bias, log_decay, skip_gain
):
    values_conv = conv_silu(values_ext, value_taps)
    states_conv = conv_silu(states_ext, state_taps)
    batch, length, channels = values_conv.shape
    heads_here = step_pre.shape[-1]
    values = values_conv.reshape(batch, length, heads_here, channels // heads_here)
    input_mat = states_conv[..., :STATE]
    output_mat = states_conv[..., STATE:]
    stepsize = jax.nn.softplus(step_pre + step_bias)
    cumulative = jnp.cumsum(-stepsize * jnp.exp(log_decay), axis=1)
    gaps = cumulative[:, :, None, :] - cumulative[:, None, :, :]
    causal = (jnp.arange(length)[:, None] >= jnp.arange(length)[None, :])[None, :, :, None]
    decays = jnp.where(causal, jnp.exp(jnp.where(causal, gaps, 0.0)), 0.0)
    scores = jnp.einsum("btn,bsn->bts", output_mat, input_mat, precision=HIGH)
    weights = decays * scores[..., None] * stepsize[:, None, :, :]
    within = (
        jnp.einsum("btsh,bshp->bthp", weights, values, precision=HIGH) + skip_gain[:, None] * values
    )
    final = cumulative[:, -1]
    ending = jnp.exp(final[:, None, :] - cumulative) * stepsize
    local_state = jnp.einsum("bth,btn,bthp->bhnp", ending, input_mat, values, precision=HIGH)
    return (within, local_state, jnp.exp(final), cumulative, output_mat)


def carried_part(cumulative, output_mat, state_in):
    return jnp.exp(cumulative)[..., None] * jnp.einsum(
        "btn,bhnp->bthp", output_mat, state_in, precision=HIGH
    )


def whole_block(
    values_ext,
    states_ext,
    step_pre,
    value_taps,
    state_taps,
    step_bias,
    log_decay,
    skip_gain,
    state_in,
):
    within, local_state, span_decay, cumulative, output_mat = local_parts(
        values_ext, states_ext, step_pre, value_taps, state_taps, step_bias, log_decay, skip_gain
    )
    result = within + carried_part(cumulative, output_mat, state_in)
    return (result.reshape(result.shape[0], result.shape[1], -1), local_state, span_decay)


def compose(earlier, later):
    return (earlier[0] * later[0], later[0][..., None, None] * earlier[1] + later[1])


def shards(
    block_input,
    output_grad,
    input_gain,
    gate_weight,
    value_weight,
    state_weight,
    step_weight,
    out_weight,
    value_taps,
    state_taps,
    step_bias,
    log_decay,
    skip_gain,
    mixer_gain,
):
    margin = CONV - 1
    width = block_input.shape[-1]
    inner_here = gate_weight.shape[1]
    state_cols = state_weight.shape[1]
    heads_here = step_weight.shape[1]
    acc_gain = jnp.zeros((width,), jnp.float32)
    acc_gate = jnp.zeros((width, inner_here), jnp.float32)
    acc_value = jnp.zeros((width, inner_here), jnp.float32)
    acc_state = jnp.zeros((width, state_cols), jnp.float32)
    acc_step = jnp.zeros((width, heads_here), jnp.float32)
    acc_out = jnp.zeros((inner_here, width), jnp.float32)
    acc_value_taps = jnp.zeros_like(value_taps)
    acc_state_taps = jnp.zeros_like(state_taps)
    acc_step_bias = jnp.zeros_like(step_bias)
    acc_log_decay = jnp.zeros_like(log_decay)
    acc_skip = jnp.zeros_like(skip_gain)
    acc_mixer_gain = jnp.zeros_like(mixer_gain)
    outputs = []
    input_grads = []
    for micro_batch in range(MB):
        weights_now = (
            lax.all_gather(input_gain, ("dp", "seq"), axis=0, tiled=True),
            lax.all_gather(gate_weight, ("dp", "seq"), axis=0, tiled=True),
            lax.all_gather(value_weight, ("dp", "seq"), axis=0, tiled=True),
            lax.all_gather(state_weight, ("dp", "seq"), axis=0, tiled=True),
            lax.all_gather(step_weight, ("dp", "seq"), axis=0, tiled=True),
            lax.all_gather(out_weight, ("dp", "seq"), axis=1, tiled=True),
        )
        gain_full, gate_full, value_full, state_full, step_full, out_full = weights_now
        tokens = block_input[micro_batch].astype(jnp.float32)
        normed = norm_rows(tokens, gain_full.astype(jnp.float32)).astype(jnp.bfloat16)
        gate_lin = jnp.einsum("btd,di->bti", normed, gate_full, preferred_element_type=jnp.float32)
        values_pre = jnp.einsum(
            "btd,di->bti", normed, value_full, preferred_element_type=jnp.float32
        )
        states_pre = jnp.einsum(
            "btd,di->bti", normed, state_full, preferred_element_type=jnp.float32
        )
        step_pre = jnp.einsum("btd,di->bti", normed, step_full, preferred_element_type=jnp.float32)
        outgoing = jnp.concatenate([values_pre[:, -margin:], states_pre[:, -margin:]], axis=2)
        incoming = shifted(outgoing, "seq", 1)
        values_ext = jnp.concatenate([incoming[..., :inner_here], values_pre], axis=1)
        states_ext = jnp.concatenate([incoming[..., inner_here:], states_pre], axis=1)
        within, local_state, span_decay, cumulative, output_mat = local_parts(
            values_ext,
            states_ext,
            step_pre,
            value_taps,
            state_taps,
            step_bias,
            log_decay,
            skip_gain,
        )
        prefix = entering(
            (span_decay, local_state),
            "seq",
            compose,
            (jnp.ones_like(span_decay), jnp.zeros_like(local_state)),
            False,
        )
        state_in = prefix[1]
        mixer = (within + carried_part(cumulative, output_mat, state_in)).reshape(gate_lin.shape)
        silu_gate = jax.nn.silu(gate_lin)
        gated = mixer * silu_gate
        total_sq = lax.psum(jnp.sum(gated * gated, axis=-1), "heads")
        inverse = lax.rsqrt(total_sq / INNER + EPS)[..., None]
        out_normed = (gated * inverse * mixer_gain).astype(jnp.bfloat16)
        partial_out = jnp.einsum(
            "bti,id->btd", out_normed, out_full, preferred_element_type=jnp.float32
        )
        branch = lax.psum(partial_out, "heads")
        outputs.append((tokens + branch).astype(jnp.bfloat16))
        weights_back = (
            lax.all_gather(input_gain, ("dp", "seq"), axis=0, tiled=True),
            lax.all_gather(gate_weight, ("dp", "seq"), axis=0, tiled=True),
            lax.all_gather(value_weight, ("dp", "seq"), axis=0, tiled=True),
            lax.all_gather(state_weight, ("dp", "seq"), axis=0, tiled=True),
            lax.all_gather(step_weight, ("dp", "seq"), axis=0, tiled=True),
            lax.all_gather(out_weight, ("dp", "seq"), axis=1, tiled=True),
        )
        gain_full, gate_full, value_full, state_full, step_full, out_full = weights_back
        grad_out = output_grad[micro_batch]
        d_out_normed = jnp.einsum(
            "btd,id->bti", grad_out, out_full, preferred_element_type=jnp.float32
        )
        acc_out = acc_out + jnp.einsum(
            "bti,btd->id", out_normed, grad_out, preferred_element_type=jnp.float32
        )
        acc_mixer_gain = acc_mixer_gain + jnp.sum(d_out_normed * gated * inverse, axis=(0, 1))
        weighted = d_out_normed * mixer_gain
        dot_total = lax.psum(jnp.sum(weighted * gated, axis=-1), "heads")
        d_gated = inverse * weighted - gated * (inverse * inverse * inverse) * (
            dot_total[..., None] / INNER
        )
        d_mixer = d_gated * silu_gate
        sigmoid_gate = jax.nn.sigmoid(gate_lin)
        d_gate_lin = d_gated * mixer * sigmoid_gate * (1.0 + gate_lin * (1.0 - sigmoid_gate))
        carry_grad = jnp.einsum(
            "bth,btn,bthp->bhnp",
            jnp.exp(cumulative),
            output_mat,
            d_mixer.reshape(within.shape),
            precision=HIGH,
        )
        suffix = entering(
            (span_decay, carry_grad),
            "seq",
            compose,
            (jnp.ones_like(span_decay), jnp.zeros_like(carry_grad)),
            True,
        )
        later_grad = suffix[1]
        d_decay = jnp.sum(later_grad * state_in, axis=(2, 3))
        ignored, pullback = jax.vjp(
            whole_block,
            values_ext,
            states_ext,
            step_pre,
            value_taps,
            state_taps,
            step_bias,
            log_decay,
            skip_gain,
            state_in,
        )
        (
            d_values_ext,
            d_states_ext,
            d_step_pre,
            g_value_taps,
            g_state_taps,
            g_step_bias,
            g_log_decay,
            g_skip,
            unused_state,
        ) = pullback((d_mixer, later_grad, d_decay))
        rim_grads = jnp.concatenate([d_values_ext[:, :margin], d_states_ext[:, :margin]], axis=2)
        returned = shifted(rim_grads, "seq", -1)
        d_values_pre = d_values_ext[:, margin:].at[:, -margin:].add(returned[..., :inner_here])
        d_states_pre = d_states_ext[:, margin:].at[:, -margin:].add(returned[..., inner_here:])
        gate_low = d_gate_lin.astype(jnp.bfloat16)
        values_low = d_values_pre.astype(jnp.bfloat16)
        step_low = d_step_pre.astype(jnp.bfloat16)
        d_normed_part = (
            jnp.einsum("bti,di->btd", gate_low, gate_full, preferred_element_type=jnp.float32)
            + jnp.einsum("bti,di->btd", values_low, value_full, preferred_element_type=jnp.float32)
            + jnp.einsum("bti,di->btd", step_low, step_full, preferred_element_type=jnp.float32)
        )
        d_normed_sum, d_states_total, state_taps_total = lax.psum(
            (d_normed_part, d_states_pre, g_state_taps), "heads"
        )
        states_low = d_states_total.astype(jnp.bfloat16)
        d_normed = d_normed_sum + jnp.einsum(
            "bti,di->btd", states_low, state_full, preferred_element_type=jnp.float32
        )
        acc_gate = acc_gate + jnp.einsum(
            "btd,bti->di", normed, gate_low, preferred_element_type=jnp.float32
        )
        acc_value = acc_value + jnp.einsum(
            "btd,bti->di", normed, values_low, preferred_element_type=jnp.float32
        )
        acc_state = acc_state + jnp.einsum(
            "btd,bti->di", normed, states_low, preferred_element_type=jnp.float32
        )
        acc_step = acc_step + jnp.einsum(
            "btd,bti->di", normed, step_low, preferred_element_type=jnp.float32
        )
        scaling = lax.rsqrt(jnp.mean(tokens * tokens, axis=-1, keepdims=True) + EPS)
        acc_gain = acc_gain + jnp.sum(d_normed * tokens * scaling, axis=(0, 1))
        pushed = d_normed * gain_full.astype(jnp.float32)
        d_tokens = scaling * pushed - tokens * (scaling * scaling * scaling) * jnp.mean(
            pushed * tokens, axis=-1, keepdims=True
        )
        input_grads.append((grad_out.astype(jnp.float32) + d_tokens).astype(jnp.bfloat16))
        acc_value_taps = acc_value_taps + g_value_taps
        acc_state_taps = acc_state_taps + state_taps_total
        acc_step_bias = acc_step_bias + g_step_bias
        acc_log_decay = acc_log_decay + g_log_decay
        acc_skip = acc_skip + g_skip
    summed = (
        lax.psum_scatter(acc_gain, ("dp", "seq"), scatter_dimension=0, tiled=True),
        lax.psum_scatter(acc_gate, ("dp", "seq"), scatter_dimension=0, tiled=True),
        lax.psum_scatter(acc_value, ("dp", "seq"), scatter_dimension=0, tiled=True),
        lax.psum_scatter(acc_state, ("dp", "seq"), scatter_dimension=0, tiled=True),
        lax.psum_scatter(acc_step, ("dp", "seq"), scatter_dimension=0, tiled=True),
        lax.psum_scatter(acc_out, ("dp", "seq"), scatter_dimension=1, tiled=True),
    )
    smalls = lax.psum(
        (acc_value_taps, acc_state_taps, acc_step_bias, acc_log_decay, acc_skip, acc_mixer_gain),
        ("dp", "seq"),
    )
    return (
        jnp.stack(outputs),
        jnp.stack(input_grads),
        summed[0],
        summed[1],
        summed[2],
        summed[3],
        summed[4],
        summed[5],
        smalls[0],
        smalls[1],
        smalls[2],
        smalls[3],
        smalls[4],
        smalls[5],
    )


BF = jnp.bfloat16
F32 = jnp.float32
CHUNK = 256
HALF = 128
VMEM = 18 * 1024 * 1024


def halves(x):
    top = x.astype(BF)
    return top, (x - top.astype(F32)).astype(BF)


def mm(a, b):
    return lax.dot_general(a, b, (((1,), (0,)), ((), ())), preferred_element_type=F32)


def mm_nt(a, b):
    return lax.dot_general(a, b, (((1,), (1,)), ((), ())), preferred_element_type=F32)


def beside(pair):
    return jnp.concatenate(pair, axis=1)


def right_side(b):
    top, rest = b
    return jnp.concatenate([beside((top, rest)), beside((top, jnp.zeros_like(top)))], axis=0)


def right_side_nt(b):
    top, rest = b
    return jnp.concatenate([beside((top, top)), beside((rest, jnp.zeros_like(top)))], axis=0)


def folded(wide):
    n = wide.shape[1] // 2
    return wide[:, :n] + wide[:, n:]


def softplus(x):
    return jnp.maximum(x, 0.0) + jnp.log1p(jnp.exp(-jnp.abs(x)))


def taps_applied(x, before, taps, moved):
    moved[:8, :] = before
    moved[8:, :] = x
    total = taps[CONV : CONV + 1, :]
    for k in range(CONV - 1):
        total = total + moved[5 + k : 5 + k + CHUNK, :] * taps[k : k + 1, :]
    return total + x * taps[CONV - 1 : CONV, :]


def summed_by(ones, x):
    top, rest = halves(x)
    low = x - top.astype(F32) - rest.astype(F32)
    return folded(mm(ones, beside((top, rest)))) + mm(ones, low.astype(BF))


def square(which):
    return lax.broadcasted_iota(jnp.int32, (CHUNK, CHUNK), which)


def step_terms(step_ref, bias_ref, log_decay_ref):
    shifted_pre = step_ref[...] + bias_ref[...]
    step = softplus(shifted_pre)
    rates = jnp.exp(log_decay_ref[...])
    cum = summed_by(jnp.where(square(0) >= square(1), 1.0, 0.0).astype(BF), -step * rates)
    return shifted_pre, step, rates, cum


def by_pair(q, p):
    left = lax.broadcasted_iota(jnp.int32, (1, 128), 1) < 64
    return jnp.where(left, q[:, 2 * p : 2 * p + 1], q[:, 2 * p + 1 : 2 * p + 2])


def forward_kernel(
    vpre, spre, spre_step, vtaps, staps, bias, log_decay, skip,
    mixer, starts, values, vslope, states_ref, sslope, state, vtail, stail, vmoved, smoved,
):
    @pl.when(pl.program_id(0) == 0)
    def _():
        state[...] = jnp.zeros_like(state)
        vtail[...] = jnp.zeros_like(vtail)
        stail[...] = jnp.zeros_like(stail)

    sx = spre[...]
    total = taps_applied(sx, stail[...], staps[...], smoved)
    sigmoid = jax.nn.sigmoid(total)
    states = total * sigmoid
    states_ref[...] = states
    sslope[...] = sigmoid * (1.0 + total * (1.0 - sigmoid))
    stail[...] = sx[CHUNK - 8 :]
    b, c = states[:, :STATE], states[:, STATE:]
    shifted_pre, step, rates, cum = step_terms(spre_step, bias, log_decay)
    cum_t = cum.T
    final = cum[CHUNK - 1 :, :]
    grown, ending, whole = jnp.exp(cum), jnp.exp(final - cum), jnp.exp(final)
    c_left, bt2 = beside(halves(c)), halves(b.T)
    scores = folded(mm_nt(c_left, right_side_nt(halves(b))))
    scores = jnp.where(square(0) >= square(1), scores, 0.0)
    left = lax.broadcasted_iota(jnp.int32, (1, 128), 1) < 64
    starts[0] = state[...]
    for p in range(vpre.shape[1] // 128):
        lanes = slice(128 * p, 128 * p + 128)
        vx = vpre[:, lanes]
        total = taps_applied(vx, vtail[:, lanes], vtaps[:, lanes], vmoved.at[p])
        vtail[:, lanes] = vx[CHUNK - 8 :]
        sigmoid = jax.nn.sigmoid(total)
        v = total * sigmoid
        values[:, lanes] = v
        vslope[:, lanes] = sigmoid * (1.0 + total * (1.0 - sigmoid))
        weighted = v * by_pair(step, p)
        w2 = halves(weighted)
        early, late = [], []
        for h in (2 * p, 2 * p + 1):
            gap = cum[:HALF, h : h + 1] - cum_t[h : h + 1, :HALF]
            early.append(jnp.exp(jnp.minimum(gap, 0.0)) * scores[:HALF, :HALF])
            gap = cum[HALF:, h : h + 1] - cum_t[h : h + 1, :]
            late.append(jnp.exp(jnp.minimum(gap, 0.0)) * scores[HALF:, :])
        early = beside(halves(jnp.concatenate(early, axis=0)))
        early = folded(mm(early, right_side((w2[0][:HALF], w2[1][:HALF]))))
        late = halves(jnp.concatenate(late, axis=0))
        late = folded(mm(late[0], beside(w2))) + mm(late[1], w2[0])
        within = jnp.concatenate(
            [
                jnp.where(left, early[:HALF], early[HALF:]),
                jnp.where(left, late[:HALF], late[HALF:]),
            ],
            axis=0,
        )
        held = state[:, lanes]
        carried = by_pair(grown, p) * folded(mm(c_left, right_side(halves(held))))
        mixer[:, lanes] = within + carried + skip[:, lanes] * v
        ends = halves(weighted * by_pair(ending, p))
        added = folded(mm(bt2[0], beside(ends))) + mm(bt2[1], ends[0])
        state[:, lanes] = held * by_pair(whole, p) + added


def forward_scan(vpre, spre, step_pre, vtaps, staps, bias, log_decay, skip):
    tokens, width = vpre.shape
    chunks = tokens // CHUNK
    row = lambda n: pl.BlockSpec((CHUNK, n), lambda i: (i, 0))
    fixed = lambda x: pl.BlockSpec(x.shape, lambda i: (0, 0))
    return pl.pallas_call(
        forward_kernel,
        grid=(chunks,),
        in_specs=[row(width), row(2 * STATE), row(128)]
        + [fixed(x) for x in (vtaps, staps, bias, log_decay, skip)],
        out_specs=[
            row(width), pl.BlockSpec((1, STATE, width), lambda i: (i, 0, 0)),
            row(width), row(width), row(2 * STATE), row(2 * STATE),
        ],
        out_shape=[
            jax.ShapeDtypeStruct((tokens, width), F32),
            jax.ShapeDtypeStruct((chunks, STATE, width), F32),
            jax.ShapeDtypeStruct((tokens, width), F32),
            jax.ShapeDtypeStruct((tokens, width), F32),
            jax.ShapeDtypeStruct((tokens, 2 * STATE), F32),
            jax.ShapeDtypeStruct((tokens, 2 * STATE), F32),
        ],
        scratch_shapes=[
            pltpu.VMEM((STATE, width), F32),
            pltpu.VMEM((8, width), F32),
            pltpu.VMEM((8, 2 * STATE), F32),
            pltpu.VMEM((width // 128, CHUNK + 8, 128), F32),
            pltpu.VMEM((CHUNK + 8, 2 * STATE), F32),
        ],
        compiler_params=pltpu.CompilerParams(vmem_limit_bytes=VMEM),
        cost_estimate=pl.CostEstimate(
            flops=tokens * width * 16 * 256,
            bytes_accessed=tokens * width * 20,
            transcendentals=tokens * width * 3,
        ),
        name="scan_forward",
    )(vpre, spre, step_pre, vtaps, staps, bias, log_decay, skip)


def taps_back(d_total, later, x, taps, moved):
    moved[:CHUNK, :] = d_total
    moved[CHUNK:, :] = later
    d_x = d_total * taps[CONV - 1 : CONV, :]
    rows = []
    for k in range(CONV - 1):
        later_rows = moved[3 - k : 3 - k + CHUNK, :]
        d_x = d_x + later_rows * taps[k : k + 1, :]
        rows.append(jnp.sum(later_rows * x, axis=0, keepdims=True))
    rows.append(jnp.sum(d_total * x, axis=0, keepdims=True))
    return d_x, rows + [jnp.sum(d_total, axis=0, keepdims=True)]


def backward_kernel(
    vpre, values, vslope, spre, states_ref, sslope, spre_step, vtaps, staps, bias, log_decay, skip, chooser,
    mixer, d_mixer, starts,
    values_low, d_spre, step_low, value_sums, state_sums, step_sums,
    later_grad, later_state, vhead, shead, vmoved, smoved,
):
    @pl.when(pl.program_id(0) == 0)
    def _():
        for ref in (later_grad, later_state, vhead, shead, value_sums, state_sums, step_sums):
            ref[...] = jnp.zeros_like(ref)

    states = states_ref[...]
    b, c = states[:, :STATE], states[:, STATE:]
    shifted_pre, step, rates, cum = step_terms(spre_step, bias, log_decay)
    cum_t = cum.T
    final = cum[CHUNK - 1 :, :]
    grown, ending, whole = jnp.exp(cum), jnp.exp(final - cum), jnp.exp(final)
    b2, c2 = halves(b), halves(c)
    b_left, ct2 = beside(b2), halves(c.T)
    causal = square(1) >= square(0)
    scores_t = jnp.where(causal, folded(mm_nt(b_left, right_side_nt(c2))), 0.0)
    left = lax.broadcasted_iota(jnp.int32, (1, 128), 1) < 64
    zero = jnp.zeros((CHUNK, 128), BF)
    d_early = jnp.zeros((HALF, CHUNK), F32)
    d_late = jnp.zeros((HALF, HALF), F32)
    d_b = jnp.zeros((CHUNK, STATE), F32)
    d_c = jnp.zeros((CHUNK, STATE), F32)
    by_head = jnp.zeros((2 * CHUNK, 128), F32)
    at_end = jnp.zeros((8, 128), F32)
    for p in range(vpre.shape[1] // 128):
        lanes = slice(128 * p, 128 * p + 128)
        pick = chooser[256 * p : 256 * p + 256, :]
        v, dy = values[:, lanes], d_mixer[:, lanes]
        steps = by_pair(step, p)
        weighted = v * steps
        w2, d2 = halves(weighted), halves(dy)
        w_rest = pltpu.roll(weighted - w2[0].astype(F32), 64, 1).astype(BF)
        d_top = pltpu.roll(d2[0].astype(F32), 64, 1).astype(BF)
        early, late = [], []
        for h, mine in ((2 * p, left), (2 * p + 1, ~left)):
            gap = cum_t[h : h + 1, :] - cum[:HALF, h : h + 1]
            decay_early = jnp.exp(jnp.minimum(gap, 0.0))
            gap = cum_t[h : h + 1, HALF:] - cum[HALF:, h : h + 1]
            decay_late = jnp.exp(jnp.minimum(gap, 0.0))
            early.append(decay_early * scores_t[:HALF, :])
            late.append(decay_late * scores_t[HALF:, HALF:])
            one = beside((jnp.where(mine, w2[0], w_rest), jnp.where(mine, w2[0], zero)))
            other = beside((jnp.where(mine, d2[0], d_top), jnp.where(mine, d2[1], zero)))
            d_mix = mm_nt(one, other)
            d_early = d_early + d_mix[:HALF, :] * decay_early
            d_late = d_late + d_mix[HALF:, HALF:] * decay_late
        early = halves(jnp.concatenate(early, axis=0))
        early = folded(mm(early[0], beside(d2))) + mm(early[1], d2[0])
        late = beside(halves(jnp.concatenate(late, axis=0)))
        late = folded(mm(late, right_side((d2[0][HALF:], d2[1][HALF:]))))
        within = jnp.concatenate(
            [
                jnp.where(left, early[:HALF], early[HALF:]),
                jnp.where(left, late[:HALF], late[HALF:]),
            ],
            axis=0,
        )
        held, after_here = starts[0, :, lanes], later_grad[:, lanes]
        after2 = halves(after_here)
        ends = by_pair(ending, p)
        d_weighted = within + ends * folded(mm(b_left, right_side(after2)))
        gain = skip[:, lanes]
        both = jnp.concatenate([dy * (mixer[:, lanes] - gain * v), v * d_weighted], axis=0)
        by_head = by_head + mm(beside(halves(both)), pick)
        ended = jnp.sum(after_here * later_state[:, lanes], axis=0, keepdims=True)
        at_end = at_end + mm(beside(halves(jnp.broadcast_to(ended, (8, 128)))), pick)
        faded = halves(by_pair(grown, p) * dy)
        d_c = d_c + folded(mm_nt(beside(faded), right_side_nt(halves(held))))
        d_b = d_b + folded(mm_nt(beside(halves(weighted * ends)), right_side_nt(after2)))
        added = folded(mm(ct2[0], beside(faded))) + mm(ct2[1], faded[0])
        later_grad[:, lanes] = after_here * by_pair(whole, p) + added
        d_total = (steps * d_weighted + gain * dy) * vslope[:, lanes]
        d_x, rows = taps_back(
            d_total, vhead[:, lanes], vpre[:, lanes], vtaps[:, lanes], vmoved.at[p]
        )
        values_low[:, lanes] = d_x.astype(BF)
        rows += [jnp.sum(v * dy, axis=0, keepdims=True), jnp.zeros((2, 128), F32)]
        value_sums[:, lanes] += jnp.concatenate(rows, axis=0)
        vhead[:, lanes] = d_total[:8]
    later_state[...] = starts[0]
    d_late = jnp.concatenate([jnp.zeros((HALF, HALF), F32), d_late], axis=1)
    d_scores_t = jnp.where(causal, jnp.concatenate([d_early, d_late], axis=0), 0.0)
    top, rest = halves(d_scores_t)
    d_b = d_b + folded(mm(top, beside(c2))) + mm(rest, c2[0])
    top, rest = halves(d_scores_t.T)
    d_c = d_c + folded(mm(top, beside(b2))) + mm(rest, b2[0])
    reached, pulled = by_head[:CHUNK], by_head[CHUNK:]
    last = lax.broadcasted_iota(jnp.int32, (CHUNK, 128), 0) == CHUNK - 1
    d_cum = reached - step * pulled + jnp.where(last, at_end[:1], 0.0)
    d_rate = summed_by(jnp.where(causal, 1.0, 0.0).astype(BF), d_cum)
    d_shifted = (pulled - rates * d_rate) * jax.nn.sigmoid(shifted_pre)
    step_low[...] = d_shifted.astype(BF)
    step_sums[0:1, :] += jnp.sum(d_shifted, axis=0, keepdims=True)
    step_sums[1:2, :] -= jnp.sum(d_rate * step, axis=0, keepdims=True) * rates
    d_total = beside((d_b, d_c)) * sslope[...]
    d_x, rows = taps_back(d_total, shead[...], spre[...], staps[...], smoved)
    d_spre[...] = d_x
    state_sums[...] += jnp.concatenate(rows + [jnp.zeros((3, 2 * STATE), F32)], axis=0)
    shead[...] = d_total[:8]


def backward_scan(
    vpre, values, vslope, spre, states, sslope, step_pre, vtaps, staps, bias, log_decay, skip, mixer, d_mixer,
    starts,
):
    tokens, width = vpre.shape
    chunks = tokens // CHUNK
    lane = jnp.arange(2 * width)
    heads = 2 * (lane // 256) + lane % 128 // 64
    chooser = (heads[:, None] == jnp.arange(128)[None, :]).astype(BF)
    row = lambda n: pl.BlockSpec((CHUNK, n), lambda i: (chunks - 1 - i, 0))
    fixed = lambda x: pl.BlockSpec(x.shape, lambda i: (0, 0))
    summed = lambda n: pl.BlockSpec((8, n), lambda i: (0, 0))
    return pl.pallas_call(
        backward_kernel,
        grid=(chunks,),
        in_specs=[row(width)] * 3 + [row(2 * STATE)] * 3 + [row(128)]
        + [fixed(x) for x in (vtaps, staps, bias, log_decay, skip, chooser)]
        + [row(width), row(width), pl.BlockSpec((1, STATE, width), lambda i: (chunks - 1 - i, 0, 0))],
        out_specs=[
            row(width), row(2 * STATE), row(128), summed(width), summed(2 * STATE), summed(128),
        ],
        out_shape=[
            jax.ShapeDtypeStruct((tokens, width), BF),
            jax.ShapeDtypeStruct((tokens, 2 * STATE), F32),
            jax.ShapeDtypeStruct((tokens, 128), BF),
            jax.ShapeDtypeStruct((8, width), F32),
            jax.ShapeDtypeStruct((8, 2 * STATE), F32),
            jax.ShapeDtypeStruct((8, 128), F32),
        ],
        scratch_shapes=[
            pltpu.VMEM((STATE, width), F32),
            pltpu.VMEM((STATE, width), F32),
            pltpu.VMEM((8, width), F32),
            pltpu.VMEM((8, 2 * STATE), F32),
            pltpu.VMEM((width // 128, CHUNK + 8, 128), F32),
            pltpu.VMEM((CHUNK + 8, 2 * STATE), F32),
        ],
        compiler_params=pltpu.CompilerParams(vmem_limit_bytes=VMEM),
        cost_estimate=pl.CostEstimate(
            flops=tokens * width * 40 * 256,
            bytes_accessed=tokens * width * 24,
            transcendentals=tokens * width * 3,
        ),
        name="scan_backward",
    )(
        vpre, values, vslope, spre, states, sslope, step_pre, vtaps, staps, bias, log_decay, skip, chooser,
        mixer, d_mixer, starts,
    )


def place(arrays, piece, targets, rows):
    count = sum(x.shape[0] // piece for x in arrays)
    assert count == len(targets)
    width, dtype = arrays[0].shape[1], arrays[0].dtype

    def kernel(at, *refs):
        sources, out, done = refs[: len(arrays)], refs[len(arrays)], refs[len(arrays) + 1]
        copies = []
        for source in sources:
            for j in range(source.shape[0] // piece):
                k = len(copies)
                start = pl.multiple_of(at[k], piece)
                copies.append(
                    pltpu.make_async_copy(
                        source.at[pl.ds(j * piece, piece)], out.at[pl.ds(start, piece)], done.at[k]
                    )
                )
        for copy in copies:
            copy.start()
        for copy in copies:
            copy.wait()

    return pl.pallas_call(
        kernel,
        grid_spec=pltpu.PrefetchScalarGridSpec(
            num_scalar_prefetch=1,
            grid=(1,),
            in_specs=[pl.BlockSpec(memory_space=pl.ANY)] * len(arrays),
            out_specs=pl.BlockSpec(memory_space=pltpu.VMEM),
            scratch_shapes=[pltpu.SemaphoreType.DMA((count,))],
        ),
        out_shape=jax.ShapeDtypeStruct((rows, width), dtype),
        compiler_params=pltpu.CompilerParams(vmem_limit_bytes=16 * 1024 * 1024),
        cost_estimate=pl.CostEstimate(
            flops=0, bytes_accessed=2 * rows * width * dtype.itemsize, transcendentals=0
        ),
        name="place",
    )(jnp.stack([jnp.asarray(t, jnp.int32) for t in targets]), *arrays)


def swap(x, axis, bit=1):
    return lax.ppermute(x, axis, [(i, i ^ bit) for i in range(lax.axis_size(axis))])


def turned(x, axis, distance):
    n = lax.axis_size(axis)
    return lax.ppermute(x, axis, [(i, (i + distance) % n) for i in range(n)])


def after(x, *earlier):
    return lax.optimization_barrier((x, *earlier))[0]


def at(x, index, axis):
    return lax.dynamic_index_in_dim(x, index, axis, keepdims=False)


def part(x, index, size, axis):
    return lax.dynamic_slice_in_dim(x, index * size, size, axis)


def ordered(flag, mine, other, axis):
    first = jnp.where(flag == 0, mine, other)
    second = jnp.where(flag == 0, other, mine)
    return jnp.concatenate([first, second], axis=axis)


def paired_kernel(count, core, *refs):
    lows, weights, outs = refs[:count], refs[count : 3 * count], refs[3 * count :]
    step, tiles = pl.program_id(0), pl.num_programs(0) // 2
    for j in range(2):

        @pl.when(step // tiles == j)
        def _(j=j):
            for out, which in zip(outs, (1 - core[0], core[0]), strict=True):
                total = 0.0
                for k, low in enumerate(lows):
                    block = low[:, which]
                    total = total + mm_nt(
                        block.reshape(-1, block.shape[-1]), weights[2 * k + j][...]
                    )
                out[...] = total.astype(out.dtype)


def paired_products(lows, weights, core, sub):
    tokens, n = lows[0].shape[0], weights[0][0].shape[0]
    groups = tokens // (4 * sub)
    split = [x.reshape(groups, 2, 2 * sub, x.shape[1]) for x in lows]
    tile = n
    tiles = n // tile
    outs = [jax.ShapeDtypeStruct((tokens // 2, 2 * n), dtype) for dtype in (BF, F32)]
    first = lambda i, core: (jnp.minimum(i, tiles - 1), 0)
    second = lambda i, core: (jnp.maximum(i - tiles, 0), 0)
    return pl.pallas_call(
        functools.partial(paired_kernel, len(lows)),
        grid_spec=pltpu.PrefetchScalarGridSpec(
            num_scalar_prefetch=1,
            grid=(2 * tiles,),
            in_specs=[pl.BlockSpec(x.shape, lambda i, core: (0, 0, 0, 0)) for x in split]
            + [
                pl.BlockSpec((tile, w.shape[1]), where)
                for pair in weights
                for w, where in zip(pair, (first, second), strict=True)
            ],
            out_specs=[pl.BlockSpec((tokens // 2, tile), lambda i, core: (0, i))] * 2,
        ),
        out_shape=outs,
        compiler_params=pltpu.CompilerParams(vmem_limit_bytes=26 * 1024 * 1024),
        cost_estimate=pl.CostEstimate(flops=1, bytes_accessed=1, transcendentals=0),
        name="paired_products",
    )(core[None], *split, *[w for pair in weights for w in pair])


def whole_sequences(
    block_input, output_grad, input_gain, gate_weight, value_weight, state_weight, step_weight,
    out_weight, value_taps, state_taps, step_bias, log_decay, skip_gain, mixer_gain,
):
    xi, ci, zi, yi = (lax.axis_index(n) for n in ("x", "core", "seq", "heads"))
    nz = lax.axis_size("seq")
    nx = lax.axis_size("x")
    d_model = block_input.shape[-1]
    half = d_model // 2
    group = block_input.shape[2]
    sub = group // 2
    tokens = group * nz
    own = sub * nz // 2
    rows = gate_weight.shape[0]
    cols = gate_weight.shape[1] // 2
    heads = step_weight.shape[1] // 2

    def turned_halves(x):
        return jnp.where(xi == 0, x, jnp.concatenate([x[:, half:], x[:, :half]], axis=1))

    def route(r):
        return [
            (c * nz + z, (z % 2) * nz + 2 * ((z // 2) ^ r) + c) for c in range(2) for z in range(nz)
        ]

    def tokens_in(x):
        rounds = []
        for r in range(2):
            piece = lax.dynamic_slice(x, ((zi // 2) ^ r, 0, yi * sub, 0), (1, 1, sub, d_model))
            rounds.append(lax.ppermute(piece.reshape(sub, d_model), ("core", "seq"), route(r)))
        return rounds

    def in_order(rounds):
        return turned_halves(ordered(zi // 2, *rounds, 0))

    def tokens_back(x):
        pieces = [part(x, (zi // 2) ^ r, sub, 0) for r in range(2)]
        return [
            lax.ppermute(piece, ("core", "seq"), [(b, a) for a, b in route(r)])
            for r, piece in enumerate(pieces)
        ]

    def tokens_home(mine, by_y):
        targets = [(2 * ((zi // 2) ^ r) + y) * sub for y in (yi, 1 - yi) for r in range(2)]
        return place([mine, by_y], sub, targets, 2 * group).reshape(block_input.shape)

    spread_targets = [
        ((2 * k + c) * 2 + y) * sub
        for y, c in ((yi, ci), (1 - yi, ci), (yi, 1 - ci), (1 - yi, 1 - ci))
        for k in range(nz // 2)
    ]

    def spread(x, by_y=None):
        by_y = swap(x, "heads") if by_y is None else by_y
        by_core = swap(x, "core")
        by_both = swap(by_y, "core")
        return place([x, by_y, by_core, by_both], sub, spread_targets, tokens)

    def of_core(x, core):
        return at(x.reshape(nz // 2, 2, 2 * sub, -1), core, 1).reshape(tokens // 2, -1)

    def over_core(send, keep, link=BF):
        return core_sum(swap(send, "core"), keep, link)

    def core_sum(received, keep, link=BF):
        received = received.reshape(nz // 2, 2, sub, keep.shape[1])
        keep = keep.reshape(received.shape)
        goes = (at(keep, 1 - yi, 1) + at(received, 1 - yi, 1).astype(F32)).astype(link)
        return at(keep, yi, 1) + at(received, yi, 1).astype(F32), goes

    def over_y(stays, received):
        return (stays + received.astype(F32)).reshape(own, -1)

    def block_of(weight):
        width = weight.shape[1] // 2
        received = swap(part(weight, 1 - ci, width, 1), "core")
        return ordered(ci, part(weight, ci, width, 1), received, 0)

    def ring(block, *earlier):
        right = turned(block, "seq", 1)
        left = turned(block, "seq", -1)
        return [block, right, left, turned(after(right, left, *earlier), "seq", 1)]

    def stacked(blocks):
        targets = [
            (c * nz + z % nz) * rows for z in (zi, zi + nz - 1, zi + 1, zi + 2) for c in range(2)
        ]
        return place(blocks, rows, targets, half)

    def products(low, features):
        return transposed(features[:, half:], low).astype(BF), transposed(features[:, :half], low)

    def over_x(kept, received):
        return (kept + received.astype(F32)).reshape(2, nz, rows, -1)

    def by_parity(summed, which):
        shape = summed.shape
        split = summed.reshape(*shape[:-3], nz // 2, 2, *shape[-2:])
        return at(split, which, split.ndim - 3)

    def first_pieces(summed):
        return by_parity(summed, 1 - zi % 2).astype(BF)

    def first_sum(summed, received):
        return by_parity(summed, zi % 2) + received.astype(F32)

    def second_pieces(summed):
        return at(summed, 1 - zi // 2, -3).astype(BF)

    def over_z(summed, received):
        return at(summed, zi // 2, -3) + received.astype(F32)

    def to_core(total):
        received = swap(at(total, 1 - ci, 0), "core")
        return at(total, ci, 0), received

    project = lambda a, b: jnp.dot(a, b, preferred_element_type=F32)
    transposed = lambda a, b: lax.dot_general(
        a, b, (((0,), (0,)), ((), ())), preferred_element_type=F32
    )
    back = lambda a, b: lax.dot_general(a, b, (((1,), (1,)), ((), ())), preferred_element_type=F32)

    pad = 128 - heads
    first = jnp.concatenate(
        [
            jnp.concatenate(
                [
                    value_weight[:, cols * k : cols * k + cols],
                    state_weight[:, STATE * k : STATE * k + STATE],
                    step_weight[:, heads * k : heads * k + heads],
                    jnp.broadcast_to(input_gain[:, None], (rows, pad)),
                ],
                axis=1,
            )
            for k in range(2)
        ],
        axis=1,
    )
    first_block = block_of(first)
    first_across = [swap(first_block, "x")]
    first_ring = ring(first_block, *first_across)
    first_across += [swap(x, "x") for x in first_ring[1:]]

    x_own = in_order(tokens_in(block_input))

    pair_weight = after(
        jnp.concatenate(
            [gate_weight[:, :cols], out_weight[:cols].T, gate_weight[:, cols:], out_weight[cols:].T],
            axis=1,
        ),
        first_block,
    )
    pair_block = block_of(pair_weight)
    pair_across = [swap(after(pair_block, first_across[0]), "x")]
    x_all = spread(after(x_own, *pair_across))
    pair_ring = ring(after(pair_block, first_ring[3]))
    pair_across += [swap(after(x, first_across[3]), "x") for x in pair_ring[1:3]] + [None]

    first_own = stacked(first_ring)
    first_other = stacked(first_across)
    def both_halves(a, w_own, w_other):
        return project(a[:, :half], w_own) + project(a[:, half:], w_other)

    split = lambda w: (w[:, :cols], w[:, cols : cols + STATE], w[:, cols + STATE :])
    value_own, state_own, step_own = split(first_own)
    value_other, state_other, step_other = split(first_other)
    gain = jnp.concatenate([step_own[:, -1], step_other[:, -1]])[None].astype(F32)
    blank = jnp.arange(128)[None, :] < heads
    step_own, step_other = jnp.where(blank, step_own, 0), jnp.where(blank, step_other, 0)

    x_wide = x_all.astype(F32)
    normed = (
        x_wide * lax.rsqrt(jnp.mean(x_wide * x_wide, axis=-1, keepdims=True) + EPS) * gain
    ).astype(BF)
    x_own = x_own.astype(F32)
    scaling = lax.rsqrt(jnp.mean(x_own * x_own, axis=-1, keepdims=True) + EPS)

    states_weights = jnp.concatenate([state_own, state_other], axis=0)
    states_received = swap(states_weights, "core")
    states_half = both_halves(normed, state_own, state_other)
    states_pre = ordered(ci, states_half, swap(states_half, "core"), 1)
    values_pre = both_halves(normed, value_own, value_other)
    step_pre = both_halves(normed, step_own, step_other)

    vtaps = part(value_taps, ci, cols, 1)
    lanes = lambda v: jnp.pad(part(v, ci, heads, 0), (0, pad))[None]
    bias, decays = lanes(step_bias), lanes(log_decay)
    skip = jnp.repeat(part(skip_gain, ci, heads, 0), cols // heads)[None]
    gain_mixer = part(mixer_gain, ci, cols, 0)[None]
    og_rounds = tokens_in(after(output_grad, pair_ring[1], pair_ring[2]))
    values_pre, states_received, *pair_across[1:3], pair_ring[3], og_rounds = lax.optimization_barrier(
        (values_pre, states_received, *pair_across[1:3], pair_ring[3], og_rounds)
    )
    og_own = in_order(og_rounds)
    og_own, values_pre = lax.optimization_barrier((og_own, values_pre))
    mixer, starts, *kept = forward_scan(
        values_pre, states_pre, step_pre, vtaps, state_taps, bias, decays, skip
    )
    pair_across[3], og_by_y, mixer = lax.optimization_barrier(
        (swap(pair_ring[3], "x"), swap(og_own, "heads"), mixer)
    )
    og = spread(og_own, og_by_y)
    pair_own = stacked(pair_ring)
    pair_other = stacked(pair_across)
    gate_own, out_own = pair_own[:, :cols], pair_own[:, cols:]
    gate_other, out_other = pair_other[:, :cols], pair_other[:, cols:]
    gate_lin = both_halves(normed, gate_own, gate_other)
    d_out = both_halves(og, out_own, out_other)
    sigmoid_gate = jax.nn.sigmoid(gate_lin)
    silu_gate = gate_lin * sigmoid_gate
    gated = mixer * silu_gate
    weighted = d_out * gain_mixer
    sums = jnp.stack([jnp.sum(gated * gated, axis=1), jnp.sum(weighted * gated, axis=1)])
    sums = sums + swap(sums, "core")
    sums = sums + swap(sums, "heads")
    inverse = lax.rsqrt(sums[0] / INNER + EPS)[:, None]
    out_normed = (gated * inverse * gain_mixer).astype(BF)
    d_gated = inverse * weighted - gated * (inverse * inverse * inverse) * (sums[1][:, None] / INNER)
    d_mixer = d_gated * silu_gate
    gate_low = (d_gated * mixer * sigmoid_gate * (1.0 + gate_lin * (1.0 - sigmoid_gate))).astype(BF)
    g_mixer_gain = jnp.sum(d_out * gated * inverse, axis=0)

    out_sum = jnp.stack(
        [transposed(og[:, :half], out_normed), transposed(og[:, half:], out_normed)]
    ).reshape(2, 2, nz, rows, cols)
    out_pieces = first_pieces(out_sum)
    branch_sends, branch_keeps = paired_products(
        [after(out_normed, out_pieces)], [(out_own, out_other)], ci, sub
    )
    gate_sends, gate_keeps = products(after(gate_low, branch_sends), normed)
    branch_stays, branch_goes = over_core(branch_sends, branch_keeps)
    d_mixer = after(d_mixer, out_pieces, gate_sends, branch_goes)
    scanned = backward_scan(
        values_pre, *kept[:2], states_pre, *kept[2:], step_pre, vtaps, state_taps, bias, decays, skip,
        mixer, d_mixer, starts,
    )
    sent = (swap(out_pieces, "seq", 1), swap(gate_sends, "x"), swap(branch_goes, "heads"))
    sent, scanned = lax.optimization_barrier((sent, scanned))
    out_received, gate_received, branch_received = sent
    values_low, d_states, step_low, value_sums, state_sums, step_sums = scanned

    out_sum = first_sum(out_sum, out_received)
    out_pieces = second_pieces(out_sum)
    value_sends, value_keeps = products(after(values_low, out_pieces), normed)
    gate_sum = over_x(after(gate_keeps, value_sends), gate_received)
    gate_pieces = first_pieces(gate_sum)
    d_states = after(d_states, gate_pieces)
    states_stay, states_go = over_core(of_core(d_states, 1 - ci), of_core(d_states, ci), F32)
    dn_sends, dn_keeps = paired_products(
        [after(gate_low, value_sends, states_go), values_low, step_low],
        [(gate_own, gate_other), (value_own, value_other), (step_own, step_other)],
        ci,
        sub,
    )
    states_low = over_y(states_stay, swap(states_go, "heads")).astype(BF)
    dn_sends = after(dn_sends, states_low)
    states_by_y = swap(states_low, "heads")
    states_by_core = swap(after(states_low, states_by_y), "core")
    states_by_both = swap(after(states_by_y, states_by_core), "core")
    states_all = place(
        [states_low, states_by_y, states_by_core, states_by_both], sub, spread_targets, tokens
    )
    parts = [
        products(part(states_all, ci, STATE, 1), normed),
        products(step_low, normed),
    ]
    small_sends, small_keeps = (jnp.concatenate(p, axis=1) for p in zip(*parts, strict=True))
    branch = over_y(branch_stays, after(branch_received, dn_sends))
    output_rows = turned_halves((x_own + branch).astype(BF))
    (
        value_received, gate_received, small_sends, dn_received, dn_keeps, out_received, output_rows
    ) = lax.optimization_barrier(
        (
            swap(value_sends, "x"), swap(gate_pieces, "seq", 1), small_sends,
            swap(dn_sends, "core"), dn_keeps, swap(out_pieces, "seq", 2), output_rows,
        )
    )

    dn_stays, dn_goes = core_sum(dn_received, dn_keeps)
    output_sent = tokens_back(output_rows)
    gate_sum = first_sum(after(gate_sum, dn_goes), gate_received)
    gate_pieces = second_pieces(gate_sum)
    value_sum = over_x(after(value_keeps, dn_goes), value_received)
    value_pieces = first_pieces(value_sum)
    states_weights = ordered(ci, states_weights, states_received, 1)
    dn_received, output_sent, value_received, small_received = lax.optimization_barrier(
        (
            swap(dn_goes, "heads"), output_sent, swap(value_pieces, "seq", 1), swap(small_sends, "x"),
        )
    )

    d_normed = over_y(dn_stays, dn_received) + back(states_low, states_weights)
    pushed = d_normed * gain
    d_tokens = scaling * pushed - x_own * (scaling * scaling * scaling) * jnp.mean(
        pushed * x_own, axis=-1, keepdims=True
    )
    input_rows = turned_halves((og_own.astype(F32) + d_tokens).astype(BF))
    g_input_gain = turned_halves(jnp.sum(d_normed * x_own * scaling, axis=0)[None])
    per_core = jnp.concatenate(
        [value_sums[:6], g_mixer_gain[None], jnp.pad(step_sums[:2].reshape(1, -1), ((0, 0), (0, cols - 256)))],
        axis=0,
    ).reshape(-1, 256)
    shared = jnp.concatenate([state_sums, g_input_gain.reshape(-1, 256)], axis=0)
    n_core = per_core.shape[0]
    pack = jnp.concatenate([per_core, shared], axis=0)
    output_sent = jnp.concatenate(output_sent, axis=0)
    small_sum = over_x(small_keeps, after(small_received, input_rows))
    small_sum = first_sum(small_sum, swap(first_pieces(small_sum), "seq", 1))
    small_pieces = second_pieces(small_sum)
    input_sent, output_by_y, gate_received, small_pieces, pack = lax.optimization_barrier(
        (
            tokens_back(input_rows), swap(output_sent, "heads"), swap(gate_pieces, "seq", 2),
            small_pieces, pack,
        )
    )

    input_sent = jnp.concatenate(input_sent, axis=0)
    value_sum = first_sum(value_sum, value_received)
    value_pieces = second_pieces(value_sum)
    g_out = over_z(out_sum, out_received)
    pack = pack + swap(pack, "x")
    pack = pack + swap(pack, "seq", 1)
    g_out = g_out[0] + swap(g_out[1].astype(BF), "x").astype(F32)
    out_mine, out_received = to_core(g_out)
    input_by_y, value_received, small_received, out_received, pack = lax.optimization_barrier(
        (
            swap(input_sent, "heads"), swap(value_pieces, "seq", 2), swap(small_pieces, "seq", 2),
            out_received, pack,
        )
    )
    g_value = over_z(value_sum, value_received)
    g_small = over_z(small_sum, small_received)
    value_cores, small_cores, pack_received = lax.optimization_barrier(
        (to_core(g_value), to_core(g_small), swap(pack, "seq", 2))
    )
    pack = pack + pack_received
    shared = pack[n_core:] + swap(pack[n_core:], "heads")
    received = swap(jnp.concatenate([pack[:n_core], shared], axis=0), "core")
    g_gate = over_z(gate_sum, gate_received)
    block_output = tokens_home(output_sent, output_by_y)
    grad_input = tokens_home(input_sent, input_by_y)

    both = ordered(ci, pack[:n_core], received[:n_core], 0).reshape(2, 8, cols)
    shared = shared + received[n_core:]
    by_channel = jnp.transpose(both, (1, 0, 2)).reshape(8, 2 * cols)
    per_head = both[:, 7, :256].reshape(2, 2, 128)[:, :, :heads]
    input_gain_all = shared[8:].reshape(nx, 2, nz, rows)
    my_gain = at(at(at(input_gain_all, xi, 0), ci, 0), zi, 0)

    def widths(mine, received):
        return ordered(ci, mine, received, 1)

    small_mine, small_received = small_cores
    steps_at = slice(STATE, STATE + heads)
    return (
        block_output,
        grad_input,
        my_gain,
        widths(*to_core(g_gate)),
        widths(*value_cores),
        widths(small_mine[:, :STATE], small_received[:, :STATE]),
        widths(small_mine[:, steps_at], small_received[:, steps_at]),
        widths(out_mine, out_received).T,
        by_channel[:5],
        shared[:5],
        per_head[:, 0].reshape(-1),
        per_head[:, 1].reshape(-1),
        jnp.sum(by_channel[5].reshape(2 * heads, -1), axis=1),
        by_channel[6],
    )


def solution(mesh):
    sizes = dict(mesh.shape)
    if sizes["seq"] == 2 * MB and sizes["dp"] == 4 and sizes["heads"] == 2:
        devices = mesh.devices.reshape(sizes["dp"] // 2, 2, sizes["seq"], sizes["heads"])
        mesh = jax.sharding.Mesh(devices, ("x", "core", "seq", "heads"))
        body, dp = whole_sequences, ("x", "core")
    else:
        body, dp = shards, ("dp",)
    tokens = P(None, dp, "seq", None)
    both = (*dp, "seq")
    return jax.shard_map(
        body,
        mesh=mesh,
        in_specs=(
            tokens,
            tokens,
            P(both),
            P(both, "heads"),
            P(both, "heads"),
            P(both, None),
            P(both, "heads"),
            P("heads", both),
            P(None, "heads"),
            P(),
            P("heads"),
            P("heads"),
            P("heads"),
            P("heads"),
        ),
        out_specs=(
            tokens,
            tokens,
            P(both),
            P(both, "heads"),
            P(both, "heads"),
            P(both, None),
            P(both, "heads"),
            P("heads", both),
            P(None, "heads"),
            P(),
            P("heads"),
            P("heads"),
            P("heads"),
            P("heads"),
        ),
        check_vma=False,
    )
```

```python
import functools

import jax
import jax.numpy as jnp
from jax import lax
from jax.experimental import pallas as pl
from jax.experimental.pallas import tpu as pltpu
from jax.sharding import PartitionSpec as P

STATE = 128
CONV = 4
MB = 2
INNER = 3072


EPS = 1e-05
HIGH = lax.Precision.HIGHEST


def shifted(block, axis, distance):
    devices = range(lax.axis_size(axis))
    route = [(i - distance, i) for i in devices if i - distance in devices]
    return lax.ppermute(block, axis, route)


def entering(x, axis, combine, identity, reverse):
    peers, index = (lax.axis_size(axis), lax.axis_index(axis))
    everything = jax.tree.map(lambda part: lax.all_gather(part, axis), x)
    start = jax.tree.map(
        lambda part, zero: jnp.broadcast_to(jnp.asarray(zero, part.dtype), part.shape), x, identity
    )

    def step(k, before):
        at = peers - 1 - k if reverse else k
        reached = at > index if reverse else at < index
        new = combine(before, jax.tree.map(lambda part: part[at], everything))
        return jax.tree.map(lambda a, b: jnp.where(reached, a, b), new, before)

    return lax.fori_loop(0, peers, step, start)


def norm_rows(values, gain):
    return values * lax.rsqrt(jnp.mean(values * values, axis=-1, keepdims=True) + EPS) * gain


def conv_silu(extended, taps):
    length = extended.shape[1] - (CONV - 1)
    total = jnp.zeros((extended.shape[0], length, extended.shape[2]), jnp.float32) + taps[CONV]
    for offset in range(CONV):
        total = total + extended[:, offset : offset + length] * taps[offset]
    return jax.nn.silu(total)


def local_parts(
    values_ext, states_ext, step_pre, value_taps, state_taps, step_bias, log_decay, skip_gain
):
    values_conv = conv_silu(values_ext, value_taps)
    states_conv = conv_silu(states_ext, state_taps)
    batch, length, channels = values_conv.shape
    heads_here = step_pre.shape[-1]
    values = values_conv.reshape(batch, length, heads_here, channels // heads_here)
    input_mat = states_conv[..., :STATE]
    output_mat = states_conv[..., STATE:]
    stepsize = jax.nn.softplus(step_pre + step_bias)
    cumulative = jnp.cumsum(-stepsize * jnp.exp(log_decay), axis=1)
    gaps = cumulative[:, :, None, :] - cumulative[:, None, :, :]
    causal = (jnp.arange(length)[:, None] >= jnp.arange(length)[None, :])[None, :, :, None]
    decays = jnp.where(causal, jnp.exp(jnp.where(causal, gaps, 0.0)), 0.0)
    scores = jnp.einsum("btn,bsn->bts", output_mat, input_mat, precision=HIGH)
    weights = decays * scores[..., None] * stepsize[:, None, :, :]
    within = (
        jnp.einsum("btsh,bshp->bthp", weights, values, precision=HIGH) + skip_gain[:, None] * values
    )
    final = cumulative[:, -1]
    ending = jnp.exp(final[:, None, :] - cumulative) * stepsize
    local_state = jnp.einsum("bth,btn,bthp->bhnp", ending, input_mat, values, precision=HIGH)
    return (within, local_state, jnp.exp(final), cumulative, output_mat)


def carried_part(cumulative, output_mat, state_in):
    return jnp.exp(cumulative)[..., None] * jnp.einsum(
        "btn,bhnp->bthp", output_mat, state_in, precision=HIGH
    )


def whole_block(
    values_ext,
    states_ext,
    step_pre,
    value_taps,
    state_taps,
    step_bias,
    log_decay,
    skip_gain,
    state_in,
):
    within, local_state, span_decay, cumulative, output_mat = local_parts(
        values_ext, states_ext, step_pre, value_taps, state_taps, step_bias, log_decay, skip_gain
    )
    result = within + carried_part(cumulative, output_mat, state_in)
    return (result.reshape(result.shape[0], result.shape[1], -1), local_state, span_decay)


def compose(earlier, later):
    return (earlier[0] * later[0], later[0][..., None, None] * earlier[1] + later[1])


def shards(
    block_input,
    output_grad,
    input_gain,
    gate_weight,
    value_weight,
    state_weight,
    step_weight,
    out_weight,
    value_taps,
    state_taps,
    step_bias,
    log_decay,
    skip_gain,
    mixer_gain,
):
    margin = CONV - 1
    width = block_input.shape[-1]
    inner_here = gate_weight.shape[1]
    state_cols = state_weight.shape[1]
    heads_here = step_weight.shape[1]
    acc_gain = jnp.zeros((width,), jnp.float32)
    acc_gate = jnp.zeros((width, inner_here), jnp.float32)
    acc_value = jnp.zeros((width, inner_here), jnp.float32)
    acc_state = jnp.zeros((width, state_cols), jnp.float32)
    acc_step = jnp.zeros((width, heads_here), jnp.float32)
    acc_out = jnp.zeros((inner_here, width), jnp.float32)
    acc_value_taps = jnp.zeros_like(value_taps)
    acc_state_taps = jnp.zeros_like(state_taps)
    acc_step_bias = jnp.zeros_like(step_bias)
    acc_log_decay = jnp.zeros_like(log_decay)
    acc_skip = jnp.zeros_like(skip_gain)
    acc_mixer_gain = jnp.zeros_like(mixer_gain)
    outputs = []
    input_grads = []
    for micro_batch in range(MB):
        weights_now = (
            lax.all_gather(input_gain, ("dp", "seq"), axis=0, tiled=True),
            lax.all_gather(gate_weight, ("dp", "seq"), axis=0, tiled=True),
            lax.all_gather(value_weight, ("dp", "seq"), axis=0, tiled=True),
            lax.all_gather(state_weight, ("dp", "seq"), axis=0, tiled=True),
            lax.all_gather(step_weight, ("dp", "seq"), axis=0, tiled=True),
            lax.all_gather(out_weight, ("dp", "seq"), axis=1, tiled=True),
        )
        gain_full, gate_full, value_full, state_full, step_full, out_full = weights_now
        tokens = block_input[micro_batch].astype(jnp.float32)
        normed = norm_rows(tokens, gain_full.astype(jnp.float32)).astype(jnp.bfloat16)
        gate_lin = jnp.einsum("btd,di->bti", normed, gate_full, preferred_element_type=jnp.float32)
        values_pre = jnp.einsum(
            "btd,di->bti", normed, value_full, preferred_element_type=jnp.float32
        )
        states_pre = jnp.einsum(
            "btd,di->bti", normed, state_full, preferred_element_type=jnp.float32
        )
        step_pre = jnp.einsum("btd,di->bti", normed, step_full, preferred_element_type=jnp.float32)
        outgoing = jnp.concatenate([values_pre[:, -margin:], states_pre[:, -margin:]], axis=2)
        incoming = shifted(outgoing, "seq", 1)
        values_ext = jnp.concatenate([incoming[..., :inner_here], values_pre], axis=1)
        states_ext = jnp.concatenate([incoming[..., inner_here:], states_pre], axis=1)
        within, local_state, span_decay, cumulative, output_mat = local_parts(
            values_ext,
            states_ext,
            step_pre,
            value_taps,
            state_taps,
            step_bias,
            log_decay,
            skip_gain,
        )
        prefix = entering(
            (span_decay, local_state),
            "seq",
            compose,
            (jnp.ones_like(span_decay), jnp.zeros_like(local_state)),
            False,
        )
        state_in = prefix[1]
        mixer = (within + carried_part(cumulative, output_mat, state_in)).reshape(gate_lin.shape)
        silu_gate = jax.nn.silu(gate_lin)
        gated = mixer * silu_gate
        total_sq = lax.psum(jnp.sum(gated * gated, axis=-1), "heads")
        inverse = lax.rsqrt(total_sq / INNER + EPS)[..., None]
        out_normed = (gated * inverse * mixer_gain).astype(jnp.bfloat16)
        partial_out = jnp.einsum(
            "bti,id->btd", out_normed, out_full, preferred_element_type=jnp.float32
        )
        branch = lax.psum(partial_out, "heads")
        outputs.append((tokens + branch).astype(jnp.bfloat16))
        weights_back = (
            lax.all_gather(input_gain, ("dp", "seq"), axis=0, tiled=True),
            lax.all_gather(gate_weight, ("dp", "seq"), axis=0, tiled=True),
            lax.all_gather(value_weight, ("dp", "seq"), axis=0, tiled=True),
            lax.all_gather(state_weight, ("dp", "seq"), axis=0, tiled=True),
            lax.all_gather(step_weight, ("dp", "seq"), axis=0, tiled=True),
            lax.all_gather(out_weight, ("dp", "seq"), axis=1, tiled=True),
        )
        gain_full, gate_full, value_full, state_full, step_full, out_full = weights_back
        grad_out = output_grad[micro_batch]
        d_out_normed = jnp.einsum(
            "btd,id->bti", grad_out, out_full, preferred_element_type=jnp.float32
        )
        acc_out = acc_out + jnp.einsum(
            "bti,btd->id", out_normed, grad_out, preferred_element_type=jnp.float32
        )
        acc_mixer_gain = acc_mixer_gain + jnp.sum(d_out_normed * gated * inverse, axis=(0, 1))
        weighted = d_out_normed * mixer_gain
        dot_total = lax.psum(jnp.sum(weighted * gated, axis=-1), "heads")
        d_gated = inverse * weighted - gated * (inverse * inverse * inverse) * (
            dot_total[..., None] / INNER
        )
        d_mixer = d_gated * silu_gate
        sigmoid_gate = jax.nn.sigmoid(gate_lin)
        d_gate_lin = d_gated * mixer * sigmoid_gate * (1.0 + gate_lin * (1.0 - sigmoid_gate))
        carry_grad = jnp.einsum(
            "bth,btn,bthp->bhnp",
            jnp.exp(cumulative),
            output_mat,
            d_mixer.reshape(within.shape),
            precision=HIGH,
        )
        suffix = entering(
            (span_decay, carry_grad),
            "seq",
            compose,
            (jnp.ones_like(span_decay), jnp.zeros_like(carry_grad)),
            True,
        )
        later_grad = suffix[1]
        d_decay = jnp.sum(later_grad * state_in, axis=(2, 3))
        ignored, pullback = jax.vjp(
            whole_block,
            values_ext,
            states_ext,
            step_pre,
            value_taps,
            state_taps,
            step_bias,
            log_decay,
            skip_gain,
            state_in,
        )
        (
            d_values_ext,
            d_states_ext,
            d_step_pre,
            g_value_taps,
            g_state_taps,
            g_step_bias,
            g_log_decay,
            g_skip,
            unused_state,
        ) = pullback((d_mixer, later_grad, d_decay))
        rim_grads = jnp.concatenate([d_values_ext[:, :margin], d_states_ext[:, :margin]], axis=2)
        returned = shifted(rim_grads, "seq", -1)
        d_values_pre = d_values_ext[:, margin:].at[:, -margin:].add(returned[..., :inner_here])
        d_states_pre = d_states_ext[:, margin:].at[:, -margin:].add(returned[..., inner_here:])
        gate_low = d_gate_lin.astype(jnp.bfloat16)
        values_low = d_values_pre.astype(jnp.bfloat16)
        step_low = d_step_pre.astype(jnp.bfloat16)
        d_normed_part = (
            jnp.einsum("bti,di->btd", gate_low, gate_full, preferred_element_type=jnp.float32)
            + jnp.einsum("bti,di->btd", values_low, value_full, preferred_element_type=jnp.float32)
            + jnp.einsum("bti,di->btd", step_low, step_full, preferred_element_type=jnp.float32)
        )
        d_normed_sum, d_states_total, state_taps_total = lax.psum(
            (d_normed_part, d_states_pre, g_state_taps), "heads"
        )
        states_low = d_states_total.astype(jnp.bfloat16)
        d_normed = d_normed_sum + jnp.einsum(
            "bti,di->btd", states_low, state_full, preferred_element_type=jnp.float32
        )
        acc_gate = acc_gate + jnp.einsum(
            "btd,bti->di", normed, gate_low, preferred_element_type=jnp.float32
        )
        acc_value = acc_value + jnp.einsum(
            "btd,bti->di", normed, values_low, preferred_element_type=jnp.float32
        )
        acc_state = acc_state + jnp.einsum(
            "btd,bti->di", normed, states_low, preferred_element_type=jnp.float32
        )
        acc_step = acc_step + jnp.einsum(
            "btd,bti->di", normed, step_low, preferred_element_type=jnp.float32
        )
        scaling = lax.rsqrt(jnp.mean(tokens * tokens, axis=-1, keepdims=True) + EPS)
        acc_gain = acc_gain + jnp.sum(d_normed * tokens * scaling, axis=(0, 1))
        pushed = d_normed * gain_full.astype(jnp.float32)
        d_tokens = scaling * pushed - tokens * (scaling * scaling * scaling) * jnp.mean(
            pushed * tokens, axis=-1, keepdims=True
        )
        input_grads.append((grad_out.astype(jnp.float32) + d_tokens).astype(jnp.bfloat16))
        acc_value_taps = acc_value_taps + g_value_taps
        acc_state_taps = acc_state_taps + state_taps_total
        acc_step_bias = acc_step_bias + g_step_bias
        acc_log_decay = acc_log_decay + g_log_decay
        acc_skip = acc_skip + g_skip
    summed = (
        lax.psum_scatter(acc_gain, ("dp", "seq"), scatter_dimension=0, tiled=True),
        lax.psum_scatter(acc_gate, ("dp", "seq"), scatter_dimension=0, tiled=True),
        lax.psum_scatter(acc_value, ("dp", "seq"), scatter_dimension=0, tiled=True),
        lax.psum_scatter(acc_state, ("dp", "seq"), scatter_dimension=0, tiled=True),
        lax.psum_scatter(acc_step, ("dp", "seq"), scatter_dimension=0, tiled=True),
        lax.psum_scatter(acc_out, ("dp", "seq"), scatter_dimension=1, tiled=True),
    )
    smalls = lax.psum(
        (acc_value_taps, acc_state_taps, acc_step_bias, acc_log_decay, acc_skip, acc_mixer_gain),
        ("dp", "seq"),
    )
    return (
        jnp.stack(outputs),
        jnp.stack(input_grads),
        summed[0],
        summed[1],
        summed[2],
        summed[3],
        summed[4],
        summed[5],
        smalls[0],
        smalls[1],
        smalls[2],
        smalls[3],
        smalls[4],
        smalls[5],
    )


BF = jnp.bfloat16
F32 = jnp.float32
CHUNK = 256
HALF = 128
VMEM = 18 * 1024 * 1024


def halves(x):
    top = x.astype(BF)
    return top, (x - top.astype(F32)).astype(BF)


def mm(a, b):
    return lax.dot_general(a, b, (((1,), (0,)), ((), ())), preferred_element_type=F32)


def mm_nt(a, b):
    return lax.dot_general(a, b, (((1,), (1,)), ((), ())), preferred_element_type=F32)


def beside(pair):
    return jnp.concatenate(pair, axis=1)


def right_side(b):
    top, rest = b
    return jnp.concatenate([beside((top, rest)), beside((top, jnp.zeros_like(top)))], axis=0)


def right_side_nt(b):
    top, rest = b
    return jnp.concatenate([beside((top, top)), beside((rest, jnp.zeros_like(top)))], axis=0)


def folded(wide):
    n = wide.shape[1] // 2
    return wide[:, :n] + wide[:, n:]


def softplus(x):
    return jnp.maximum(x, 0.0) + jnp.log1p(jnp.exp(-jnp.abs(x)))


def taps_applied(x, before, taps, moved):
    moved[:8, :] = before
    moved[8:, :] = x
    total = taps[CONV : CONV + 1, :]
    for k in range(CONV - 1):
        total = total + moved[5 + k : 5 + k + CHUNK, :] * taps[k : k + 1, :]
    return total + x * taps[CONV - 1 : CONV, :]


def summed_by(ones, x):
    top, rest = halves(x)
    low = x - top.astype(F32) - rest.astype(F32)
    return folded(mm(ones, beside((top, rest)))) + mm(ones, low.astype(BF))


def square(which):
    return lax.broadcasted_iota(jnp.int32, (CHUNK, CHUNK), which)


def step_terms(step_ref, bias_ref, log_decay_ref):
    shifted_pre = step_ref[...] + bias_ref[...]
    step = softplus(shifted_pre)
    rates = jnp.exp(log_decay_ref[...])
    cum = summed_by(jnp.where(square(0) >= square(1), 1.0, 0.0).astype(BF), -step * rates)
    return shifted_pre, step, rates, cum


def by_pair(q, p):
    left = lax.broadcasted_iota(jnp.int32, (1, 128), 1) < 64
    return jnp.where(left, q[:, 2 * p : 2 * p + 1], q[:, 2 * p + 1 : 2 * p + 2])


def forward_kernel(
    vpre, spre, spre_step, vtaps, staps, bias, log_decay, skip,
    mixer, starts, values, vslope, states_ref, sslope, state, vtail, stail, vmoved, smoved,
):
    @pl.when(pl.program_id(0) == 0)
    def _():
        state[...] = jnp.zeros_like(state)
        vtail[...] = jnp.zeros_like(vtail)
        stail[...] = jnp.zeros_like(stail)

    sx = spre[...]
    total = taps_applied(sx, stail[...], staps[...], smoved)
    sigmoid = jax.nn.sigmoid(total)
    states = total * sigmoid
    states_ref[...] = states
    sslope[...] = sigmoid * (1.0 + total * (1.0 - sigmoid))
    stail[...] = sx[CHUNK - 8 :]
    b, c = states[:, :STATE], states[:, STATE:]
    shifted_pre, step, rates, cum = step_terms(spre_step, bias, log_decay)
    cum_t = cum.T
    final = cum[CHUNK - 1 :, :]
    grown, ending, whole = jnp.exp(cum), jnp.exp(final - cum), jnp.exp(final)
    c_left, bt2 = beside(halves(c)), halves(b.T)
    scores = folded(mm_nt(c_left, right_side_nt(halves(b))))
    scores = jnp.where(square(0) >= square(1), scores, 0.0)
    left = lax.broadcasted_iota(jnp.int32, (1, 128), 1) < 64
    starts[0] = state[...]
    for p in range(vpre.shape[1] // 128):
        lanes = slice(128 * p, 128 * p + 128)
        vx = vpre[:, lanes]
        total = taps_applied(vx, vtail[:, lanes], vtaps[:, lanes], vmoved.at[p])
        vtail[:, lanes] = vx[CHUNK - 8 :]
        sigmoid = jax.nn.sigmoid(total)
        v = total * sigmoid
        values[:, lanes] = v
        vslope[:, lanes] = sigmoid * (1.0 + total * (1.0 - sigmoid))
        weighted = v * by_pair(step, p)
        w2 = halves(weighted)
        early, late = [], []
        for h in (2 * p, 2 * p + 1):
            gap = cum[:HALF, h : h + 1] - cum_t[h : h + 1, :HALF]
            early.append(jnp.exp(jnp.minimum(gap, 0.0)) * scores[:HALF, :HALF])
            gap = cum[HALF:, h : h + 1] - cum_t[h : h + 1, :]
            late.append(jnp.exp(jnp.minimum(gap, 0.0)) * scores[HALF:, :])
        early = beside(halves(jnp.concatenate(early, axis=0)))
        early = folded(mm(early, right_side((w2[0][:HALF], w2[1][:HALF]))))
        late = halves(jnp.concatenate(late, axis=0))
        late = folded(mm(late[0], beside(w2))) + mm(late[1], w2[0])
        within = jnp.concatenate(
            [
                jnp.where(left, early[:HALF], early[HALF:]),
                jnp.where(left, late[:HALF], late[HALF:]),
            ],
            axis=0,
        )
        held = state[:, lanes]
        carried = by_pair(grown, p) * folded(mm(c_left, right_side(halves(held))))
        mixer[:, lanes] = within + carried + skip[:, lanes] * v
        ends = halves(weighted * by_pair(ending, p))
        added = folded(mm(bt2[0], beside(ends))) + mm(bt2[1], ends[0])
        state[:, lanes] = held * by_pair(whole, p) + added


def forward_scan(vpre, spre, step_pre, vtaps, staps, bias, log_decay, skip):
    tokens, width = vpre.shape
    chunks = tokens // CHUNK
    row = lambda n: pl.BlockSpec((CHUNK, n), lambda i: (i, 0))
    fixed = lambda x: pl.BlockSpec(x.shape, lambda i: (0, 0))
    return pl.pallas_call(
        forward_kernel,
        grid=(chunks,),
        in_specs=[row(width), row(2 * STATE), row(128)]
        + [fixed(x) for x in (vtaps, staps, bias, log_decay, skip)],
        out_specs=[
            row(width), pl.BlockSpec((1, STATE, width), lambda i: (i, 0, 0)),
            row(width), row(width), row(2 * STATE), row(2 * STATE),
        ],
        out_shape=[
            jax.ShapeDtypeStruct((tokens, width), F32),
            jax.ShapeDtypeStruct((chunks, STATE, width), F32),
            jax.ShapeDtypeStruct((tokens, width), F32),
            jax.ShapeDtypeStruct((tokens, width), F32),
            jax.ShapeDtypeStruct((tokens, 2 * STATE), F32),
            jax.ShapeDtypeStruct((tokens, 2 * STATE), F32),
        ],
        scratch_shapes=[
            pltpu.VMEM((STATE, width), F32),
            pltpu.VMEM((8, width), F32),
            pltpu.VMEM((8, 2 * STATE), F32),
            pltpu.VMEM((width // 128, CHUNK + 8, 128), F32),
            pltpu.VMEM((CHUNK + 8, 2 * STATE), F32),
        ],
        compiler_params=pltpu.CompilerParams(vmem_limit_bytes=VMEM),
        cost_estimate=pl.CostEstimate(
            flops=tokens * width * 16 * 256,
            bytes_accessed=tokens * width * 20,
            transcendentals=tokens * width * 3,
        ),
        name="scan_forward",
    )(vpre, spre, step_pre, vtaps, staps, bias, log_decay, skip)


def taps_back(d_total, later, x, taps, moved):
    moved[:CHUNK, :] = d_total
    moved[CHUNK:, :] = later
    d_x = d_total * taps[CONV - 1 : CONV, :]
    rows = []
    for k in range(CONV - 1):
        later_rows = moved[3 - k : 3 - k + CHUNK, :]
        d_x = d_x + later_rows * taps[k : k + 1, :]
        rows.append(jnp.sum(later_rows * x, axis=0, keepdims=True))
    rows.append(jnp.sum(d_total * x, axis=0, keepdims=True))
    return d_x, rows + [jnp.sum(d_total, axis=0, keepdims=True)]


def backward_kernel(
    vpre, values, vslope, spre, states_ref, sslope, spre_step, vtaps, staps, bias, log_decay, skip, chooser,
    mixer, d_mixer, starts,
    values_low, d_spre, step_low, value_sums, state_sums, step_sums,
    later_grad, later_state, vhead, shead, vmoved, smoved,
):
    @pl.when(pl.program_id(0) == 0)
    def _():
        for ref in (later_grad, later_state, vhead, shead, value_sums, state_sums, step_sums):
            ref[...] = jnp.zeros_like(ref)

    states = states_ref[...]
    b, c = states[:, :STATE], states[:, STATE:]
    shifted_pre, step, rates, cum = step_terms(spre_step, bias, log_decay)
    cum_t = cum.T
    final = cum[CHUNK - 1 :, :]
    grown, ending, whole = jnp.exp(cum), jnp.exp(final - cum), jnp.exp(final)
    b2, c2 = halves(b), halves(c)
    b_left, ct2 = beside(b2), halves(c.T)
    causal = square(1) >= square(0)
    scores_t = jnp.where(causal, folded(mm_nt(b_left, right_side_nt(c2))), 0.0)
    left = lax.broadcasted_iota(jnp.int32, (1, 128), 1) < 64
    zero = jnp.zeros((CHUNK, 128), BF)
    d_early = jnp.zeros((HALF, CHUNK), F32)
    d_late = jnp.zeros((HALF, HALF), F32)
    d_b = jnp.zeros((CHUNK, STATE), F32)
    d_c = jnp.zeros((CHUNK, STATE), F32)
    by_head = jnp.zeros((2 * CHUNK, 128), F32)
    at_end = jnp.zeros((8, 128), F32)
    for p in range(vpre.shape[1] // 128):
        lanes = slice(128 * p, 128 * p + 128)
        pick = chooser[256 * p : 256 * p + 256, :]
        v, dy = values[:, lanes], d_mixer[:, lanes]
        steps = by_pair(step, p)
        weighted = v * steps
        w2, d2 = halves(weighted), halves(dy)
        w_rest = pltpu.roll(weighted - w2[0].astype(F32), 64, 1).astype(BF)
        d_top = pltpu.roll(d2[0].astype(F32), 64, 1).astype(BF)
        early, late = [], []
        for h, mine in ((2 * p, left), (2 * p + 1, ~left)):
            gap = cum_t[h : h + 1, :] - cum[:HALF, h : h + 1]
            decay_early = jnp.exp(jnp.minimum(gap, 0.0))
            gap = cum_t[h : h + 1, HALF:] - cum[HALF:, h : h + 1]
            decay_late = jnp.exp(jnp.minimum(gap, 0.0))
            early.append(decay_early * scores_t[:HALF, :])
            late.append(decay_late * scores_t[HALF:, HALF:])
            one = beside((jnp.where(mine, w2[0], w_rest), jnp.where(mine, w2[0], zero)))
            other = beside((jnp.where(mine, d2[0], d_top), jnp.where(mine, d2[1], zero)))
            d_mix = mm_nt(one, other)
            d_early = d_early + d_mix[:HALF, :] * decay_early
            d_late = d_late + d_mix[HALF:, HALF:] * decay_late
        early = halves(jnp.concatenate(early, axis=0))
        early = folded(mm(early[0], beside(d2))) + mm(early[1], d2[0])
        late = beside(halves(jnp.concatenate(late, axis=0)))
        late = folded(mm(late, right_side((d2[0][HALF:], d2[1][HALF:]))))
        within = jnp.concatenate(
            [
                jnp.where(left, early[:HALF], early[HALF:]),
                jnp.where(left, late[:HALF], late[HALF:]),
            ],
            axis=0,
        )
        held, after_here = starts[0, :, lanes], later_grad[:, lanes]
        after2 = halves(after_here)
        ends = by_pair(ending, p)
        d_weighted = within + ends * folded(mm(b_left, right_side(after2)))
        gain = skip[:, lanes]
        both = jnp.concatenate([dy * (mixer[:, lanes] - gain * v), v * d_weighted], axis=0)
        by_head = by_head + mm(beside(halves(both)), pick)
        ended = jnp.sum(after_here * later_state[:, lanes], axis=0, keepdims=True)
        at_end = at_end + mm(beside(halves(jnp.broadcast_to(ended, (8, 128)))), pick)
        faded = halves(by_pair(grown, p) * dy)
        d_c = d_c + folded(mm_nt(beside(faded), right_side_nt(halves(held))))
        d_b = d_b + folded(mm_nt(beside(halves(weighted * ends)), right_side_nt(after2)))
        added = folded(mm(ct2[0], beside(faded))) + mm(ct2[1], faded[0])
        later_grad[:, lanes] = after_here * by_pair(whole, p) + added
        d_total = (steps * d_weighted + gain * dy) * vslope[:, lanes]
        d_x, rows = taps_back(
            d_total, vhead[:, lanes], vpre[:, lanes], vtaps[:, lanes], vmoved.at[p]
        )
        values_low[:, lanes] = d_x.astype(BF)
        rows += [jnp.sum(v * dy, axis=0, keepdims=True), jnp.zeros((2, 128), F32)]
        value_sums[:, lanes] += jnp.concatenate(rows, axis=0)
        vhead[:, lanes] = d_total[:8]
    later_state[...] = starts[0]
    d_late = jnp.concatenate([jnp.zeros((HALF, HALF), F32), d_late], axis=1)
    d_scores_t = jnp.where(causal, jnp.concatenate([d_early, d_late], axis=0), 0.0)
    top, rest = halves(d_scores_t)
    d_b = d_b + folded(mm(top, beside(c2))) + mm(rest, c2[0])
    top, rest = halves(d_scores_t.T)
    d_c = d_c + folded(mm(top, beside(b2))) + mm(rest, b2[0])
    reached, pulled = by_head[:CHUNK], by_head[CHUNK:]
    last = lax.broadcasted_iota(jnp.int32, (CHUNK, 128), 0) == CHUNK - 1
    d_cum = reached - step * pulled + jnp.where(last, at_end[:1], 0.0)
    d_rate = summed_by(jnp.where(causal, 1.0, 0.0).astype(BF), d_cum)
    d_shifted = (pulled - rates * d_rate) * jax.nn.sigmoid(shifted_pre)
    step_low[...] = d_shifted.astype(BF)
    step_sums[0:1, :] += jnp.sum(d_shifted, axis=0, keepdims=True)
    step_sums[1:2, :] -= jnp.sum(d_rate * step, axis=0, keepdims=True) * rates
    d_total = beside((d_b, d_c)) * sslope[...]
    d_x, rows = taps_back(d_total, shead[...], spre[...], staps[...], smoved)
    d_spre[...] = d_x
    state_sums[...] += jnp.concatenate(rows + [jnp.zeros((3, 2 * STATE), F32)], axis=0)
    shead[...] = d_total[:8]


def backward_scan(
    vpre, values, vslope, spre, states, sslope, step_pre, vtaps, staps, bias, log_decay, skip, mixer, d_mixer,
    starts,
):
    tokens, width = vpre.shape
    chunks = tokens // CHUNK
    lane = jnp.arange(2 * width)
    heads = 2 * (lane // 256) + lane % 128 // 64
    chooser = (heads[:, None] == jnp.arange(128)[None, :]).astype(BF)
    row = lambda n: pl.BlockSpec((CHUNK, n), lambda i: (chunks - 1 - i, 0))
    fixed = lambda x: pl.BlockSpec(x.shape, lambda i: (0, 0))
    summed = lambda n: pl.BlockSpec((8, n), lambda i: (0, 0))
    return pl.pallas_call(
        backward_kernel,
        grid=(chunks,),
        in_specs=[row(width)] * 3 + [row(2 * STATE)] * 3 + [row(128)]
        + [fixed(x) for x in (vtaps, staps, bias, log_decay, skip, chooser)]
        + [row(width), row(width), pl.BlockSpec((1, STATE, width), lambda i: (chunks - 1 - i, 0, 0))],
        out_specs=[
            row(width), row(2 * STATE), row(128), summed(width), summed(2 * STATE), summed(128),
        ],
        out_shape=[
            jax.ShapeDtypeStruct((tokens, width), BF),
            jax.ShapeDtypeStruct((tokens, 2 * STATE), F32),
            jax.ShapeDtypeStruct((tokens, 128), BF),
            jax.ShapeDtypeStruct((8, width), F32),
            jax.ShapeDtypeStruct((8, 2 * STATE), F32),
            jax.ShapeDtypeStruct((8, 128), F32),
        ],
        scratch_shapes=[
            pltpu.VMEM((STATE, width), F32),
            pltpu.VMEM((STATE, width), F32),
            pltpu.VMEM((8, width), F32),
            pltpu.VMEM((8, 2 * STATE), F32),
            pltpu.VMEM((width // 128, CHUNK + 8, 128), F32),
            pltpu.VMEM((CHUNK + 8, 2 * STATE), F32),
        ],
        compiler_params=pltpu.CompilerParams(vmem_limit_bytes=VMEM),
        cost_estimate=pl.CostEstimate(
            flops=tokens * width * 40 * 256,
            bytes_accessed=tokens * width * 24,
            transcendentals=tokens * width * 3,
        ),
        name="scan_backward",
    )(
        vpre, values, vslope, spre, states, sslope, step_pre, vtaps, staps, bias, log_decay, skip, chooser,
        mixer, d_mixer, starts,
    )


def place(arrays, piece, targets, rows):
    count = sum(x.shape[0] // piece for x in arrays)
    assert count == len(targets)
    width, dtype = arrays[0].shape[1], arrays[0].dtype

    def kernel(at, *refs):
        sources, out, done = refs[: len(arrays)], refs[len(arrays)], refs[len(arrays) + 1]
        copies = []
        for source in sources:
            for j in range(source.shape[0] // piece):
                k = len(copies)
                start = pl.multiple_of(at[k], piece)
                copies.append(
                    pltpu.make_async_copy(
                        source.at[pl.ds(j * piece, piece)], out.at[pl.ds(start, piece)], done.at[k]
                    )
                )
        for copy in copies:
            copy.start()
        for copy in copies:
            copy.wait()

    return pl.pallas_call(
        kernel,
        grid_spec=pltpu.PrefetchScalarGridSpec(
            num_scalar_prefetch=1,
            grid=(1,),
            in_specs=[pl.BlockSpec(memory_space=pl.ANY)] * len(arrays),
            out_specs=pl.BlockSpec(memory_space=pltpu.VMEM),
            scratch_shapes=[pltpu.SemaphoreType.DMA((count,))],
        ),
        out_shape=jax.ShapeDtypeStruct((rows, width), dtype),
        compiler_params=pltpu.CompilerParams(vmem_limit_bytes=16 * 1024 * 1024),
        cost_estimate=pl.CostEstimate(
            flops=0, bytes_accessed=2 * rows * width * dtype.itemsize, transcendentals=0
        ),
        name="place",
    )(jnp.stack([jnp.asarray(t, jnp.int32) for t in targets]), *arrays)


def swap(x, axis, bit=1):
    return lax.ppermute(x, axis, [(i, i ^ bit) for i in range(lax.axis_size(axis))])


def turned(x, axis, distance):
    n = lax.axis_size(axis)
    return lax.ppermute(x, axis, [(i, (i + distance) % n) for i in range(n)])


def after(x, *earlier):
    return lax.optimization_barrier((x, *earlier))[0]


def at(x, index, axis):
    return lax.dynamic_index_in_dim(x, index, axis, keepdims=False)


def part(x, index, size, axis):
    return lax.dynamic_slice_in_dim(x, index * size, size, axis)


def ordered(flag, mine, other, axis):
    first = jnp.where(flag == 0, mine, other)
    second = jnp.where(flag == 0, other, mine)
    return jnp.concatenate([first, second], axis=axis)


def paired_kernel(count, core, *refs):
    lows, weights, outs = refs[:count], refs[count : 3 * count], refs[3 * count :]
    step, tiles = pl.program_id(0), pl.num_programs(0) // 2
    for j in range(2):

        @pl.when(step // tiles == j)
        def _(j=j):
            for out, which in zip(outs, (1 - core[0], core[0]), strict=True):
                total = 0.0
                for k, low in enumerate(lows):
                    block = low[:, which]
                    total = total + mm_nt(
                        block.reshape(-1, block.shape[-1]), weights[2 * k + j][...]
                    )
                out[...] = total.astype(out.dtype)


def paired_products(lows, weights, core, sub):
    tokens, n = lows[0].shape[0], weights[0][0].shape[0]
    groups = tokens // (4 * sub)
    split = [x.reshape(groups, 2, 2 * sub, x.shape[1]) for x in lows]
    tile = n
    tiles = n // tile
    outs = [jax.ShapeDtypeStruct((tokens // 2, 2 * n), dtype) for dtype in (BF, F32)]
    first = lambda i, core: (jnp.minimum(i, tiles - 1), 0)
    second = lambda i, core: (jnp.maximum(i - tiles, 0), 0)
    return pl.pallas_call(
        functools.partial(paired_kernel, len(lows)),
        grid_spec=pltpu.PrefetchScalarGridSpec(
            num_scalar_prefetch=1,
            grid=(2 * tiles,),
            in_specs=[pl.BlockSpec(x.shape, lambda i, core: (0, 0, 0, 0)) for x in split]
            + [
                pl.BlockSpec((tile, w.shape[1]), where)
                for pair in weights
                for w, where in zip(pair, (first, second), strict=True)
            ],
            out_specs=[pl.BlockSpec((tokens // 2, tile), lambda i, core: (0, i))] * 2,
        ),
        out_shape=outs,
        compiler_params=pltpu.CompilerParams(vmem_limit_bytes=26 * 1024 * 1024),
        cost_estimate=pl.CostEstimate(flops=1, bytes_accessed=1, transcendentals=0),
        name="paired_products",
    )(core[None], *split, *[w for pair in weights for w in pair])


def whole_sequences(
    block_input, output_grad, input_gain, gate_weight, value_weight, state_weight, step_weight,
    out_weight, value_taps, state_taps, step_bias, log_decay, skip_gain, mixer_gain,
):
    xi, ci, zi, yi = (lax.axis_index(n) for n in ("x", "core", "seq", "heads"))
    nz = lax.axis_size("seq")
    nx = lax.axis_size("x")
    d_model = block_input.shape[-1]
    half = d_model // 2
    group = block_input.shape[2]
    sub = group // 2
    tokens = group * nz
    own = sub * nz // 2
    rows = gate_weight.shape[0]
    cols = gate_weight.shape[1] // 2
    heads = step_weight.shape[1] // 2

    def turned_halves(x):
        return jnp.where(xi == 0, x, jnp.concatenate([x[:, half:], x[:, :half]], axis=1))

    def route(r):
        return [
            (c * nz + z, (z % 2) * nz + 2 * ((z // 2) ^ r) + c) for c in range(2) for z in range(nz)
        ]

    def tokens_in(x):
        rounds = []
        for r in range(2):
            piece = lax.dynamic_slice(x, ((zi // 2) ^ r, 0, yi * sub, 0), (1, 1, sub, d_model))
            rounds.append(lax.ppermute(piece.reshape(sub, d_model), ("core", "seq"), route(r)))
        return rounds

    def in_order(rounds):
        return turned_halves(ordered(zi // 2, *rounds, 0))

    def tokens_back(x):
        pieces = [part(x, (zi // 2) ^ r, sub, 0) for r in range(2)]
        return [
            lax.ppermute(piece, ("core", "seq"), [(b, a) for a, b in route(r)])
            for r, piece in enumerate(pieces)
        ]

    def tokens_home(mine, by_y):
        targets = [(2 * ((zi // 2) ^ r) + y) * sub for y in (yi, 1 - yi) for r in range(2)]
        return place([mine, by_y], sub, targets, 2 * group).reshape(block_input.shape)

    spread_targets = [
        ((2 * k + c) * 2 + y) * sub
        for y, c in ((yi, ci), (1 - yi, ci), (yi, 1 - ci), (1 - yi, 1 - ci))
        for k in range(nz // 2)
    ]

    def spread(x, by_y=None):
        by_y = swap(x, "heads") if by_y is None else by_y
        by_core = swap(x, "core")
        by_both = swap(by_y, "core")
        return place([x, by_y, by_core, by_both], sub, spread_targets, tokens)

    def of_core(x, core):
        return at(x.reshape(nz // 2, 2, 2 * sub, -1), core, 1).reshape(tokens // 2, -1)

    def over_core(send, keep, link=BF):
        return core_sum(swap(send, "core"), keep, link)

    def core_sum(received, keep, link=BF):
        received = received.reshape(nz // 2, 2, sub, keep.shape[1])
        keep = keep.reshape(received.shape)
        goes = (at(keep, 1 - yi, 1) + at(received, 1 - yi, 1).astype(F32)).astype(link)
        return at(keep, yi, 1) + at(received, yi, 1).astype(F32), goes

    def over_y(stays, received):
        return (stays + received.astype(F32)).reshape(own, -1)

    def block_of(weight):
        width = weight.shape[1] // 2
        received = swap(part(weight, 1 - ci, width, 1), "core")
        return ordered(ci, part(weight, ci, width, 1), received, 0)

    def ring(block, *earlier):
        right = turned(block, "seq", 1)
        left = turned(block, "seq", -1)
        return [block, right, left, turned(after(right, left, *earlier), "seq", 1)]

    def stacked(blocks):
        targets = [
            (c * nz + z % nz) * rows for z in (zi, zi + nz - 1, zi + 1, zi + 2) for c in range(2)
        ]
        return place(blocks, rows, targets, half)

    def products(low, features):
        return transposed(features[:, half:], low).astype(BF), transposed(features[:, :half], low)

    def over_x(kept, received):
        return (kept + received.astype(F32)).reshape(2, nz, rows, -1)

    def by_parity(summed, which):
        shape = summed.shape
        split = summed.reshape(*shape[:-3], nz // 2, 2, *shape[-2:])
        return at(split, which, split.ndim - 3)

    def first_pieces(summed):
        return by_parity(summed, 1 - zi % 2).astype(BF)

    def first_sum(summed, received):
        return by_parity(summed, zi % 2) + received.astype(F32)

    def second_pieces(summed):
        return at(summed, 1 - zi // 2, -3).astype(BF)

    def over_z(summed, received):
        return at(summed, zi // 2, -3) + received.astype(F32)

    def to_core(total):
        received = swap(at(total, 1 - ci, 0), "core")
        return at(total, ci, 0), received

    project = lambda a, b: jnp.dot(a, b, preferred_element_type=F32)
    transposed = lambda a, b: lax.dot_general(
        a, b, (((0,), (0,)), ((), ())), preferred_element_type=F32
    )
    back = lambda a, b: lax.dot_general(a, b, (((1,), (1,)), ((), ())), preferred_element_type=F32)

    pad = 128 - heads
    first = jnp.concatenate(
        [
            jnp.concatenate(
                [
                    value_weight[:, cols * k : cols * k + cols],
                    state_weight[:, STATE * k : STATE * k + STATE],
                    step_weight[:, heads * k : heads * k + heads],
                    jnp.broadcast_to(input_gain[:, None], (rows, pad)),
                ],
                axis=1,
            )
            for k in range(2)
        ],
        axis=1,
    )
    first_block = block_of(first)
    first_across = [swap(first_block, "x")]
    first_ring = ring(first_block, *first_across)
    first_across += [swap(x, "x") for x in first_ring[1:]]

    x_own = in_order(tokens_in(block_input))

    pair_weight = after(
        jnp.concatenate(
            [gate_weight[:, :cols], out_weight[:cols].T, gate_weight[:, cols:], out_weight[cols:].T],
            axis=1,
        ),
        first_block,
    )
    pair_block = block_of(pair_weight)
    pair_across = [swap(after(pair_block, first_across[0]), "x")]
    x_all = spread(after(x_own, *pair_across))
    pair_ring = ring(after(pair_block, first_ring[3]))
    pair_across += [swap(after(x, first_across[3]), "x") for x in pair_ring[1:3]] + [None]

    first_own = stacked(first_ring)
    first_other = stacked(first_across)
    def both_halves(a, w_own, w_other):
        return project(a[:, :half], w_own) + project(a[:, half:], w_other)

    split = lambda w: (w[:, :cols], w[:, cols : cols + STATE], w[:, cols + STATE :])
    value_own, state_own, step_own = split(first_own)
    value_other, state_other, step_other = split(first_other)
    gain = jnp.concatenate([step_own[:, -1], step_other[:, -1]])[None].astype(F32)
    blank = jnp.arange(128)[None, :] < heads
    step_own, step_other = jnp.where(blank, step_own, 0), jnp.where(blank, step_other, 0)

    x_wide = x_all.astype(F32)
    normed = (
        x_wide * lax.rsqrt(jnp.mean(x_wide * x_wide, axis=-1, keepdims=True) + EPS) * gain
    ).astype(BF)
    x_own = x_own.astype(F32)
    scaling = lax.rsqrt(jnp.mean(x_own * x_own, axis=-1, keepdims=True) + EPS)

    states_weights = jnp.concatenate([state_own, state_other], axis=0)
    states_received = swap(states_weights, "core")
    states_half = both_halves(normed, state_own, state_other)
    states_pre = ordered(ci, states_half, swap(states_half, "core"), 1)
    values_pre = both_halves(normed, value_own, value_other)
    step_pre = both_halves(normed, step_own, step_other)

    vtaps = part(value_taps, ci, cols, 1)
    lanes = lambda v: jnp.pad(part(v, ci, heads, 0), (0, pad))[None]
    bias, decays = lanes(step_bias), lanes(log_decay)
    skip = jnp.repeat(part(skip_gain, ci, heads, 0), cols // heads)[None]
    gain_mixer = part(mixer_gain, ci, cols, 0)[None]
    og_rounds = tokens_in(after(output_grad, pair_ring[1], pair_ring[2]))
    values_pre, states_received, *pair_across[1:3], pair_ring[3], og_rounds = lax.optimization_barrier(
        (values_pre, states_received, *pair_across[1:3], pair_ring[3], og_rounds)
    )
    og_own = in_order(og_rounds)
    og_own, values_pre = lax.optimization_barrier((og_own, values_pre))
    mixer, starts, *kept = forward_scan(
        values_pre, states_pre, step_pre, vtaps, state_taps, bias, decays, skip
    )
    pair_across[3], og_by_y, mixer = lax.optimization_barrier(
        (swap(pair_ring[3], "x"), swap(og_own, "heads"), mixer)
    )
    og = spread(og_own, og_by_y)
    pair_own = stacked(pair_ring)
    pair_other = stacked(pair_across)
    gate_own, out_own = pair_own[:, :cols], pair_own[:, cols:]
    gate_other, out_other = pair_other[:, :cols], pair_other[:, cols:]
    gate_lin = both_halves(normed, gate_own, gate_other)
    d_out = both_halves(og, out_own, out_other)
    sigmoid_gate = jax.nn.sigmoid(gate_lin)
    silu_gate = gate_lin * sigmoid_gate
    gated = mixer * silu_gate
    weighted = d_out * gain_mixer
    sums = jnp.stack([jnp.sum(gated * gated, axis=1), jnp.sum(weighted * gated, axis=1)])
    sums = sums + swap(sums, "core")
    sums = sums + swap(sums, "heads")
    inverse = lax.rsqrt(sums[0] / INNER + EPS)[:, None]
    out_normed = (gated * inverse * gain_mixer).astype(BF)
    d_gated = inverse * weighted - gated * (inverse * inverse * inverse) * (sums[1][:, None] / INNER)
    d_mixer = d_gated * silu_gate
    gate_low = (d_gated * mixer * sigmoid_gate * (1.0 + gate_lin * (1.0 - sigmoid_gate))).astype(BF)
    g_mixer_gain = jnp.sum(d_out * gated * inverse, axis=0)

    out_sum = jnp.stack(
        [transposed(og[:, :half], out_normed), transposed(og[:, half:], out_normed)]
    ).reshape(2, 2, nz, rows, cols)
    out_pieces = first_pieces(out_sum)
    branch_sends, branch_keeps = paired_products(
        [after(out_normed, out_pieces)], [(out_own, out_other)], ci, sub
    )
    gate_sends, gate_keeps = products(after(gate_low, branch_sends), normed)
    branch_stays, branch_goes = over_core(branch_sends, branch_keeps)
    d_mixer = after(d_mixer, out_pieces, gate_sends, branch_goes)
    scanned = backward_scan(
        values_pre, *kept[:2], states_pre, *kept[2:], step_pre, vtaps, state_taps, bias, decays, skip,
        mixer, d_mixer, starts,
    )
    sent = (swap(out_pieces, "seq", 1), swap(gate_sends, "x"), swap(branch_goes, "heads"))
    sent, scanned = lax.optimization_barrier((sent, scanned))
    out_received, gate_received, branch_received = sent
    values_low, d_states, step_low, value_sums, state_sums, step_sums = scanned

    out_sum = first_sum(out_sum, out_received)
    out_pieces = second_pieces(out_sum)
    value_sends, value_keeps = products(after(values_low, out_pieces), normed)
    gate_sum = over_x(after(gate_keeps, value_sends), gate_received)
    gate_pieces = first_pieces(gate_sum)
    d_states = after(d_states, gate_pieces)
    states_stay, states_go = over_core(of_core(d_states, 1 - ci), of_core(d_states, ci), F32)
    dn_sends, dn_keeps = paired_products(
        [after(gate_low, value_sends, states_go), values_low, step_low],
        [(gate_own, gate_other), (value_own, value_other), (step_own, step_other)],
        ci,
        sub,
    )
    states_low = over_y(states_stay, swap(states_go, "heads")).astype(BF)
    dn_sends = after(dn_sends, states_low)
    states_by_y = swap(states_low, "heads")
    states_by_core = swap(after(states_low, states_by_y), "core")
    states_by_both = swap(after(states_by_y, states_by_core), "core")
    states_all = place(
        [states_low, states_by_y, states_by_core, states_by_both], sub, spread_targets, tokens
    )
    small_low = jnp.concatenate([part(states_all, ci, STATE, 1), step_low], axis=1)
    small_sends, small_keeps = products(small_low, normed)
    branch = over_y(branch_stays, after(branch_received, dn_sends))
    output_rows = turned_halves((x_own + branch).astype(BF))
    (
        value_received, gate_received, small_sends, dn_received, dn_keeps, out_received, output_rows
    ) = lax.optimization_barrier(
        (
            swap(value_sends, "x"), swap(gate_pieces, "seq", 1), small_sends,
            swap(dn_sends, "core"), dn_keeps, swap(out_pieces, "seq", 2), output_rows,
        )
    )

    dn_stays, dn_goes = core_sum(dn_received, dn_keeps)
    output_sent = tokens_back(output_rows)
    gate_sum = first_sum(after(gate_sum, dn_goes), gate_received)
    gate_pieces = second_pieces(gate_sum)
    value_sum = over_x(after(value_keeps, dn_goes), value_received)
    value_pieces = first_pieces(value_sum)
    states_weights = ordered(ci, states_weights, states_received, 1)
    dn_received, output_sent, value_received, small_received = lax.optimization_barrier(
        (
            swap(dn_goes, "heads"), output_sent, swap(value_pieces, "seq", 1), swap(small_sends, "x"),
        )
    )

    d_normed = over_y(dn_stays, dn_received) + back(states_low, states_weights)
    pushed = d_normed * gain
    d_tokens = scaling * pushed - x_own * (scaling * scaling * scaling) * jnp.mean(
        pushed * x_own, axis=-1, keepdims=True
    )
    input_rows = turned_halves((og_own.astype(F32) + d_tokens).astype(BF))
    g_input_gain = turned_halves(jnp.sum(d_normed * x_own * scaling, axis=0)[None])
    per_core = jnp.concatenate(
        [value_sums[:6], g_mixer_gain[None], jnp.pad(step_sums[:2].reshape(1, -1), ((0, 0), (0, cols - 256)))],
        axis=0,
    ).reshape(-1, 256)
    shared = jnp.concatenate([state_sums, g_input_gain.reshape(-1, 256)], axis=0)
    n_core = per_core.shape[0]
    pack = jnp.concatenate([per_core, shared], axis=0)
    output_sent = jnp.concatenate(output_sent, axis=0)
    small_sum = over_x(small_keeps, after(small_received, input_rows))
    small_sum = first_sum(small_sum, swap(first_pieces(small_sum), "seq", 1))
    small_pieces = second_pieces(small_sum)
    input_sent, output_by_y, gate_received, small_pieces, pack = lax.optimization_barrier(
        (
            tokens_back(input_rows), swap(output_sent, "heads"), swap(gate_pieces, "seq", 2),
            small_pieces, pack,
        )
    )

    input_sent = jnp.concatenate(input_sent, axis=0)
    value_sum = first_sum(value_sum, value_received)
    value_pieces = second_pieces(value_sum)
    g_out = over_z(out_sum, out_received)
    pack = pack + swap(pack, "x")
    pack = pack + swap(pack, "seq", 1)
    g_out = g_out[0] + swap(g_out[1].astype(BF), "x").astype(F32)
    out_mine, out_received = to_core(g_out)
    input_by_y, value_received, small_received, out_received, pack = lax.optimization_barrier(
        (
            swap(input_sent, "heads"), swap(value_pieces, "seq", 2), swap(small_pieces, "seq", 2),
            out_received, pack,
        )
    )
    g_value = over_z(value_sum, value_received)
    g_small = over_z(small_sum, small_received)
    value_cores, small_cores, pack_received = lax.optimization_barrier(
        (to_core(g_value), to_core(g_small), swap(pack, "seq", 2))
    )
    pack = pack + pack_received
    shared = pack[n_core:] + swap(pack[n_core:], "heads")
    received = swap(jnp.concatenate([pack[:n_core], shared], axis=0), "core")
    g_gate = over_z(gate_sum, gate_received)
    block_output = tokens_home(output_sent, output_by_y)
    grad_input = tokens_home(input_sent, input_by_y)

    both = ordered(ci, pack[:n_core], received[:n_core], 0).reshape(2, 8, cols)
    shared = shared + received[n_core:]
    by_channel = jnp.transpose(both, (1, 0, 2)).reshape(8, 2 * cols)
    per_head = both[:, 7, :256].reshape(2, 2, 128)[:, :, :heads]
    input_gain_all = shared[8:].reshape(nx, 2, nz, rows)
    my_gain = at(at(at(input_gain_all, xi, 0), ci, 0), zi, 0)

    def widths(mine, received):
        return ordered(ci, mine, received, 1)

    small_mine, small_received = small_cores
    steps_at = slice(STATE, STATE + heads)
    return (
        block_output,
        grad_input,
        my_gain,
        widths(*to_core(g_gate)),
        widths(*value_cores),
        widths(small_mine[:, :STATE], small_received[:, :STATE]),
        widths(small_mine[:, steps_at], small_received[:, steps_at]),
        widths(out_mine, out_received).T,
        by_channel[:5],
        shared[:5],
        per_head[:, 0].reshape(-1),
        per_head[:, 1].reshape(-1),
        jnp.sum(by_channel[5].reshape(2 * heads, -1), axis=1),
        by_channel[6],
    )


def solution(mesh):
    sizes = dict(mesh.shape)
    if sizes["seq"] == 2 * MB and sizes["dp"] == 4 and sizes["heads"] == 2:
        devices = mesh.devices.reshape(sizes["dp"] // 2, 2, sizes["seq"], sizes["heads"])
        mesh = jax.sharding.Mesh(devices, ("x", "core", "seq", "heads"))
        body, dp = whole_sequences, ("x", "core")
    else:
        body, dp = shards, ("dp",)
    tokens = P(None, dp, "seq", None)
    both = (*dp, "seq")
    return jax.shard_map(
        body,
        mesh=mesh,
        in_specs=(
            tokens,
            tokens,
            P(both),
            P(both, "heads"),
            P(both, "heads"),
            P(both, None),
            P(both, "heads"),
            P("heads", both),
            P(None, "heads"),
            P(),
            P("heads"),
            P("heads"),
            P("heads"),
            P("heads"),
        ),
        out_specs=(
            tokens,
            tokens,
            P(both),
            P(both, "heads"),
            P(both, "heads"),
            P(both, None),
            P(both, "heads"),
            P("heads", both),
            P(None, "heads"),
            P(),
            P("heads"),
            P("heads"),
            P("heads"),
            P("heads"),
        ),
        check_vma=False,
    )
```
